128 devices in a mesh: lat: 16 (over x, z), lon: 8 (over y, core).
Axes of the slice: x: 4, y: 4, z: 4, core: 2. Of those that a mesh axis runs over, the one named last changes fastest.
Arguments:
- field: bfloat16 [384, 720, 384], P('lat', 'lon'), may hold values from -6 to 6
- cotangent: bfloat16 [384, 720, 384], P('lat', 'lon'), may hold values from -6 to 6
- kernel_weights: bfloat16 [3, 384, 384], replicated, may hold values from -0.1875 to 0.1875
- spectral_weight: bfloat16 [384, 384], replicated, may hold values from -0.3125 to 0.3125
- out_weight: bfloat16 [384, 384], replicated, may hold values from -0.3125 to 0.3125
- degree_gain: float32 [192, 384], replicated, may hold values from 0.5 to 4
- kernel_basis: float32 [3, 3, 7, 384], replicated, may hold values from -2.5 to 2.5
- lon_reach: int32 [3, 384], replicated, may hold values from 1 to 3, as said below
Outputs:
- output_field: bfloat16 [384, 720, 384], P('lat', 'lon')
- grad_field: bfloat16 [384, 720, 384], P('lat', 'lon')
- weight_grads: float32 [5, 384, 384], replicated
- gain_grad: float32 [192, 384], replicated
The draws below stay inside these ranges and needn't reach their ends.
Inputs may be any that keep to these rules, and one draw needn't show every extreme that they name: lon_reach[r, i] counts the longitude cells on each side that the kernels of output row i cover at row offset r - 1; the two polar rows cover 3.
All inputs are finite; a program needn't handle non-finite values.
Results may differ from the reference program's by a relative error of at most 0.03.
Values may be sent and summed in bfloat16 or wider, within the bound.
A program may use at most 192 MiB of HBM per device.

```python
import math
import jax
import jax.numpy as jnp
from jax import lax

CHANNELS = 384
DEGREES = 192
ORDERS = 192
LONGITUDES = 720
LATITUDES = 384
KERNELS = 3
LON_SPAN = 3
LAT_DEV = 24
N_LAT = 16


def draw_lon_reach(key, part):
    key = jax.random.fold_in(key, 11)
    reaches = jax.random.randint(key, (3, LATITUDES), 1, LON_SPAN + 1, dtype=jnp.int32)
    row_index = jnp.arange(LATITUDES, dtype=jnp.int32)[None, :]
    at_poles = (row_index == 0) | (row_index == LATITUDES - 1)
    reaches = jnp.where(at_poles, LON_SPAN, reaches)
    return jnp.where(row_index == LATITUDES // 2, 1, reaches).astype(jnp.int32)


def block_scale(rng, dims, pieces, smallest, top_value):
    level = 1.0
    for position, parts in pieces:
        heights = jax.random.uniform(jax.random.fold_in(jax.random.fold_in(rng, 6), position), (parts,), jnp.float32, smallest / len(pieces), top_value / len(pieces))
        level = level * jnp.repeat(jnp.exp(heights), dims[position] // parts).reshape((-1,) + (1,) * (len(dims) - 1 - position))
    return level


def bell_draw(stream_key, dims, spread, most, cuts=(), kind=jnp.bfloat16):
    entries = jax.random.normal(stream_key, dims, jnp.float32) * spread
    if len(cuts) > 0:
        entries = block_scale(stream_key, dims, cuts, -0.22, 0.18) * entries
    return jnp.clip(entries, min=-most, max=most).astype(kind)


def setup_inputs(seed: int = 0) -> dict:
    keys = jax.random.split(jax.random.key(seed), 9)
    return {
        "field": bell_draw(keys[0], (LATITUDES, LONGITUDES, CHANNELS), 1.0, 6.0, ((0, 16), (1, 8))),
        "cotangent": bell_draw(keys[1], (LATITUDES, LONGITUDES, CHANNELS), 1.0, 6.0, ((0, 16), (1, 8))),
        "kernel_weights": bell_draw(keys[2], (KERNELS, CHANNELS, CHANNELS), (KERNELS * CHANNELS) ** -0.5, 0.1875),
        "spectral_weight": bell_draw(keys[3], (CHANNELS, CHANNELS), CHANNELS ** -0.5, 0.3125),
        "out_weight": bell_draw(keys[4], (CHANNELS, CHANNELS), CHANNELS ** -0.5, 0.3125),
        "degree_gain": jnp.clip(jnp.exp(jax.random.uniform(keys[5], (DEGREES, CHANNELS), jnp.float32, math.log(0.5), math.log(4.0))), 0.5, 4.0),
        "kernel_basis": bell_draw(keys[6], (KERNELS, 3, 2 * LON_SPAN + 1, LATITUDES), 0.3, 2.5, (), jnp.float32),
        "lon_reach": draw_lon_reach(jax.random.fold_in(keys[8], 71), 0),
    }


def colatitudes(row_index, lat_count):
    return (row_index.astype(jnp.float32) + 0.5) * (math.pi / lat_count)

def quadrature(colatitude, lat_count, lon_count):
    return 2.0 * math.pi / lon_count * (math.pi / lat_count) * jnp.sin(colatitude)

def legendre_table(colatitude, orders, degree_count):
    cos_rows = jnp.cos(colatitude)[:, None]
    sin_rows = jnp.sin(colatitude)[:, None]
    order_f = orders.astype(jnp.float32)[None, :]
    log_start = 0.5 * (lax.lgamma(order_f + 1.5) - lax.lgamma(order_f + 1.0) - lax.lgamma(jnp.float32(1.5) + 0.0 * order_f)) + order_f * jnp.log(sin_rows)
    diagonal = jnp.exp(log_start) / math.sqrt(4.0 * math.pi)

    def advance(running, degree):
        previous, before, ratio_prev = running
        degree_f = degree.astype(jnp.float32)
        above = degree_f > order_f
        denominator = jnp.where(above, degree_f * degree_f - order_f * order_f, 1.0)
        ratio_now = jnp.where(above, jnp.sqrt((4.0 * degree_f * degree_f - 1.0) / denominator), 1.0)
        current = jnp.where(degree_f == order_f, diagonal, jnp.where(above, ratio_now * (cos_rows * previous - before / ratio_prev), 0.0))
        return ((current, previous, ratio_now), current)
    blank = jnp.zeros((colatitude.shape[0], orders.shape[0]), jnp.float32)
    initial = (blank, blank, jnp.ones((1, orders.shape[0]), jnp.float32))
    final_state, legendre_values = lax.scan(advance, initial, jnp.arange(degree_count, dtype=jnp.int32))
    return legendre_values

def fourier_table(lon_count, order_count):
    columns = jnp.arange(2 * order_count, dtype=jnp.int32)
    orders = columns % order_count
    row_index = jnp.arange(lon_count, dtype=jnp.int32)
    angles = (row_index[:, None] * orders[None, :] % lon_count).astype(jnp.float32) * (2.0 * math.pi / lon_count)
    return jnp.where(columns[None, :] < order_count, jnp.cos(angles), -jnp.sin(angles)).astype(jnp.bfloat16)

def tap_table(kernel_basis, lon_reach):
    tap_count = kernel_basis.shape[2]
    offsets = jnp.abs(jnp.arange(tap_count, dtype=jnp.int32) - tap_count // 2)
    reach_mask = offsets[None, :, None] <= lon_reach[:, None, :]
    return kernel_basis * reach_mask[None].astype(jnp.float32)

def gelu_value(pre_act):
    inside = 0.7978845608 * (pre_act + 0.044715 * pre_act * pre_act * pre_act)
    return 0.5 * pre_act * (1.0 + jnp.tanh(inside))

def gelu_slope(pre_act):
    inside = 0.7978845608 * (pre_act + 0.044715 * pre_act * pre_act * pre_act)
    tangent = jnp.tanh(inside)
    return 0.5 * (1.0 + tangent) + 0.5 * pre_act * (1.0 - tangent * tangent) * 0.7978845608 * (1.0 + 3.0 * 0.044715 * pre_act * pre_act)

def analyze(inputs, legendre):
    blocked_in = inputs.reshape(inputs.shape[0], N_LAT, LAT_DEV, inputs.shape[2])
    blocked_table = legendre.reshape(legendre.shape[0], N_LAT, LAT_DEV, legendre.shape[2])

    def add_block(running, block_index):
        table_rows = lax.dynamic_index_in_dim(blocked_table, block_index, 1, keepdims=False)
        input_rows = lax.dynamic_index_in_dim(blocked_in, block_index, 1, keepdims=False)
        block_term = jnp.einsum('lag,cag->lcg', table_rows, input_rows, precision=lax.Precision.HIGHEST)
        return (running + lax.optimization_barrier(block_term.astype(jnp.bfloat16)).astype(jnp.float32), None)
    initial = jnp.zeros((legendre.shape[0], inputs.shape[0], inputs.shape[2]), jnp.float32)
    result, unused = lax.scan(add_block, initial, jnp.arange(N_LAT, dtype=jnp.int32))
    return result

def kernel_apply(field, tap_weights):
    padded_rows = jnp.pad(field, ((1, 1), (0, 0), (0, 0)))
    extended = jnp.concatenate([padded_rows[:, -LON_SPAN:], padded_rows, padded_rows[:, :LON_SPAN]], axis=1)
    outputs = []
    for kernel in range(KERNELS):
        summed = jnp.zeros(field.shape, jnp.float32)
        for lat_step in range(3):
            for lon_step in range(2 * LON_SPAN + 1):
                window = extended[lat_step:lat_step + LATITUDES, lon_step:lon_step + LONGITUDES, :]
                summed = summed + tap_weights[kernel, lat_step, lon_step, :, None, None] * window.astype(jnp.float32)
        outputs.append(summed.astype(jnp.bfloat16))
    return jnp.stack(outputs)

def kernel_adjoint(grad_kernel, tap_weights):
    padded_rows = jnp.pad(grad_kernel, ((0, 0), (1, 1), (0, 0), (0, 0)))
    extended = jnp.concatenate([padded_rows[:, :, -LON_SPAN:], padded_rows, padded_rows[:, :, :LON_SPAN]], axis=2)
    tap_rows = jnp.pad(tap_weights, ((0, 0), (0, 0), (0, 0), (1, 1)))
    summed = jnp.zeros(grad_kernel.shape[1:], jnp.float32)
    for lat_step in range(3):
        row_first = 2 - lat_step
        for lon_step in range(2 * LON_SPAN + 1):
            col_first = 2 * LON_SPAN - lon_step
            for kernel in range(KERNELS):
                window = extended[kernel, row_first:row_first + LATITUDES, col_first:col_first + LONGITUDES, :]
                summed = summed + tap_rows[kernel, lat_step, lon_step, row_first:row_first + LATITUDES, None, None] * window.astype(jnp.float32)
    return summed

def reference(field, cotangent, kernel_weights, spectral_weight, out_weight, degree_gain, kernel_basis, lon_reach):
    tap_weights = tap_table(kernel_basis, lon_reach)
    kernel_out = kernel_apply(field, tap_weights)
    kernel_mix = jnp.zeros((LATITUDES * LONGITUDES, CHANNELS), jnp.float32)
    for kernel in range(KERNELS):
        kernel_mix = kernel_mix + jnp.dot(kernel_out[kernel].reshape(-1, CHANNELS), kernel_weights[kernel], preferred_element_type=jnp.float32)
    field_rows = field.reshape(-1, CHANNELS)
    mixed_in = jnp.dot(field_rows, spectral_weight, preferred_element_type=jnp.float32).astype(jnp.bfloat16).reshape(field.shape)
    table_values = fourier_table(LONGITUDES, ORDERS).astype(jnp.float32)
    orders_all = jnp.arange(2 * ORDERS, dtype=jnp.int32) % ORDERS
    mode_weight = jnp.where(orders_all == 0, 1.0, 2.0).astype(jnp.float32)
    colatitude_all = colatitudes(jnp.arange(LATITUDES, dtype=jnp.int32), LATITUDES)
    quad_weights = quadrature(colatitude_all, LATITUDES, LONGITUDES)
    legendre = legendre_table(colatitude_all, orders_all, DEGREES)
    forward_modes = jnp.einsum('ajc,jq->caq', mixed_in.astype(jnp.float32), table_values, precision=lax.Precision.HIGHEST)
    band_sums = analyze(quad_weights[None, :, None] * forward_modes, legendre)
    filtered = (degree_gain[:, :, None] * band_sums).astype(jnp.bfloat16)
    synth_rows = jnp.einsum('lag,lcg->cag', legendre, filtered.astype(jnp.float32), precision=lax.Precision.HIGHEST).astype(jnp.bfloat16)
    scaled_rows = (synth_rows * mode_weight.astype(jnp.bfloat16)[None, None, :]).astype(jnp.float32)
    spectral_out = jnp.einsum('caq,jq->ajc', scaled_rows, table_values, precision=lax.Precision.HIGHEST).astype(jnp.bfloat16)
    pre_act = kernel_mix + spectral_out.reshape(-1, CHANNELS).astype(jnp.float32)
    hidden = gelu_value(pre_act).astype(jnp.bfloat16)
    output_field = (field_rows.astype(jnp.float32) + jnp.dot(hidden, out_weight, preferred_element_type=jnp.float32)).astype(jnp.bfloat16).reshape(field.shape)
    cotangent_rows = cotangent.reshape(-1, CHANNELS)
    grad_hidden = jnp.dot(cotangent_rows, out_weight.T, preferred_element_type=jnp.float32).astype(jnp.bfloat16)
    grad_pre = (grad_hidden.astype(jnp.float32) * gelu_slope(pre_act)).astype(jnp.bfloat16)
    grad_out_w = jnp.dot(hidden.T, cotangent_rows, preferred_element_type=jnp.float32)
    grad_grid = grad_pre.reshape(field.shape)
    grad_modes = mode_weight[None, None, :] * jnp.einsum('ajc,jq->caq', grad_grid.astype(jnp.float32), table_values, precision=lax.Precision.HIGHEST)
    grad_sums = analyze(grad_modes, legendre)
    grad_filtered = (degree_gain[:, :, None] * grad_sums).astype(jnp.bfloat16)
    grad_synth = (quad_weights[None, :, None] * jnp.einsum('lag,lcg->cag', legendre, grad_filtered.astype(jnp.float32), precision=lax.Precision.HIGHEST)).astype(jnp.bfloat16)
    grad_mixed = jnp.einsum('caq,jq->ajc', grad_synth.astype(jnp.float32), table_values, precision=lax.Precision.HIGHEST).astype(jnp.bfloat16).reshape(-1, CHANNELS)
    grad_mix_w = jnp.dot(field_rows.T, grad_mixed, preferred_element_type=jnp.float32)
    grad_kernel = jnp.stack([jnp.dot(grad_pre, kernel_weights[kernel].T, preferred_element_type=jnp.float32).astype(jnp.bfloat16) for kernel in range(KERNELS)])
    grad_kernel_w = jnp.stack([jnp.dot(kernel_out[kernel].reshape(-1, CHANNELS).T, grad_pre, preferred_element_type=jnp.float32) for kernel in range(KERNELS)])
    adjoint = kernel_adjoint(grad_kernel.reshape(KERNELS, LATITUDES, LONGITUDES, CHANNELS), tap_weights).reshape(-1, CHANNELS)
    grad_field = (cotangent_rows.astype(jnp.float32) + adjoint + jnp.dot(grad_mixed, spectral_weight.T, preferred_element_type=jnp.float32)).astype(jnp.bfloat16).reshape(field.shape)
    weight_grads = jnp.concatenate([grad_kernel_w, grad_mix_w[None], grad_out_w[None]], axis=0) / math.sqrt(LATITUDES * LONGITUDES)
    gain_grad = lax.optimization_barrier(jnp.sum(band_sums * grad_sums, axis=2))
    return (output_field, grad_field, weight_grads, gain_grad)
```

```python
import functools
import math

import jax
import jax.numpy as jnp
from jax import lax
from jax.experimental import pallas as pl
from jax.experimental.pallas import tpu as pltpu
from jax.sharding import PartitionSpec as P

ORDERS = 192
BF = jnp.bfloat16
F32 = jnp.float32
VMEM = pl.BlockSpec(memory_space=pltpu.VMEM)
ROWS = 96
EXT = 128


def dot(a, b, dims=((1,), (0,))):
    return lax.dot_general(a, b, (dims, ((), ())), preferred_element_type=F32)


def ring(x, axis, step, closed):
    n = lax.axis_size(axis)
    pairs = [(i, (i + step) % n) for i in range(n)]
    if not closed:
        pairs = [(a, b) for a, b in pairs if b - a == step]
    return lax.ppermute(x, axis, pairs)


def extend(x):
    rows, cells, chans = x.shape
    left = ring(x[:, cells - 3 :], "lon", 1, True)
    right = ring(x[:, :3], "lon", -1, True)
    gap = jnp.zeros((rows, EXT - cells - 6, chans), x.dtype)
    wide = jnp.concatenate([x, right, gap, left], axis=1)
    above = ring(wide[rows - 1 :], "lat", 1, False)
    below = ring(wide[:1], "lat", -1, False)
    return jnp.concatenate([above, wide, below], axis=0)


def tap_rows(taps):
    k, r, t, n = taps.shape
    flat = jnp.transpose(taps, (3, 0, 1, 2)).reshape(n, k * r, t)
    wide = jnp.concatenate([flat[:, :, 3:], jnp.zeros((n, k * r, EXT - t), F32), flat[:, :, :3]], axis=2)
    return jnp.pad(wide, ((0, 0), (0, 16 - k * r), (0, 0)))


def band_matrix(taps_ref, i, band_ref, cells):
    keep = lax.broadcasted_iota(jnp.int32, (ROWS, EXT), 0) < cells
    rows = taps_ref[i]
    for k in range(3):
        for r in range(3):
            row = jnp.broadcast_to(rows[3 * k + r : 3 * k + r + 1], (ROWS, EXT))
            block = pltpu.roll(row, 0, 1, stride=1, stride_axis=0)
            band_ref[k * ROWS : (k + 1) * ROWS, r * EXT : (r + 1) * EXT] = jnp.where(keep, block, 0.0).astype(BF)


def stencil_forward(cells, ext_ref, taps_ref, w_ref, out_ref, band_ref):
    def step(i, carry):
        band_matrix(taps_ref, i, band_ref, cells)
        source = ext_ref[pl.ds(i, 3)].reshape(3 * EXT, -1)
        total = None
        for k in range(3):
            part = dot(band_ref[k * ROWS : (k + 1) * ROWS], source).astype(BF)
            part = dot(part, w_ref[k])
            total = part if total is None else total + part
        out_ref[i] = total
        return carry

    lax.fori_loop(0, out_ref.shape[0], step, 0)


def stencil_backward(cells, ext_ref, taps_ref, wt_ref, field_ref, adj_ref, grad_ref, band_ref, part_ref):
    grad_ref[...] = jnp.zeros_like(grad_ref)
    group = 4

    def outer(o, carry):
        def step(a, inner):
            i = o * group + a
            band_matrix(taps_ref, i, band_ref, cells)
            source = ext_ref[pl.ds(i, 3)].reshape(3 * EXT, -1)
            total = None
            for k in range(3):
                part = dot(band_ref[k * ROWS : (k + 1) * ROWS], source).astype(BF)
                part_ref[k, a] = part
                part = dot(part, wt_ref[k])
                total = part if total is None else total + part
            adj_ref[i] = total
            return inner

        lax.fori_loop(0, group, step, 0)
        rows = field_ref[pl.ds(o * group, group)].reshape(group * ROWS, -1)
        for k in range(3):
            grad_ref[k] += dot(rows, part_ref[k].reshape(group * ROWS, -1), ((0,), (0,)))
        return carry

    lax.fori_loop(0, adj_ref.shape[0] // group, outer, 0)


def pointwise(cells, km_ref, so_ref, f_ref, ct_ref, w_ref, wt_ref, out_ref, gp_ref, gow_ref):
    @pl.when(pl.program_id(0) == 0)
    def _():
        gow_ref[...] = jnp.zeros_like(gow_ref)

    group, rows, chans = km_ref.shape
    flat = (group * rows, chans)
    v = (km_ref[...] + so_ref[...].astype(F32)).reshape(flat)
    ct = ct_ref[...].reshape(flat)
    square = v * v
    s = jnp.tanh(0.7978845608 * v * (1.0 + 0.044715 * square))
    half = 0.5 * (1.0 + s)
    hidden = (v * half).astype(BF)
    slope = half + 0.5 * v * (1.0 - s * s) * (0.7978845608 * (1.0 + 3.0 * 0.044715 * square))
    out = f_ref[...].astype(F32) + dot(hidden, w_ref[...]).reshape(km_ref.shape)
    out_ref[...] = out.astype(BF)[:, :cells]
    gp_ref[...] = (dot(ct, wt_ref[...]) * slope).astype(BF).reshape(km_ref.shape)
    gow_ref[...] += dot(hidden, ct, ((0,), (0,)))


def finish(cells, adj_ref, gm_ref, f_ref, ct_ref, wt_ref, out_ref, gmw_ref):
    @pl.when(pl.program_id(0) == 0)
    def _():
        gmw_ref[...] = jnp.zeros_like(gmw_ref)

    group, rows, chans = adj_ref.shape
    flat = (group * rows, chans)
    gm = gm_ref[...].reshape(flat)
    out = ct_ref[...].astype(F32) + adj_ref[...] + dot(gm, wt_ref[...]).reshape(adj_ref.shape)
    out_ref[...] = out.astype(BF)[:, :cells]
    gmw_ref[...] += dot(f_ref[...].reshape(flat), gm, ((0,), (0,)))


def legendre_kernel(m_ref, x_ref, diag_ref, out_ref):
    m = m_ref[...]
    x = x_ref[...]
    diag = diag_ref[...]
    reps = x.shape[1] // m.shape[1]

    def wide(a):
        return jnp.concatenate([a] * reps, axis=1)

    mw = wide(m)

    def step(l, carry):
        prev, before, a_prev = carry
        lf = l.astype(F32)
        above = lf > m
        den = jnp.where(above, lf * lf - m * m, 1.0)
        a = jnp.where(above, jnp.sqrt((4.0 * lf * lf - 1.0) / den), 1.0)
        cur = wide(a) * (x * prev - before * wide(1.0 / a_prev))
        cur = jnp.where(lf == mw, diag, jnp.where(lf > mw, cur, 0.0))
        out_ref[l] = cur.astype(BF)
        return cur, prev, a

    blank = x * 0.0
    lax.fori_loop(0, out_ref.shape[0], step, (blank, blank, m * 0.0 + 1.0), unroll=4)


def colatitudes(row_index, lat_count):
    return (row_index.astype(F32) + 0.5) * (math.pi / lat_count)


def legendre_rows(orders, lat_count, degrees):
    slots = 16
    m = jnp.pad(orders, (0, slots - orders.shape[0])).astype(F32)[:, None]
    colat = colatitudes(jnp.arange(lat_count, dtype=jnp.int32), lat_count)[None, :]
    log_start = 0.5 * (lax.lgamma(m + 1.5) - lax.lgamma(m + 1.0) - lax.lgamma(F32(1.5) + 0.0 * m))
    diag = jnp.exp(log_start + m * jnp.log(jnp.sin(colat))) / math.sqrt(4.0 * math.pi)
    x = jnp.broadcast_to(jnp.cos(colat), diag.shape)
    table = pl.pallas_call(
        legendre_kernel,
        out_shape=jax.ShapeDtypeStruct((degrees, slots, lat_count), BF),
        in_specs=[VMEM] * 3,
        out_specs=VMEM,
        compiler_params=pltpu.CompilerParams(vmem_limit_bytes=40 << 20),
    )(jnp.broadcast_to(m, (slots, 128)), x, diag)
    return jnp.transpose(table[:, : orders.shape[0]], (1, 0, 2))


def fourier(lon_count, orders):
    j = jnp.arange(lon_count, dtype=jnp.int32)
    angles = (j[:, None] * orders[None, :] % lon_count).astype(F32) * (2.0 * math.pi / lon_count)
    return jnp.stack([jnp.cos(angles), -jnp.sin(angles)], axis=-1).astype(BF)


def tap_table(kernel_basis, lon_reach):
    count = kernel_basis.shape[2]
    offsets = jnp.abs(jnp.arange(count, dtype=jnp.int32) - count // 2)
    mask = offsets[None, :, None] <= lon_reach[:, None, :]
    return kernel_basis * mask[None].astype(F32)


def call(body, outs, scratch, limit=56, **kw):
    return pl.pallas_call(
        body,
        out_shape=outs,
        out_specs=jax.tree.map(lambda _: VMEM, outs),
        scratch_shapes=scratch,
        compiler_params=pltpu.CompilerParams(vmem_limit_bytes=limit << 20),
        **kw,
    )


def by_rows(body, args, whole, outs, totals, group=4):
    def cut(a):
        return pl.BlockSpec((group,) + a.shape[1:], lambda g: (g, 0, 0))

    def full(a):
        return pl.BlockSpec(a.shape, lambda g: (0,) * len(a.shape))

    return pl.pallas_call(
        body,
        grid=(args[0].shape[0] // group,),
        in_specs=[cut(a) for a in args] + [full(a) for a in whole],
        out_specs=[cut(a) for a in outs] + [full(a) for a in totals],
        out_shape=list(outs) + list(totals),
        compiler_params=pltpu.CompilerParams(vmem_limit_bytes=56 << 20),
    )(*args, *whole)


def local(field, cotangent, kernel_weights, spectral_weight, out_weight, degree_gain, kernel_basis, lon_reach):
    rows, cells, chans = field.shape
    lat_parts, lon_parts = lax.axis_size("lat"), lax.axis_size("lon")
    lat, lon = lax.axis_index("lat"), lax.axis_index("lon")
    lat_count, lon_count = rows * lat_parts, cells * lon_parts
    share = chans // lon_parts
    degrees = degree_gain.shape[0]
    slots = ORDERS // lat_parts
    shape = jax.ShapeDtypeStruct

    taps = tap_table(kernel_basis, lon_reach)
    near = lax.dynamic_slice_in_dim(jnp.pad(taps, ((0, 0), (0, 0), (0, 0), (1, 1))), lat * rows, rows + 2, 3)
    own_taps = tap_rows(near[:, :, :, 1 : rows + 1])
    turned = near[:, ::-1, ::-1]
    adj_taps = tap_rows(jnp.stack([turned[:, r, :, r : r + rows] for r in range(3)], axis=1))

    all_orders = jnp.arange(ORDERS, dtype=jnp.int32).reshape(lat_parts, slots)
    my_orders = lat * slots + jnp.arange(slots, dtype=jnp.int32)
    table = legendre_rows(my_orders, lat_count, degrees)
    waves = fourier(lon_count, all_orders.reshape(-1)).reshape(lon_count, 2 * ORDERS)
    quad = 2.0 * math.pi / lon_count * (math.pi / lat_count) * jnp.sin(
        colatitudes(jnp.arange(lat_count, dtype=jnp.int32), lat_count)
    )
    quad = quad.reshape(1, lat_count, 1, 1)
    mode_weight = jnp.where(my_orders == 0, 1.0, 2.0).astype(F32)[:, None, None, None]
    gain = lax.dynamic_slice_in_dim(degree_gain, lon * share, share, 1)[None, :, None, :]

    def spectral(grid, scale_in, scale_out):
        send = grid.reshape(rows, cells, lon_parts, share).transpose(2, 1, 0, 3).reshape(lon_parts, cells, rows * share)
        columns = lax.all_to_all(send, "lon", 0, 0, tiled=True).reshape(lon_count, rows * share)
        modes = dot(waves, columns, ((0,), (0,))).astype(BF)
        modes = lax.all_to_all(modes.reshape(lat_parts, 2 * slots, rows * share), "lat", 0, 0, tiled=True)
        modes = modes.reshape(lat_parts, slots, 2, rows, share).transpose(1, 0, 3, 2, 4)
        modes = modes.reshape(slots, lat_count, 2, share)
        modes = (modes.astype(F32) * scale_in).astype(BF)
        bands = jnp.einsum("sli,sipc->slpc", table, modes, preferred_element_type=F32)
        filtered = (gain * bands).astype(BF)
        synth = jnp.einsum("sli,slpc->sipc", table, filtered, preferred_element_type=F32)
        synth = (synth * scale_out).astype(BF)
        synth = synth.reshape(slots, lat_parts, rows, 2, share).transpose(1, 0, 3, 2, 4)
        synth = lax.all_to_all(synth.reshape(lat_parts, 2 * slots, rows * share), "lat", 0, 0, tiled=True)
        back = dot(waves, synth.reshape(2 * ORDERS, rows * share)).astype(BF)
        back = lax.all_to_all(back.reshape(lon_parts, cells, rows * share), "lon", 0, 0, tiled=True)
        back = back.reshape(lon_parts, cells, rows, share).transpose(2, 1, 0, 3).reshape(rows, cells, chans)
        return bands, back

    padding = ((0, 0), (0, ROWS - cells), (0, 0))
    field_pad = jnp.pad(field, padding)
    cot_pad = jnp.pad(cotangent, padding)
    ext = extend(field)
    kernel_mix = call(
        functools.partial(stencil_forward, cells),
        shape((rows, ROWS, chans), F32),
        [pltpu.VMEM((3 * ROWS, 3 * EXT), BF)],
        in_specs=[VMEM] * 3,
    )(ext, own_taps, kernel_weights)
    mixed = jnp.dot(field.reshape(-1, chans), spectral_weight, preferred_element_type=F32).astype(BF).reshape(field.shape)
    bands, spec_out = spectral(mixed, quad, mode_weight)
    output_field, grad_pre, grad_out_w = by_rows(
        functools.partial(pointwise, cells),
        [kernel_mix, jnp.pad(spec_out, padding), field_pad, cot_pad],
        [out_weight, out_weight.T],
        [shape(field.shape, BF), shape((rows, ROWS, chans), BF)],
        [shape((chans, chans), F32)],
    )
    grad_pre_cut = grad_pre[:, :cells]
    adj, grad_kernel_w = call(
        functools.partial(stencil_backward, cells),
        [shape((rows, ROWS, chans), F32), shape((3, chans, chans), F32)],
        [pltpu.VMEM((3 * ROWS, 3 * EXT), BF), pltpu.VMEM((3, 4, ROWS, chans), BF)],
        in_specs=[VMEM] * 4,
    )(extend(grad_pre_cut), adj_taps, jnp.transpose(kernel_weights, (0, 2, 1)), field_pad)
    grad_bands, grad_mixed = spectral(grad_pre_cut, mode_weight, quad)
    gain_part = jnp.sum(bands * grad_bands, axis=(0, 2))
    gain_place = lax.dynamic_update_slice(jnp.zeros((degrees, chans), F32), gain_part, (0, lon * share))
    early = lax.psum((jnp.concatenate([grad_kernel_w, grad_out_w[None]]), gain_place), ("lat", "lon"))
    grad_field, grad_mix_w = by_rows(
        functools.partial(finish, cells),
        [adj, jnp.pad(grad_mixed, padding), field_pad, cot_pad],
        [spectral_weight.T],
        [shape(field.shape, BF)],
        [shape((chans, chans), F32)],
    )
    grad_mix_w = lax.psum(grad_mix_w, ("lat", "lon"))
    weight_grads = jnp.concatenate([early[0][:3], grad_mix_w[None], early[0][3:]]) / math.sqrt(lat_count * lon_count)
    return output_field, grad_field, weight_grads, early[1]


def solution(mesh):
    placed = (P("lat", "lon", None), P("lat", "lon", None), P(), P(), P(), P(), P(), P())
    return jax.shard_map(
        local,
        mesh=mesh,
        in_specs=placed,
        out_specs=(P("lat", "lon", None), P("lat", "lon", None), P(), P()),
        check_vma=False,
    )
```

```python
import functools
import math

import jax
import jax.numpy as jnp
from jax import lax
from jax.experimental import pallas as pl
from jax.experimental.pallas import tpu as pltpu
from jax.sharding import PartitionSpec as P

ORDERS = 192
BF = jnp.bfloat16
F32 = jnp.float32
VMEM = pl.BlockSpec(memory_space=pltpu.VMEM)
ROWS = 96
EXT = 128


def dot(a, b, dims=((1,), (0,))):
    return lax.dot_general(a, b, (dims, ((), ())), preferred_element_type=F32)


def ring(x, axis, step, closed):
    n = lax.axis_size(axis)
    pairs = [(i, (i + step) % n) for i in range(n)]
    if not closed:
        pairs = [(a, b) for a, b in pairs if b - a == step]
    return lax.ppermute(x, axis, pairs)


def extend(x):
    rows, cells, chans = x.shape
    left = ring(x[:, cells - 3 :], "lon", 1, True)
    right = ring(x[:, :3], "lon", -1, True)
    gap = jnp.zeros((rows, EXT - cells - 6, chans), x.dtype)
    wide = jnp.concatenate([x, right, gap, left], axis=1)
    above = ring(wide[rows - 1 :], "lat", 1, False)
    below = ring(wide[:1], "lat", -1, False)
    return jnp.concatenate([above, wide, below], axis=0)


def tap_rows(taps):
    k, r, t, n = taps.shape
    flat = jnp.transpose(taps, (3, 0, 1, 2)).reshape(n, k * r, t)
    wide = jnp.concatenate([flat[:, :, 3:], jnp.zeros((n, k * r, EXT - t), F32), flat[:, :, :3]], axis=2)
    return jnp.pad(wide, ((0, 0), (0, 16 - k * r), (0, 0)))


def band_matrix(taps_ref, i, band_ref, cells):
    keep = lax.broadcasted_iota(jnp.int32, (ROWS, EXT), 0) < cells
    rows = taps_ref[i]
    for k in range(3):
        for r in range(3):
            row = jnp.broadcast_to(rows[3 * k + r : 3 * k + r + 1], (ROWS, EXT))
            block = pltpu.roll(row, 0, 1, stride=1, stride_axis=0)
            band_ref[k * ROWS : (k + 1) * ROWS, r * EXT : (r + 1) * EXT] = jnp.where(keep, block, 0.0).astype(BF)


def stencil_forward(cells, ext_ref, taps_ref, w_ref, out_ref, band_ref):
    def step(i, carry):
        band_matrix(taps_ref, i, band_ref, cells)
        source = ext_ref[pl.ds(i, 3)].reshape(3 * EXT, -1)
        total = None
        for k in range(3):
            part = dot(band_ref[k * ROWS : (k + 1) * ROWS], source).astype(BF)
            part = dot(part, w_ref[k])
            total = part if total is None else total + part
        out_ref[i] = total
        return carry

    lax.fori_loop(0, out_ref.shape[0], step, 0)


def stencil_backward(cells, ext_ref, taps_ref, wt_ref, field_ref, adj_ref, grad_ref, band_ref, part_ref):
    grad_ref[...] = jnp.zeros_like(grad_ref)
    group = 4

    def outer(o, carry):
        def step(a, inner):
            i = o * group + a
            band_matrix(taps_ref, i, band_ref, cells)
            source = ext_ref[pl.ds(i, 3)].reshape(3 * EXT, -1)
            total = None
            for k in range(3):
                part = dot(band_ref[k * ROWS : (k + 1) * ROWS], source).astype(BF)
                part_ref[k, a] = part
                part = dot(part, wt_ref[k])
                total = part if total is None else total + part
            adj_ref[i] = total
            return inner

        lax.fori_loop(0, group, step, 0)
        rows = field_ref[pl.ds(o * group, group)].reshape(group * ROWS, -1)
        for k in range(3):
            grad_ref[k] += dot(rows, part_ref[k].reshape(group * ROWS, -1), ((0,), (0,)))
        return carry

    lax.fori_loop(0, adj_ref.shape[0] // group, outer, 0)


def pointwise(cells, km_ref, so_ref, f_ref, ct_ref, w_ref, wt_ref, out_ref, gp_ref, gow_ref):
    @pl.when(pl.program_id(0) == 0)
    def _():
        gow_ref[...] = jnp.zeros_like(gow_ref)

    group, rows, chans = km_ref.shape
    flat = (group * rows, chans)
    v = (km_ref[...] + so_ref[...].astype(F32)).reshape(flat)
    ct = ct_ref[...].reshape(flat)
    square = v * v
    s = jnp.tanh(0.7978845608 * v * (1.0 + 0.044715 * square))
    half = 0.5 * (1.0 + s)
    hidden = (v * half).astype(BF)
    slope = half + 0.5 * v * (1.0 - s * s) * (0.7978845608 * (1.0 + 3.0 * 0.044715 * square))
    out = f_ref[...].astype(F32) + dot(hidden, w_ref[...]).reshape(km_ref.shape)
    out_ref[...] = out.astype(BF)[:, :cells]
    gp_ref[...] = (dot(ct, wt_ref[...]) * slope).astype(BF).reshape(km_ref.shape)
    gow_ref[...] += dot(hidden, ct, ((0,), (0,)))


def finish(cells, adj_ref, gm_ref, f_ref, ct_ref, wt_ref, out_ref, gmw_ref):
    @pl.when(pl.program_id(0) == 0)
    def _():
        gmw_ref[...] = jnp.zeros_like(gmw_ref)

    group, rows, chans = adj_ref.shape
    flat = (group * rows, chans)
    gm = gm_ref[...].reshape(flat)
    out = ct_ref[...].astype(F32) + adj_ref[...] + dot(gm, wt_ref[...]).reshape(adj_ref.shape)
    out_ref[...] = out.astype(BF)[:, :cells]
    gmw_ref[...] += dot(f_ref[...].reshape(flat), gm, ((0,), (0,)))


def block_swap(parts):
    group = lax.broadcasted_iota(jnp.int32, parts[0].shape, 1) // 16
    for k in range(3):
        high = (group >> k) & 1 == 1
        width = 16 << k
        fresh = list(parts)
        for a in range(8):
            if (a >> k) & 1 == 0:
                b = a + (1 << k)
                fresh[a] = jnp.where(high, pltpu.roll(parts[b], width, 1), parts[a])
                fresh[b] = jnp.where(high, parts[b], pltpu.roll(parts[a], 128 - width, 1))
        parts = fresh
    return parts


def tile_swap(x):
    row = lax.broadcasted_iota(jnp.int32, x.shape, 1)
    group = lax.broadcasted_iota(jnp.int32, x.shape, 2) // 16
    for k in range(3):
        row_bit = (row >> k) & 1
        group_bit = (group >> k) & 1
        width = 16 << k
        down = pltpu.roll(pltpu.roll(x, 8 - (1 << k), 1), width, 2)
        up = down if k == 2 else pltpu.roll(pltpu.roll(x, 1 << k, 1), 128 - width, 2)
        x = jnp.where(row_bit == group_bit, x, jnp.where(group_bit == 1, down, up))
    return x


PAD = 80


def exchange(axis, me, parts, send, recv, send_sem, recv_sem):
    def copy(v, peer, slot):
        return pltpu.make_async_remote_copy(
            src_ref=send.at[v, peer],
            dst_ref=recv.at[v, slot],
            send_sem=send_sem.at[v, peer],
            recv_sem=recv_sem.at[v, slot],
            device_id={axis: peer},
            device_id_type=pl.DeviceIdType.MESH,
        )

    def over(body):
        lax.fori_loop(1, parts, lambda d, carry: (body(lax.rem(me + d, parts)), carry)[1], 0)

    def start(v):
        over(lambda peer: copy(v, peer, me).start())
        recv[v, me] = send[v, me]

    def arrive(v):
        over(lambda peer: copy(v, peer, peer).wait_recv())

    def drain(v):
        over(lambda peer: copy(v, peer, peer).wait_send())

    return start, arrive, drain


def spectral_kernel(
    x_ref, table_ref, turned_ref, into_ref, back_ref, gain_ref, in_ref, out_ref_scale,
    grid_ref, bands_ref,
    send1, recv1, send2, recv2, send3, recv3, send4, recv4, modes, rows_ref,
    s1, r1, s2, r2, s3, r3, s4, r4,
):
    lat, lon = lax.axis_index("lat"), lax.axis_index("lon")
    lons, lats = lax.axis_size("lon"), lax.axis_size("lat")
    barrier = pltpu.get_barrier_semaphore()

    def greet(axis, me, parts):
        def body(d, carry):
            pl.semaphore_signal(
                barrier, inc=1, device_id={axis: lax.rem(me + d, parts)}, device_id_type=pl.DeviceIdType.MESH
            )
            return carry

        lax.fori_loop(1, parts, body, 0)

    greet("lon", lon, lons)
    greet("lat", lat, lats)

    start1, arrive1, drain1 = exchange("lon", lon, lons, send1, recv1, s1, r1)
    start2, arrive2, drain2 = exchange("lat", lat, lats, send2, recv2, s2, r2)
    start3, arrive3, drain3 = exchange("lat", lat, lats, send3, recv3, s3, r3)
    start4, arrive4, drain4 = exchange("lon", lon, lons, send4, recv4, s4, r4)
    order = lax.broadcasted_iota(jnp.int32, (192, 128), 1) // 32
    blank = jnp.zeros((8, 128), F32)

    def tiles(body):
        def step(n, carry):
            body(n // 6, pl.multiple_of(n % 6 * 16, 16))
            return carry

        lax.fori_loop(0, 18, step, 0)

    def split(v):
        def body(g, j):
            parts = [x_ref[g * 8 + n, pl.ds(j, 16), v * 128 : (v + 1) * 128].astype(F32) for n in range(8)]
            lanes = pl.ds(pl.multiple_of(g * 128, 128), 128)
            for p, part in enumerate(block_swap(parts)):
                send1[v, p, pl.ds(j, 16), lanes] = part.astype(BF)

        tiles(body)

    def analyse(v):
        modes[...] = dot(into_ref[...], recv1[v].reshape(768, 384))

        def step(b, carry):
            block = modes[pl.ds(pl.multiple_of(b * 24, 8), 24), :]
            turned = [tile_swap(block[:, g * 128 : (g + 1) * 128].reshape(3, 8, 128)) for g in range(3)]
            pieces = [turned[g][o] for o in range(3) for g in range(3)] + [blank]
            send2[v, b] = jnp.concatenate(pieces, axis=0).astype(BF)
            return carry

        lax.fori_loop(0, lats, step, 0)

    def filter_bands(v):
        def gather(b, carry):
            rows = pl.ds(pl.multiple_of(b * 24, 8), 24)
            block = recv2[v, b].astype(F32)
            for o in range(3):
                rows_ref[o, rows] = block[o * 24 : (o + 1) * 24] * in_ref[o, rows]
            return carry

        lax.fori_loop(0, lats, gather, 0)
        for o in range(3):
            every = dot(table_ref[o], rows_ref[o].astype(BF))
            band = every[:192]
            for m in range(1, 4):
                band = jnp.where(order == m, every[m * 192 : (m + 1) * 192], band)
            bands_ref[o, :, v * 128 : (v + 1) * 128] = band
            band = band * gain_ref[:, v * 128 : (v + 1) * 128]
            spread = jnp.concatenate([jnp.where(order == m, band, 0.0).astype(BF) for m in range(4)], axis=0)
            rows_ref[o] = dot(turned_ref[o], spread) * out_ref_scale[o]

        def scatter(b, carry):
            rows = pl.ds(pl.multiple_of(b * 24, 8), 24)
            send3[v, b] = jnp.concatenate([rows_ref[o, rows] for o in range(3)] + [blank], axis=0).astype(BF)
            return carry

        lax.fori_loop(0, lats, scatter, 0)

    def synthesise(v):
        def step(b, carry):
            block = recv3[v, b].astype(F32)[:72].reshape(9, 8, 128)
            turned = tile_swap(block)
            wide = [jnp.concatenate([turned[o * 3 + g] for o in range(3)], axis=0) for g in range(3)]
            modes[pl.ds(pl.multiple_of(b * 24, 8), 24), :] = jnp.concatenate(wide, axis=1)
            return carry

        lax.fori_loop(0, lats, step, 0)
        send4[v] = dot(back_ref[...], modes[...].astype(BF)).astype(BF).reshape(8, ROWS, 384)

    def join(v):
        def body(g, j):
            lanes = pl.ds(pl.multiple_of(g * 128, 128), 128)
            parts = [recv4[v, p, pl.ds(j, 16), lanes].astype(F32) for p in range(8)]
            for n, part in enumerate(block_swap(parts)):
                grid_ref[g * 8 + n, pl.ds(j, 16), v * 128 : (v + 1) * 128] = part.astype(BF)

        tiles(body)

    for v in range(3):
        split(v)
        if v == 0:
            pl.semaphore_wait(barrier, lons + lats - 2)
        start1(v)

    def two(v):
        arrive1(v)
        analyse(v)
        start2(v)

    def three(v):
        arrive2(v)
        filter_bands(v)
        start3(v)

    def four(v):
        arrive3(v)
        synthesise(v)
        start4(v)

    def five(v):
        arrive4(v)
        join(v)

    for stage, v in ((two, 0), (three, 0), (two, 1), (four, 0), (three, 1), (two, 2), (four, 1), (three, 2), (five, 0), (four, 2), (five, 1), (five, 2)):
        stage(v)
    for v in range(3):
        for drain in (drain1, drain2, drain3, drain4):
            drain(v)


def spectral_call(x, table, turned, into, back, gain, scale_in, scale_out):
    shape = jax.ShapeDtypeStruct
    lons, lats = lax.axis_size("lon"), lax.axis_size("lat")
    lon_buf = pltpu.VMEM((3, lons, ROWS, 384), BF)
    lat_buf = pltpu.VMEM((3, lats, PAD, 128), BF)
    lon_sem = pltpu.SemaphoreType.DMA((3, lons))
    lat_sem = pltpu.SemaphoreType.DMA((3, lats))
    return pl.pallas_call(
        spectral_kernel,
        out_shape=[shape(x.shape, BF), shape((3, 192, 384), F32)],
        in_specs=[VMEM] * 8,
        out_specs=[VMEM] * 2,
        scratch_shapes=[lon_buf, lon_buf] + [lat_buf] * 4 + [lon_buf, lon_buf]
        + [pltpu.VMEM((384, 384), F32), pltpu.VMEM((3, 384, 128), F32)]
        + [lon_sem, lon_sem, lat_sem, lat_sem, lat_sem, lat_sem, lon_sem, lon_sem],
        compiler_params=pltpu.CompilerParams(collective_id=1, has_side_effects=True, vmem_limit_bytes=56 << 20),
    )(x, table, turned, into, back, gain, scale_in, scale_out)


def legendre_kernel(m_ref, x_ref, diag_ref, out_ref):
    m = m_ref[...]
    x = x_ref[...]
    diag = diag_ref[...]
    reps = x.shape[1] // m.shape[1]

    def wide(a):
        return jnp.concatenate([a] * reps, axis=1)

    mw = wide(m)

    def step(l, carry):
        prev, before, a_prev = carry
        lf = l.astype(F32)
        above = lf > m
        den = jnp.where(above, lf * lf - m * m, 1.0)
        a = jnp.where(above, jnp.sqrt((4.0 * lf * lf - 1.0) / den), 1.0)
        cur = wide(a) * (x * prev - before * wide(1.0 / a_prev))
        cur = jnp.where(lf == mw, diag, jnp.where(lf > mw, cur, 0.0))
        out_ref[l] = cur.astype(BF)
        return cur, prev, a

    blank = x * 0.0
    lax.fori_loop(0, out_ref.shape[0], step, (blank, blank, m * 0.0 + 1.0), unroll=4)


def colatitudes(row_index, lat_count):
    return (row_index.astype(F32) + 0.5) * (math.pi / lat_count)


def legendre_rows(orders, lat_count, degrees):
    slots = 16
    m = jnp.pad(orders, (0, slots - orders.shape[0])).astype(F32)[:, None]
    colat = colatitudes(jnp.arange(lat_count, dtype=jnp.int32), lat_count)[None, :]
    log_start = 0.5 * (lax.lgamma(m + 1.5) - lax.lgamma(m + 1.0) - lax.lgamma(F32(1.5) + 0.0 * m))
    diag = jnp.exp(log_start + m * jnp.log(jnp.sin(colat))) / math.sqrt(4.0 * math.pi)
    x = jnp.broadcast_to(jnp.cos(colat), diag.shape)
    table = pl.pallas_call(
        legendre_kernel,
        out_shape=jax.ShapeDtypeStruct((degrees, slots, lat_count), BF),
        in_specs=[VMEM] * 3,
        out_specs=VMEM,
        compiler_params=pltpu.CompilerParams(vmem_limit_bytes=40 << 20),
    )(jnp.broadcast_to(m, (slots, 128)), x, diag)
    return jnp.transpose(table[:, : orders.shape[0]], (1, 0, 2))


def fourier(lon_count, orders):
    j = jnp.arange(lon_count, dtype=jnp.int32)
    angles = (j[:, None] * orders[None, :] % lon_count).astype(F32) * (2.0 * math.pi / lon_count)
    return jnp.stack([jnp.cos(angles), -jnp.sin(angles)], axis=-1).astype(BF)


def tap_table(kernel_basis, lon_reach):
    count = kernel_basis.shape[2]
    offsets = jnp.abs(jnp.arange(count, dtype=jnp.int32) - count // 2)
    mask = offsets[None, :, None] <= lon_reach[:, None, :]
    return kernel_basis * mask[None].astype(F32)


def call(body, outs, scratch, limit=56, **kw):
    return pl.pallas_call(
        body,
        out_shape=outs,
        out_specs=jax.tree.map(lambda _: VMEM, outs),
        scratch_shapes=scratch,
        compiler_params=pltpu.CompilerParams(vmem_limit_bytes=limit << 20),
        **kw,
    )


def by_rows(body, args, whole, outs, totals, group=4):
    def cut(a):
        return pl.BlockSpec((group,) + a.shape[1:], lambda g: (g, 0, 0))

    def full(a):
        return pl.BlockSpec(a.shape, lambda g: (0,) * len(a.shape))

    return pl.pallas_call(
        body,
        grid=(args[0].shape[0] // group,),
        in_specs=[cut(a) for a in args] + [full(a) for a in whole],
        out_specs=[cut(a) for a in outs] + [full(a) for a in totals],
        out_shape=list(outs) + list(totals),
        compiler_params=pltpu.CompilerParams(vmem_limit_bytes=56 << 20),
    )(*args, *whole)


def local(field, cotangent, kernel_weights, spectral_weight, out_weight, degree_gain, kernel_basis, lon_reach):
    rows, cells, chans = field.shape
    lat_parts, lon_parts = lax.axis_size("lat"), lax.axis_size("lon")
    lat, lon = lax.axis_index("lat"), lax.axis_index("lon")
    lat_count, lon_count = rows * lat_parts, cells * lon_parts
    degrees = degree_gain.shape[0]
    slots = ORDERS // lat_parts
    shape = jax.ShapeDtypeStruct

    taps = tap_table(kernel_basis, lon_reach)
    near = lax.dynamic_slice_in_dim(jnp.pad(taps, ((0, 0), (0, 0), (0, 0), (1, 1))), lat * rows, rows + 2, 3)
    own_taps = tap_rows(near[:, :, :, 1 : rows + 1])
    turned = near[:, ::-1, ::-1]
    adj_taps = tap_rows(jnp.stack([turned[:, r, :, r : r + rows] for r in range(3)], axis=1))

    all_orders = jnp.arange(ORDERS, dtype=jnp.int32).reshape(lat_parts, slots)
    my_orders = lat * slots + jnp.arange(slots, dtype=jnp.int32)
    table = legendre_rows(my_orders, lat_count, degrees)
    waves = fourier(lon_count, all_orders.reshape(-1)).reshape(lon_count, 2 * ORDERS)
    waves = jnp.pad(waves.reshape(lon_parts, cells, -1), ((0, 0), (0, ROWS - cells), (0, 0))).reshape(lon_parts * ROWS, -1)
    table = table.reshape(3, 4 * degrees, lat_count)
    turned = jnp.transpose(table, (0, 2, 1))
    quad = 2.0 * math.pi / lon_count * (math.pi / lat_count) * jnp.sin(
        colatitudes(jnp.arange(lat_count, dtype=jnp.int32), lat_count)
    )
    quad = jnp.broadcast_to(quad[None, :, None], (3, lat_count, 128))
    mode_weight = jnp.where(my_orders == 0, 1.0, 2.0).astype(F32).reshape(3, 1, 4, 1)
    mode_weight = jnp.broadcast_to(mode_weight, (3, lat_count, 4, 32)).reshape(3, lat_count, 128)
    groups = degree_gain.reshape(degrees, 3, lon_parts, 16)
    gain = lax.dynamic_slice_in_dim(groups, lon, 1, 2)
    gain = jnp.broadcast_to(gain, groups.shape).reshape(degrees, chans)

    def spectral(grid, scale_in, scale_out):
        return spectral_call(grid, table, turned, waves.T, waves, gain, scale_in, scale_out)

    padding = ((0, 0), (0, ROWS - cells), (0, 0))
    field_pad = jnp.pad(field, padding)
    cot_pad = jnp.pad(cotangent, padding)
    ext = extend(field)
    kernel_mix = call(
        functools.partial(stencil_forward, cells),
        shape((rows, ROWS, chans), F32),
        [pltpu.VMEM((3 * ROWS, 3 * EXT), BF)],
        in_specs=[VMEM] * 3,
    )(ext, own_taps, kernel_weights)
    mixed = jnp.dot(field.reshape(-1, chans), spectral_weight, preferred_element_type=F32).astype(BF).reshape(field.shape)
    spec_out, bands = spectral(jnp.pad(mixed, padding), quad, mode_weight)
    output_field, grad_pre, grad_out_w = by_rows(
        functools.partial(pointwise, cells),
        [kernel_mix, spec_out, field_pad, cot_pad],
        [out_weight, out_weight.T],
        [shape(field.shape, BF), shape((rows, ROWS, chans), BF)],
        [shape((chans, chans), F32)],
    )
    grad_pre_cut = grad_pre[:, :cells]
    adj, grad_kernel_w = call(
        functools.partial(stencil_backward, cells),
        [shape((rows, ROWS, chans), F32), shape((3, chans, chans), F32)],
        [pltpu.VMEM((3 * ROWS, 3 * EXT), BF), pltpu.VMEM((3, 4, ROWS, chans), BF)],
        in_specs=[VMEM] * 4,
    )(extend(grad_pre_cut), adj_taps, jnp.transpose(kernel_weights, (0, 2, 1)), field_pad)
    grad_mixed, grad_bands = spectral(grad_pre, mode_weight, quad)
    gain_part = jnp.sum(bands * grad_bands, axis=0).reshape(degrees, 3, 8, 16).sum(axis=2, keepdims=True)
    gain_place = lax.dynamic_update_slice(jnp.zeros(groups.shape, F32), gain_part, (0, 0, lon, 0)).reshape(degrees, chans)
    early = lax.psum(jnp.concatenate([grad_kernel_w, grad_out_w[None]]), ("lat", "lon"))
    grad_field, grad_mix_w = by_rows(
        functools.partial(finish, cells),
        [adj, grad_mixed, field_pad, cot_pad],
        [spectral_weight.T],
        [shape(field.shape, BF)],
        [shape((chans, chans), F32)],
    )
    late = jnp.concatenate([grad_mix_w, gain_place])
    late, early = lax.optimization_barrier((late, early))
    late = lax.psum(late, ("lat", "lon"))
    weight_grads = jnp.concatenate([early[:3], late[None, :chans], early[3:]]) / math.sqrt(lat_count * lon_count)
    return output_field, grad_field, weight_grads, late[chans:]


def solution(mesh):
    placed = (P("lat", "lon", None), P("lat", "lon", None), P(), P(), P(), P(), P(), P())
    return jax.shard_map(
        local,
        mesh=mesh,
        in_specs=placed,
        out_specs=(P("lat", "lon", None), P("lat", "lon", None), P(), P()),
        check_vma=False,
    )
```

```python
import functools
import math

import jax
import jax.numpy as jnp
import numpy as np
from jax import lax
from jax.experimental import pallas as pl
from jax.experimental.pallas import tpu as pltpu
from jax.sharding import PartitionSpec as P

ORDERS = 192
BF = jnp.bfloat16
F32 = jnp.float32
VMEM = pl.BlockSpec(memory_space=pltpu.VMEM)
ROWS = 96
EXT = 128


def dot(a, b, dims=((1,), (0,))):
    return lax.dot_general(a, b, (dims, ((), ())), preferred_element_type=F32)


def tap_rows(taps):
    k, r, t, n = taps.shape
    flat = jnp.transpose(taps, (3, 0, 1, 2)).reshape(n, k * r, t)
    wide = jnp.concatenate([flat[:, :, 3:], jnp.zeros((n, k * r, EXT - t), F32), flat[:, :, :3]], axis=2)
    return jnp.pad(wide, ((0, 0), (0, 16 - k * r), (0, 0)))


def band_matrix(taps_ref, i, band_ref, cells):
    keep = lax.broadcasted_iota(jnp.int32, (ROWS, EXT), 0) < cells
    rows = taps_ref[i]
    for k in range(3):
        for r in range(3):
            row = jnp.broadcast_to(rows[3 * k + r : 3 * k + r + 1], (ROWS, EXT))
            block = pltpu.roll(row, 0, 1, stride=1, stride_axis=0)
            band_ref[k * ROWS : (k + 1) * ROWS, r * EXT : (r + 1) * EXT] = jnp.where(keep, block, 0.0).astype(BF)


def padded(pad_ref, ref, cells):
    pad_ref[:, 80:] = jnp.zeros_like(pad_ref[:, 80:])
    pad_ref[:, :cells] = ref[...]
    return pad_ref[...].reshape(-1, pad_ref.shape[2])


def pointwise(cells, km_ref, so_ref, f_ref, ct_ref, w_ref, wt_ref, out_ref, gp_ref, gow_ref, pad_ref):
    @pl.when(pl.program_id(0) == 0)
    def _():
        gow_ref[...] = jnp.zeros_like(gow_ref)

    group, rows, chans = km_ref.shape
    v = (km_ref[...] + so_ref[...].astype(F32)).reshape(group * rows, chans)
    ct = padded(pad_ref, ct_ref, cells)
    square = v * v
    s = jnp.tanh(0.7978845608 * v * (1.0 + 0.044715 * square))
    half = 0.5 * (1.0 + s)
    hidden = (v * half).astype(BF)
    slope = half + 0.5 * v * (1.0 - s * s) * (0.7978845608 * (1.0 + 3.0 * 0.044715 * square))
    mixed = dot(hidden, w_ref[...]).reshape(km_ref.shape)[:, :cells]
    out_ref[...] = (f_ref[...].astype(F32) + mixed).astype(BF)
    gp_ref[...] = (dot(ct, wt_ref[...]) * slope).astype(BF).reshape(km_ref.shape)
    gow_ref[...] += dot(hidden, ct, ((0,), (0,)))


def block_swap(parts):
    group = lax.broadcasted_iota(jnp.int32, parts[0].shape, 1) // 16
    for k in range(3):
        high = (group >> k) & 1 == 1
        width = 16 << k
        fresh = list(parts)
        for a in range(8):
            if (a >> k) & 1 == 0:
                b = a + (1 << k)
                fresh[a] = jnp.where(high, pltpu.roll(parts[b], width, 1), parts[a])
                fresh[b] = jnp.where(high, parts[b], pltpu.roll(parts[a], 128 - width, 1))
        parts = fresh
    return parts


def tile_swap(x):
    row = lax.broadcasted_iota(jnp.int32, x.shape, 1)
    group = lax.broadcasted_iota(jnp.int32, x.shape, 2) // 16
    for k in range(3):
        row_bit = (row >> k) & 1
        group_bit = (group >> k) & 1
        width = 16 << k
        down = pltpu.roll(pltpu.roll(x, 8 - (1 << k), 1), width, 2)
        up = down if k == 2 else pltpu.roll(pltpu.roll(x, 1 << k, 1), 128 - width, 2)
        x = jnp.where(row_bit == group_bit, x, jnp.where(group_bit == 1, down, up))
    return x


PAD = 80
MESH = pl.DeviceIdType.MESH


def transfer(axis, me, parts, source, target, send_sem, recv_sem):
    def copy(peer, slot):
        return pltpu.make_async_remote_copy(
            src_ref=source(peer),
            dst_ref=target(slot),
            send_sem=send_sem(peer),
            recv_sem=recv_sem(slot),
            device_id={axis: peer},
            device_id_type=MESH,
        )

    def over(body):
        lax.fori_loop(1, parts, lambda d, carry: (body(lax.rem(me + d, parts)), carry)[1], 0)

    def start():
        over(lambda peer: copy(peer, me).start())

    def arrive():
        over(lambda peer: copy(peer, peer).wait_recv())

    def drain():
        over(lambda peer: copy(peer, peer).wait_send())

    return start, arrive, drain


def greet():
    barrier = pltpu.get_barrier_semaphore()
    total = 0
    for axis in ("lon", "lat"):
        me, parts = lax.axis_index(axis), lax.axis_size(axis)

        def body(d, carry, axis=axis, me=me, parts=parts):
            pl.semaphore_signal(barrier, inc=1, device_id={axis: lax.rem(me + d, parts)}, device_id_type=MESH)
            return carry

        lax.fori_loop(1, parts, body, 0)
        total += parts - 1
    return lambda: pl.semaphore_wait(barrier, total)


def reducer(flat, got1, part, got2, whole, sems):
    s1, r1, s2, r2, s3, r3 = sems
    lat, lon = lax.axis_index("lat"), lax.axis_index("lon")
    lats, lons = lax.axis_size("lat"), lax.axis_size("lon")
    n = part.shape[0]

    def block(ref, b):
        return ref.at[pl.ds(pl.multiple_of(b * n, 16), n)]

    first = transfer("lat", lat, lats, lambda p: block(flat, p), lambda s: got1.at[s], lambda p: s1.at[p], lambda s: r1.at[s])
    second = transfer("lon", lon, lons, lambda p: part, lambda s: got2.at[s], lambda p: s2.at[p], lambda s: r2.at[s])
    third = transfer(
        "lat", lat, lats, lambda p: block(whole, lat), lambda s: block(whole, s), lambda p: s3.at[p], lambda s: r3.at[s]
    )

    def total(ref):
        add = lambda s, carry: carry + ref[s].astype(F32)
        return lax.fori_loop(1, ref.shape[0], add, ref[0].astype(F32)).astype(BF)

    def begin():
        first[0]()
        got1[lat] = flat[pl.ds(pl.multiple_of(lat * n, 16), n)]

    def across():
        first[1]()
        part[...] = total(got1)
        second[0]()
        got2[lon] = part[...]

    def spread():
        second[1]()
        whole[pl.ds(pl.multiple_of(lat * n, 16), n)] = total(got2)
        third[0]()

    def end():
        third[1]()
        for t in (first, second, third):
            t[2]()

    return begin, across, spread, end


def reducer_scratch(lats, lons, n):
    lat_sem, lon_sem = pltpu.SemaphoreType.DMA((lats,)), pltpu.SemaphoreType.DMA((lons,))
    return [
        pltpu.VMEM((lats * n, 128), BF),
        pltpu.VMEM((lats, n, 128), BF),
        pltpu.VMEM((n, 128), BF),
        pltpu.VMEM((lons, n, 128), BF),
        pltpu.VMEM((lats * n, 128), BF),
        lat_sem, lat_sem, lon_sem, lon_sem, lat_sem, lat_sem,
    ]


EARLY = 288
LATE = 112


def pass_kernel(forward, cells, *refs):
    refs = list(refs)

    def take(n):
        head = refs[:n]
        del refs[:n]
        return head

    x_ref, table_ref, turned_ref, into_ref, back_ref, gain_ref, in_scale, out_scale, taps_ref, kernel_ref = take(10)
    if forward:
        (mix_ref,) = take(1)
        grid_ref, stencil_ref, bands_ref = take(3)
    else:
        field_ref, gow_ref, bands_ref = take(3)
        grid_ref, stencil_ref, early_ref, gain_out = take(4)
    send1, recv1, send2, recv2, send3, recv3, send4, recv4 = take(8)
    modes, rows_ref, ext, from_left, from_right, band_ref, spare = take(7)
    s1, r1, s2, r2, s3, r3, s4, r4, hs, hr = take(10)
    if not forward:
        part_ref, pad_ref, grad_ref = take(3)
        red = take(11)
        begin, across, spread, end = reducer(*red[:5], red[5:])
    lat, lon = lax.axis_index("lat"), lax.axis_index("lon")
    lons, lats = lax.axis_size("lon"), lax.axis_size("lat")
    rows = x_ref.shape[0]
    chans = x_ref.shape[2]
    enter = greet()

    def way(axis, me, parts, send, recv, ss, rs):
        def at(v):
            start, arrive, drain = transfer(
                axis, me, parts,
                lambda p: send.at[v, p], lambda s: recv.at[v, s], lambda p: ss.at[v, p], lambda s: rs.at[v, s],
            )

            def go():
                start()
                recv[v, me] = send[v, me]

            return go, arrive, drain

        return [at(v) for v in range(3)]

    lon_in = way("lon", lon, lons, send1, recv1, s1, r1)
    lat_in = way("lat", lat, lats, send2, recv2, s2, r2)
    lat_out = way("lat", lat, lats, send3, recv3, s3, r3)
    lon_out = way("lon", lon, lons, send4, recv4, s4, r4)
    order = lax.broadcasted_iota(jnp.int32, (192, 128), 1) // 32
    lane_group = lax.broadcasted_iota(jnp.int32, (192, 128), 1) // 16
    blank = jnp.zeros((8, 128), F32)

    def sideways(source, target, n, step):
        return pltpu.make_async_remote_copy(
            src_ref=source, dst_ref=target, send_sem=hs.at[n], recv_sem=hr.at[n],
            device_id={"lon": lax.rem(lon + step + lons, lons)}, device_id_type=MESH,
        )

    def vertical(source, target, n, step):
        return pltpu.make_async_remote_copy(
            src_ref=source, dst_ref=target, send_sem=hs.at[n], recv_sem=hr.at[n],
            device_id={"lat": lax.rem(lat + step + lats, lats)}, device_id_type=MESH,
        )

    to_right = sideways(ext.at[pl.ds(1, rows), pl.ds(80, 16)], from_left, 0, 1)
    to_left = sideways(ext.at[pl.ds(1, rows), pl.ds(0, 16)], from_right, 1, -1)
    to_below = vertical(ext.at[rows], ext.at[0], 2, 1)
    to_above = vertical(ext.at[1], ext.at[rows + 1], 3, -1)

    def fill(i, carry):
        if forward:
            ext[1 + i, 80:96] = jnp.zeros((16, chans), BF)
        ext[1 + i, : x_ref.shape[1]] = x_ref[i]
        return carry

    def halo_columns():
        for c in (to_right, to_left):
            c.wait()
        place = lax.broadcasted_iota(jnp.int32, (16, chans), 0)

        def step(i, carry):
            own = ext[1 + i, 80:96].astype(F32)
            right = pltpu.roll(from_right[i].astype(F32), 10, 0)
            left = pltpu.roll(from_left[i].astype(F32), 6, 0)
            ext[1 + i, 80:96] = jnp.where(place < 10, own, jnp.where(place < 13, right, 0.0)).astype(BF)
            ext[1 + i, 96:112] = jnp.zeros((16, chans), BF)
            ext[1 + i, 112:128] = jnp.where(place >= 13, left, 0.0).astype(BF)
            return carry

        lax.fori_loop(0, rows, step, 0)

        @pl.when(lat < lats - 1)
        def _():
            to_below.start()

        @pl.when(lat > 0)
        def _():
            to_above.start()

        @pl.when(lat == 0)
        def _():
            ext[0] = jnp.zeros((EXT, chans), BF)

        @pl.when(lat == lats - 1)
        def _():
            ext[rows + 1] = jnp.zeros((EXT, chans), BF)

    def halo_rows():
        @pl.when(lat > 0)
        def _():
            to_below.wait_recv()

        @pl.when(lat < lats - 1)
        def _():
            to_above.wait_recv()

    def halo_drain():
        @pl.when(lat < lats - 1)
        def _():
            to_below.wait_send()

        @pl.when(lat > 0)
        def _():
            to_above.wait_send()

    def stencil(first):
        def step(a, carry):
            i = first + a
            band_matrix(taps_ref, i, band_ref, cells)
            source = ext[pl.ds(i, 3)].reshape(3 * EXT, chans)
            total = None
            for k in range(3):
                part = dot(band_ref[k * ROWS : (k + 1) * ROWS], source).astype(BF)
                if not forward:
                    part_ref[k, a] = part
                part = dot(part, kernel_ref[k])
                total = part if total is None else total + part
            stencil_ref[i] = total
            if not forward:
                pad_ref[a, 80:96] = jnp.zeros((16, chans), BF)
                pad_ref[a, :cells] = field_ref[i]
            return carry

        lax.fori_loop(0, 4, step, 0)
        if not forward:
            own = pad_ref[...].reshape(4 * ROWS, chans)
            for k in range(3):
                add = dot(own, part_ref[k].reshape(4 * ROWS, chans), ((0,), (0,)))
                grad_ref[k] = add if first == START else grad_ref[k] + add

    def tiles(body):
        def step(n, carry):
            body(n // 6, pl.multiple_of(n % 6 * 16, 16))
            return carry

        lax.fori_loop(0, 18, step, 0)

    def split(v):
        lanes_v = slice(v * 128, (v + 1) * 128)
        if forward:
            def mix(g, carry):
                block = ext[pl.ds(1 + g * 8, 8), 0:ROWS].reshape(8 * ROWS, chans)
                spare[pl.ds(g * 8, 8)] = dot(block, mix_ref[:, lanes_v]).reshape(8, ROWS, 128)
                return carry

            lax.fori_loop(0, 3, mix, 0)

        def body(g, j):
            if forward:
                parts = [spare[g * 8 + n, pl.ds(j, 16)] for n in range(8)]
            else:
                parts = [ext[1 + g * 8 + n, pl.ds(j, 16), lanes_v].astype(F32) for n in range(8)]
            lanes = pl.ds(pl.multiple_of(g * 128, 128), 128)
            for p, part in enumerate(block_swap(parts)):
                send1[v, p, pl.ds(j, 16), lanes] = part.astype(BF)

        tiles(body)
        lon_in[v][0]()

    def analyse(v):
        lon_in[v][1]()
        modes[...] = dot(into_ref[...], recv1[v].reshape(lons * ROWS, 384))

        def step(b, carry):
            block = modes[pl.ds(pl.multiple_of(b * 24, 8), 24), :]
            turned = [tile_swap(block[:, g * 128 : (g + 1) * 128].reshape(3, 8, 128)) for g in range(3)]
            pieces = [turned[g][o] for o in range(3) for g in range(3)] + [blank]
            send2[v, b] = jnp.concatenate(pieces, axis=0).astype(BF)
            return carry

        lax.fori_loop(0, lats, step, 0)
        lat_in[v][0]()

    def filter_bands(v):
        lat_in[v][1]()
        lanes = slice(v * 128, (v + 1) * 128)

        def gather(b, carry):
            at = pl.ds(pl.multiple_of(b * 24, 8), 24)
            block = recv2[v, b].astype(F32)
            for o in range(3):
                rows_ref[o, at] = block[o * 24 : (o + 1) * 24] * in_scale[o, at]
            return carry

        lax.fori_loop(0, lats, gather, 0)
        gain_sum = None
        for o in range(3):
            every = dot(table_ref[o], rows_ref[o].astype(BF))
            band = every[:192]
            for m in range(1, 4):
                band = jnp.where(order == m, every[m * 192 : (m + 1) * 192], band)
            if forward:
                bands_ref[o, :, lanes] = band
            else:
                term = band * bands_ref[o, :, lanes]
                gain_sum = term if gain_sum is None else gain_sum + term
            band = band * gain_ref[:, lanes]
            spread_out = jnp.concatenate([jnp.where(order == m, band, 0.0).astype(BF) for m in range(4)], axis=0)
            rows_ref[o] = dot(turned_ref[o], spread_out) * out_scale[o]

        def scatter(b, carry):
            at = pl.ds(pl.multiple_of(b * 24, 8), 24)
            send3[v, b] = jnp.concatenate([rows_ref[o, at] for o in range(3)] + [blank], axis=0).astype(BF)
            return carry

        lax.fori_loop(0, lats, scatter, 0)
        lat_out[v][0]()
        if not forward:
            for width in (16, 32, 64):
                gain_sum = gain_sum + pltpu.roll(gain_sum, width, 1)
            gain_out[:, lanes] = jnp.where(lane_group == lon, gain_sum, 0.0)

    def synthesise(v):
        lat_out[v][1]()

        def step(b, carry):
            turned = tile_swap(recv3[v, b].astype(F32)[:72].reshape(9, 8, 128))
            wide = [jnp.concatenate([turned[o * 3 + g] for o in range(3)], axis=0) for g in range(3)]
            modes[pl.ds(pl.multiple_of(b * 24, 8), 24), :] = jnp.concatenate(wide, axis=1)
            return carry

        lax.fori_loop(0, lats, step, 0)
        send4[v] = dot(back_ref[...], modes[...].astype(BF)).astype(BF).reshape(lons, ROWS, 384)
        lon_out[v][0]()

    def join(v):
        lon_out[v][1]()

        def body(g, j):
            lanes = pl.ds(pl.multiple_of(g * 128, 128), 128)
            parts = [recv4[v, p, pl.ds(j, 16), lanes].astype(F32) for p in range(8)]
            for n, part in enumerate(block_swap(parts)):
                grid_ref[g * 8 + n, pl.ds(j, 16), v * 128 : (v + 1) * 128] = part.astype(BF)

        tiles(body)

    def early_begin():
        flat = red[0]
        for k in range(4):
            for v in range(3):
                block = (grad_ref[k] if k < 3 else gow_ref[...])[:, v * 128 : (v + 1) * 128]
                flat[(k * 3 + v) * 384 : (k * 3 + v + 1) * 384] = block.astype(BF)
        begin()

    def early_end():
        end()
        whole = red[4]
        for k in range(4):
            for v in range(3):
                early_ref[k, :, v * 128 : (v + 1) * 128] = whole[(k * 3 + v) * 384 : (k * 3 + v + 1) * 384].astype(F32)

    lax.fori_loop(0, rows, fill, 0)
    enter()
    to_right.start()
    to_left.start()
    for v in range(3):
        split(v)
    halo_columns()
    START = 4
    stencil(4)
    stencil(8)
    analyse(0)
    stencil(12)
    filter_bands(0)
    analyse(1)
    stencil(16)
    synthesise(0)
    filter_bands(1)
    halo_rows()
    if not forward:
        stencil(20)
        stencil(0)
        early_begin()
    analyse(2)
    if forward:
        stencil(20)
    synthesise(1)
    filter_bands(2)
    if not forward:
        across()
    if forward:
        stencil(0)
    join(0)
    synthesise(2)
    if not forward:
        spread()
    join(1)
    join(2)
    if not forward:
        early_end()
    halo_drain()
    for road in (lon_in, lat_in, lat_out, lon_out):
        for v in range(3):
            road[v][2]()


def pass_call(forward, cells, args, outs):
    lons, lats = lax.axis_size("lon"), lax.axis_size("lat")
    rows, _, chans = args[0].shape
    lon_buf = pltpu.VMEM((3, lons, ROWS, 384), BF)
    lat_buf = pltpu.VMEM((3, lats, PAD, 128), BF)
    lon_sem = pltpu.SemaphoreType.DMA((3, lons))
    lat_sem = pltpu.SemaphoreType.DMA((3, lats))
    scratch = [lon_buf, lon_buf] + [lat_buf] * 4 + [lon_buf, lon_buf]
    scratch += [
        pltpu.VMEM((384, 384), F32),
        pltpu.VMEM((3, 384, 128), F32),
        pltpu.VMEM((rows + 2, EXT, chans), BF),
        pltpu.VMEM((rows, 16, chans), BF),
        pltpu.VMEM((rows, 16, chans), BF),
        pltpu.VMEM((3 * ROWS, 3 * EXT), BF),
        pltpu.VMEM((rows, ROWS, 128) if forward else (8, 128), F32),
    ]
    scratch += [lon_sem, lon_sem, lat_sem, lat_sem, lat_sem, lat_sem, lon_sem, lon_sem]
    scratch += [pltpu.SemaphoreType.DMA((4,)), pltpu.SemaphoreType.DMA((4,))]
    if not forward:
        scratch += [pltpu.VMEM((3, 4, ROWS, chans), BF), pltpu.VMEM((4, ROWS, chans), BF), pltpu.VMEM((3, chans, chans), F32)]
        scratch += reducer_scratch(lats, lons, EARLY)
    return pl.pallas_call(
        functools.partial(pass_kernel, forward, cells),
        out_shape=outs,
        in_specs=[VMEM] * len(args),
        out_specs=[VMEM] * len(outs),
        scratch_shapes=scratch,
        compiler_params=pltpu.CompilerParams(
            collective_id=1 if forward else 2, has_side_effects=True, vmem_limit_bytes=60 << 20
        ),
    )(*args)


def finish(cells, adj_ref, gm_ref, f_ref, ct_ref, wt_ref, gain_ref, out_ref, gmw_ref, gain_out, pad_ref, *red):
    begin, across, spread, end = reducer(*red[:5], red[5:])
    flat, whole = red[0], red[4]
    enter = greet()
    rows, chans = adj_ref.shape[0], adj_ref.shape[2]
    group = pad_ref.shape[0]

    def weigh(n, carry):
        some = pl.ds(n * group, group)
        own = padded(pad_ref, f_ref.at[some], cells)
        add = dot(own, gm_ref[some].reshape(group * ROWS, chans), ((0,), (0,)))
        gmw_ref[...] = gmw_ref[...] + add
        return carry

    gmw_ref[...] = jnp.zeros_like(gmw_ref)
    lax.fori_loop(0, rows // group, weigh, 0)
    for v in range(3):
        lanes = slice(v * 128, (v + 1) * 128)
        flat[v * 576 : v * 576 + 384] = gmw_ref[:, lanes].astype(BF)
        flat[v * 576 + 384 : (v + 1) * 576] = gain_ref[:, lanes].astype(BF)
    flat[1728:] = jnp.zeros((64, 128), BF)
    enter()
    begin()

    def field_rows(first):
        def step(n, carry):
            some = pl.ds(first + n * group, group)
            add = adj_ref[some] + dot(gm_ref[some].reshape(group * ROWS, chans), wt_ref[...]).reshape(group, ROWS, chans)
            out_ref[some] = (ct_ref[some].astype(F32) + add[:, :cells]).astype(BF)
            return carry

        lax.fori_loop(0, 2, step, 0)

    field_rows(0)
    across()
    field_rows(8)
    spread()
    field_rows(16)
    end()
    for v in range(3):
        lanes = slice(v * 128, (v + 1) * 128)
        gmw_ref[:, lanes] = whole[v * 576 : v * 576 + 384].astype(F32)
        gain_out[:, lanes] = whole[v * 576 + 384 : (v + 1) * 576].astype(F32)


def fourier_tables(lon_count, cells, lat_parts):
    j = np.arange(lon_count)
    angles = (j[:, None] * np.arange(ORDERS)[None, :] % lon_count) * (2.0 * np.pi / lon_count)
    waves = np.stack([np.cos(angles), -np.sin(angles)], axis=-1).reshape(lon_count // cells, cells, 2 * ORDERS)
    waves = np.pad(waves, ((0, 0), (0, ROWS - cells), (0, 0))).reshape(-1, 2 * ORDERS)
    return jnp.asarray(waves.T, BF), jnp.asarray(waves, BF)


def legendre_kernel(m_ref, x_ref, diag_ref, out_ref):
    m = m_ref[...]
    x = x_ref[...]
    diag = diag_ref[...]
    reps = x.shape[1] // m.shape[1]

    def wide(a):
        return jnp.concatenate([a] * reps, axis=1)

    mw = wide(m)

    def step(l, carry):
        prev, before, a_prev = carry
        lf = l.astype(F32)
        above = lf > m
        den = jnp.where(above, lf * lf - m * m, 1.0)
        a = jnp.where(above, jnp.sqrt((4.0 * lf * lf - 1.0) / den), 1.0)
        cur = wide(a) * (x * prev - before * wide(1.0 / a_prev))
        cur = jnp.where(lf == mw, diag, jnp.where(lf > mw, cur, 0.0))
        out_ref[l] = cur.astype(BF)
        return cur, prev, a

    blank = x * 0.0
    lax.fori_loop(0, out_ref.shape[0], step, (blank, blank, m * 0.0 + 1.0), unroll=4)


def colatitudes(row_index, lat_count):
    return (row_index.astype(F32) + 0.5) * (math.pi / lat_count)


def legendre_rows(orders, lat_count, degrees):
    slots = 16
    m = jnp.pad(orders, (0, slots - orders.shape[0])).astype(F32)[:, None]
    colat = colatitudes(jnp.arange(lat_count, dtype=jnp.int32), lat_count)[None, :]
    log_start = 0.5 * (lax.lgamma(m + 1.5) - lax.lgamma(m + 1.0) - lax.lgamma(F32(1.5) + 0.0 * m))
    diag = jnp.exp(log_start + m * jnp.log(jnp.sin(colat))) / math.sqrt(4.0 * math.pi)
    x = jnp.broadcast_to(jnp.cos(colat), diag.shape)
    table = pl.pallas_call(
        legendre_kernel,
        out_shape=jax.ShapeDtypeStruct((degrees, slots, lat_count), BF),
        in_specs=[VMEM] * 3,
        out_specs=VMEM,
        compiler_params=pltpu.CompilerParams(vmem_limit_bytes=40 << 20),
    )(jnp.broadcast_to(m, (slots, 128)), x, diag)
    return jnp.transpose(table[:, : orders.shape[0]], (1, 0, 2))


def tap_table(kernel_basis, lon_reach):
    count = kernel_basis.shape[2]
    offsets = jnp.abs(jnp.arange(count, dtype=jnp.int32) - count // 2)
    mask = offsets[None, :, None] <= lon_reach[:, None, :]
    return kernel_basis * mask[None].astype(F32)


def by_rows(body, args, whole, outs, totals, scratch, group=4):
    def cut(a):
        return pl.BlockSpec((group,) + a.shape[1:], lambda g: (g, 0, 0))

    def full(a):
        return pl.BlockSpec(a.shape, lambda g: (0,) * len(a.shape))

    return pl.pallas_call(
        body,
        grid=(args[0].shape[0] // group,),
        in_specs=[cut(a) for a in args] + [full(a) for a in whole],
        out_specs=[cut(a) for a in outs] + [full(a) for a in totals],
        out_shape=list(outs) + list(totals),
        scratch_shapes=scratch,
        compiler_params=pltpu.CompilerParams(vmem_limit_bytes=56 << 20),
    )(*args, *whole)


def local(field, cotangent, kernel_weights, spectral_weight, out_weight, degree_gain, kernel_basis, lon_reach):
    rows, cells, chans = field.shape
    lat_parts, lon_parts = lax.axis_size("lat"), lax.axis_size("lon")
    lat, lon = lax.axis_index("lat"), lax.axis_index("lon")
    lat_count, lon_count = rows * lat_parts, cells * lon_parts
    degrees = degree_gain.shape[0]
    slots = ORDERS // lat_parts
    shape = jax.ShapeDtypeStruct

    taps = tap_table(kernel_basis, lon_reach)
    near = lax.dynamic_slice_in_dim(jnp.pad(taps, ((0, 0), (0, 0), (0, 0), (1, 1))), lat * rows, rows + 2, 3)
    own_taps = tap_rows(near[:, :, :, 1 : rows + 1])
    turned = near[:, ::-1, ::-1]
    adj_taps = tap_rows(jnp.stack([turned[:, r, :, r : r + rows] for r in range(3)], axis=1))

    my_orders = lat * slots + jnp.arange(slots, dtype=jnp.int32)
    table = legendre_rows(my_orders, lat_count, degrees)
    into, back = fourier_tables(lon_count, cells, lat_parts)
    table = table.reshape(3, 4 * degrees, lat_count)
    turned = jnp.transpose(table, (0, 2, 1))
    quad = 2.0 * math.pi / lon_count * (math.pi / lat_count) * jnp.sin(
        colatitudes(jnp.arange(lat_count, dtype=jnp.int32), lat_count)
    )
    quad = jnp.broadcast_to(quad[None, :, None], (3, lat_count, 128))
    mode_weight = jnp.where(my_orders == 0, 1.0, 2.0).astype(F32).reshape(3, 1, 4, 1)
    mode_weight = jnp.broadcast_to(mode_weight, (3, lat_count, 4, 32)).reshape(3, lat_count, 128)
    groups = degree_gain.reshape(degrees, 3, lon_parts, 16)
    gain = lax.dynamic_slice_in_dim(groups, lon, 1, 2)
    gain = jnp.broadcast_to(gain, groups.shape).reshape(degrees, chans)

    shared = [table, turned, into, back, gain]
    wide = (rows, ROWS, chans)
    spec_out, kernel_mix, bands = pass_call(
        True,
        cells,
        [field, *shared, quad, mode_weight, own_taps, kernel_weights, spectral_weight],
        [shape(wide, BF), shape(wide, F32), shape((3, degrees, chans), F32)],
    )
    output_field, grad_pre, grad_out_w = by_rows(
        functools.partial(pointwise, cells),
        [kernel_mix, spec_out, field, cotangent],
        [out_weight, out_weight.T],
        [shape(field.shape, BF), shape(wide, BF)],
        [shape((chans, chans), F32)],
        [pltpu.VMEM((4, ROWS, chans), BF)],
    )
    turned_weights = jnp.transpose(kernel_weights, (0, 2, 1))
    grad_mixed, adj, early, gain_place = pass_call(
        False,
        cells,
        [grad_pre, *shared, mode_weight, quad, adj_taps, turned_weights, field, grad_out_w, bands],
        [shape(wide, BF), shape(wide, F32), shape((4, chans, chans), F32), shape((degrees, chans), F32)],
    )
    grad_field, grad_mix_w, gain_total = pl.pallas_call(
        functools.partial(finish, cells),
        out_shape=[shape(field.shape, BF), shape((chans, chans), F32), shape((degrees, chans), F32)],
        in_specs=[VMEM] * 6,
        out_specs=[VMEM] * 3,
        scratch_shapes=[pltpu.VMEM((4, ROWS, chans), BF)] + reducer_scratch(lat_parts, lon_parts, LATE),
        compiler_params=pltpu.CompilerParams(collective_id=3, has_side_effects=True, vmem_limit_bytes=56 << 20),
    )(adj, grad_mixed, field, cotangent, spectral_weight.T, gain_place)
    weight_grads = jnp.concatenate([early[:3], grad_mix_w[None], early[3:]]) / math.sqrt(lat_count * lon_count)
    return output_field, grad_field, weight_grads, gain_total


def solution(mesh):
    placed = (P("lat", "lon", None), P("lat", "lon", None), P(), P(), P(), P(), P(), P())
    return jax.shard_map(
        local,
        mesh=mesh,
        in_specs=placed,
        out_specs=(P("lat", "lon", None), P("lat", "lon", None), P(), P()),
        check_vma=False,
    )
```

```python
import functools
import math

import jax
import jax.numpy as jnp
import numpy as np
from jax import lax
from jax.experimental import pallas as pl
from jax.experimental.pallas import tpu as pltpu
from jax.sharding import PartitionSpec as P

ORDERS = 192
BF = jnp.bfloat16
F32 = jnp.float32
VMEM = pl.BlockSpec(memory_space=pltpu.VMEM)
ROWS = 96
EXT = 128


def dot(a, b, dims=((1,), (0,))):
    return lax.dot_general(a, b, (dims, ((), ())), preferred_element_type=F32)


def tap_rows(taps):
    k, r, t, n = taps.shape
    flat = jnp.transpose(taps, (3, 0, 1, 2)).reshape(n, k * r, t)
    wide = jnp.concatenate([flat[:, :, 3:], jnp.zeros((n, k * r, EXT - t), F32), flat[:, :, :3]], axis=2)
    return jnp.pad(wide, ((0, 0), (0, 16 - k * r), (0, 0)))


def band_matrix(taps_ref, i, band_ref, cells):
    keep = lax.broadcasted_iota(jnp.int32, (ROWS, EXT), 0) < cells
    rows = taps_ref[i]
    for k in range(3):
        for r in range(3):
            row = jnp.broadcast_to(rows[3 * k + r : 3 * k + r + 1], (ROWS, EXT))
            block = pltpu.roll(row, 0, 1, stride=1, stride_axis=0)
            band_ref[k * ROWS : (k + 1) * ROWS, r * EXT : (r + 1) * EXT] = jnp.where(keep, block, 0.0).astype(BF)


def padded(pad_ref, ref, cells):
    pad_ref[:, 80:] = jnp.zeros_like(pad_ref[:, 80:])
    pad_ref[:, :cells] = ref[...]
    return pad_ref[...].reshape(-1, pad_ref.shape[2])


def pointwise(cells, km_ref, so_ref, f_ref, ct_ref, w_ref, wt_ref, out_ref, gp_ref, gow_ref, pad_ref):
    @pl.when(pl.program_id(0) == 0)
    def _():
        gow_ref[...] = jnp.zeros_like(gow_ref)

    group, rows, chans = km_ref.shape
    v = (km_ref[...] + so_ref[...].astype(F32)).reshape(group * rows, chans)
    ct = padded(pad_ref, ct_ref, cells)
    square = v * v
    s = jnp.tanh(0.7978845608 * v * (1.0 + 0.044715 * square))
    half = 0.5 * (1.0 + s)
    hidden = (v * half).astype(BF)
    slope = half + 0.5 * v * (1.0 - s * s) * (0.7978845608 * (1.0 + 3.0 * 0.044715 * square))
    mixed = dot(hidden, w_ref[...]).reshape(km_ref.shape)[:, :cells]
    out_ref[...] = (f_ref[...].astype(F32) + mixed).astype(BF)
    gp_ref[...] = (dot(ct, wt_ref[...]) * slope).astype(BF).reshape(km_ref.shape)
    gow_ref[...] += dot(hidden, ct, ((0,), (0,)))


def block_swap(parts):
    group = lax.broadcasted_iota(jnp.int32, parts[0].shape, 1) // 16
    for k in range(3):
        high = (group >> k) & 1 == 1
        width = 16 << k
        fresh = list(parts)
        for a in range(8):
            if (a >> k) & 1 == 0:
                b = a + (1 << k)
                fresh[a] = jnp.where(high, pltpu.roll(parts[b], width, 1), parts[a])
                fresh[b] = jnp.where(high, parts[b], pltpu.roll(parts[a], 128 - width, 1))
        parts = fresh
    return parts


def tile_swap(x):
    row = lax.broadcasted_iota(jnp.int32, x.shape, 1)
    group = lax.broadcasted_iota(jnp.int32, x.shape, 2) // 16
    for k in range(3):
        row_bit = (row >> k) & 1
        group_bit = (group >> k) & 1
        width = 16 << k
        down = pltpu.roll(pltpu.roll(x, 8 - (1 << k), 1), width, 2)
        up = down if k == 2 else pltpu.roll(pltpu.roll(x, 1 << k, 1), 128 - width, 2)
        x = jnp.where(row_bit == group_bit, x, jnp.where(group_bit == 1, down, up))
    return x


PAD = 80
MESH = pl.DeviceIdType.MESH


def transfer(axis, me, parts, source, target, send_sem, recv_sem):
    def copy(peer, slot):
        return pltpu.make_async_remote_copy(
            src_ref=source(peer),
            dst_ref=target(slot),
            send_sem=send_sem(peer),
            recv_sem=recv_sem(slot),
            device_id={axis: peer},
            device_id_type=MESH,
        )

    def over(body):
        lax.fori_loop(1, parts, lambda d, carry: (body(lax.rem(me + d, parts)), carry)[1], 0)

    def start():
        over(lambda peer: copy(peer, me).start())

    def arrive():
        over(lambda peer: copy(peer, peer).wait_recv())

    def drain():
        over(lambda peer: copy(peer, peer).wait_send())

    return start, arrive, drain


def greet():
    barrier = pltpu.get_barrier_semaphore()
    total = 0
    for axis in ("lon", "lat"):
        me, parts = lax.axis_index(axis), lax.axis_size(axis)

        def body(d, carry, axis=axis, me=me, parts=parts):
            pl.semaphore_signal(barrier, inc=1, device_id={axis: lax.rem(me + d, parts)}, device_id_type=MESH)
            return carry

        lax.fori_loop(1, parts, body, 0)
        total += parts - 1
    return lambda: pl.semaphore_wait(barrier, total)


def reducer(flat, got1, part, got2, whole, sems):
    s1, r1, s2, r2, s3, r3 = sems
    lat, lon = lax.axis_index("lat"), lax.axis_index("lon")
    lats, lons = lax.axis_size("lat"), lax.axis_size("lon")
    n = part.shape[0]

    def block(ref, b):
        return ref.at[pl.ds(pl.multiple_of(b * n, 16), n)]

    first = transfer("lat", lat, lats, lambda p: block(flat, p), lambda s: got1.at[s], lambda p: s1.at[p], lambda s: r1.at[s])
    second = transfer("lon", lon, lons, lambda p: part, lambda s: got2.at[s], lambda p: s2.at[p], lambda s: r2.at[s])
    third = transfer(
        "lat", lat, lats, lambda p: block(whole, lat), lambda s: block(whole, s), lambda p: s3.at[p], lambda s: r3.at[s]
    )

    def total(ref):
        add = lambda s, carry: carry + ref[s].astype(F32)
        return lax.fori_loop(1, ref.shape[0], add, ref[0].astype(F32)).astype(BF)

    def begin():
        first[0]()
        got1[lat] = flat[pl.ds(pl.multiple_of(lat * n, 16), n)]

    def across():
        first[1]()
        part[...] = total(got1)
        second[0]()
        got2[lon] = part[...]

    def spread():
        second[1]()
        whole[pl.ds(pl.multiple_of(lat * n, 16), n)] = total(got2)
        third[0]()

    def end():
        third[1]()
        for t in (first, second, third):
            t[2]()

    return begin, across, spread, end


def reducer_scratch(lats, lons, n):
    lat_sem, lon_sem = pltpu.SemaphoreType.DMA((lats,)), pltpu.SemaphoreType.DMA((lons,))
    return [
        pltpu.VMEM((lats * n, 128), BF),
        pltpu.VMEM((lats, n, 128), BF),
        pltpu.VMEM((n, 128), BF),
        pltpu.VMEM((lons, n, 128), BF),
        pltpu.VMEM((lats * n, 128), BF),
        lat_sem, lat_sem, lon_sem, lon_sem, lat_sem, lat_sem,
    ]


EARLY = 288
LATE = 112


def pass_kernel(forward, cells, *refs):
    refs = list(refs)

    def take(n):
        head = refs[:n]
        del refs[:n]
        return head

    x_ref, into_ref = take(2)
    if forward:
        (mix_ref,) = take(1)
    late_in = take(8 if forward else 13)
    if forward:
        grid_ref, stencil_ref, bands_ref = take(3)
    else:
        out_ref, early_ref, gmw_ref, gain_total = take(4)
    late_ref = take(len(late_in))
    (late_sem,) = take(1)
    table_ref, turned_ref, back_ref, gain_ref, in_scale, out_scale, taps_ref, kernel_ref = late_ref[:8]
    if not forward:
        field_ref, gow_ref, bands_ref, ct_ref, wt_ref = late_ref[8:]
    send1, recv1, send2, recv2, send3, recv3, send4, recv4 = take(8)
    modes, rows_ref, ext, from_left, from_right, band_ref, spare, part_ref = take(8)
    s1, r1, s2, r2, s3, r3, s4, r4, hs, hr = take(10)
    if not forward:
        pad_ref, grad_ref, grid_ref, stencil_ref, gain_out = take(5)
        red = take(11)
        begin, across, spread, end = reducer(*red[:5], red[5:])
        red2 = take(11)
        begin2, across2, spread2, end2 = reducer(*red2[:5], red2[5:])
    late_copies = [pltpu.make_async_copy(a, b, late_sem.at[n]) for n, (a, b) in enumerate(zip(late_in, late_ref))]
    lat, lon = lax.axis_index("lat"), lax.axis_index("lon")
    lons, lats = lax.axis_size("lon"), lax.axis_size("lat")
    rows = x_ref.shape[0]
    chans = x_ref.shape[2]
    enter = greet()

    def way(axis, me, parts, send, recv, ss, rs):
        def at(v):
            start, arrive, drain = transfer(
                axis, me, parts,
                lambda p: send.at[v, p], lambda s: recv.at[v, s], lambda p: ss.at[v, p], lambda s: rs.at[v, s],
            )

            def go():
                start()
                recv[v, me] = send[v, me]

            return go, arrive, drain

        return [at(v) for v in range(3)]

    lon_in = way("lon", lon, lons, send1, recv1, s1, r1)
    lat_in = way("lat", lat, lats, send2, recv2, s2, r2)
    lat_out = way("lat", lat, lats, send3, recv3, s3, r3)
    lon_out = way("lon", lon, lons, send4, recv4, s4, r4)
    order = lax.broadcasted_iota(jnp.int32, (192, 128), 1) // 32
    lane_group = lax.broadcasted_iota(jnp.int32, (192, 128), 1) // 16
    blank = jnp.zeros((8, 128), F32)

    def sideways(source, target, n, step):
        return pltpu.make_async_remote_copy(
            src_ref=source, dst_ref=target, send_sem=hs.at[n], recv_sem=hr.at[n],
            device_id={"lon": lax.rem(lon + step + lons, lons)}, device_id_type=MESH,
        )

    def vertical(source, target, n, step):
        return pltpu.make_async_remote_copy(
            src_ref=source, dst_ref=target, send_sem=hs.at[n], recv_sem=hr.at[n],
            device_id={"lat": lax.rem(lat + step + lats, lats)}, device_id_type=MESH,
        )

    to_right = sideways(ext.at[pl.ds(1, rows), pl.ds(80, 16)], from_left, 0, 1)
    to_left = sideways(ext.at[pl.ds(1, rows), pl.ds(0, 16)], from_right, 1, -1)
    to_below = vertical(ext.at[rows], ext.at[0], 2, 1)
    to_above = vertical(ext.at[1], ext.at[rows + 1], 3, -1)

    def fill(i, carry):
        if forward:
            ext[1 + i, 80:96] = jnp.zeros((16, chans), BF)
        ext[1 + i, : x_ref.shape[1]] = x_ref[i]
        return carry

    def halo_columns():
        for c in (to_right, to_left):
            c.wait()
        place = lax.broadcasted_iota(jnp.int32, (16, chans), 0)

        def step(i, carry):
            own = ext[1 + i, 80:96].astype(F32)
            right = pltpu.roll(from_right[i].astype(F32), 10, 0)
            left = pltpu.roll(from_left[i].astype(F32), 6, 0)
            ext[1 + i, 80:96] = jnp.where(place < 10, own, jnp.where(place < 13, right, 0.0)).astype(BF)
            ext[1 + i, 96:112] = jnp.zeros((16, chans), BF)
            ext[1 + i, 112:128] = jnp.where(place >= 13, left, 0.0).astype(BF)
            return carry

        lax.fori_loop(0, rows, step, 0, unroll=2)

        @pl.when(lat < lats - 1)
        def _():
            to_below.start()

        @pl.when(lat > 0)
        def _():
            to_above.start()

        @pl.when(lat == 0)
        def _():
            ext[0] = jnp.zeros((EXT, chans), BF)

        @pl.when(lat == lats - 1)
        def _():
            ext[rows + 1] = jnp.zeros((EXT, chans), BF)

    def halo_rows():
        @pl.when(lat > 0)
        def _():
            to_below.wait_recv()

        @pl.when(lat < lats - 1)
        def _():
            to_above.wait_recv()

    def halo_drain():
        @pl.when(lat < lats - 1)
        def _():
            to_below.wait_send()

        @pl.when(lat > 0)
        def _():
            to_above.wait_send()

    def stencil(first):
        def step(n, carry):
            for a in range(2):
                i = first + 2 * n + a
                band_matrix(taps_ref, i, band_ref.at[a], cells)
                source = ext[pl.ds(i, 3)].reshape(3 * EXT, chans)
                part = dot(band_ref[a], source).astype(BF)
                for k in range(3):
                    part_ref[k, 2 * n + a] = part[k * ROWS : (k + 1) * ROWS]
            return carry

        lax.fori_loop(0, 2, step, 0)
        total = None
        for k in range(3):
            part = dot(part_ref[k].reshape(4 * ROWS, chans), kernel_ref[k])
            total = part if total is None else total + part
        stencil_ref[first : first + 4] = total.reshape(4, ROWS, chans)
        if not forward:
            own = pad_ref[first : first + 4].reshape(4 * ROWS, chans)
            for k in range(3):
                add = dot(own, part_ref[k].reshape(4 * ROWS, chans), ((0,), (0,)))
                grad_ref[k] = add if first == START else grad_ref[k] + add

    def tiles(body):
        def step(n, carry):
            body(n // 6, pl.multiple_of(n % 6 * 16, 16))
            return carry

        lax.fori_loop(0, 18, step, 0, unroll=3)

    def split(v):
        lanes_v = slice(v * 128, (v + 1) * 128)
        if forward:
            def mix(g, carry):
                block = ext[pl.ds(1 + g * 8, 8), 0:ROWS].reshape(8 * ROWS, chans)
                spare[pl.ds(g * 8, 8)] = dot(block, mix_ref[:, lanes_v]).reshape(8, ROWS, 128)
                return carry

            lax.fori_loop(0, 3, mix, 0)

        def body(g, j):
            if forward:
                parts = [spare[g * 8 + n, pl.ds(j, 16)] for n in range(8)]
            else:
                parts = [ext[1 + g * 8 + n, pl.ds(j, 16), lanes_v].astype(F32) for n in range(8)]
            lanes = pl.ds(pl.multiple_of(g * 128, 128), 128)
            for p, part in enumerate(block_swap(parts)):
                send1[v, p, pl.ds(j, 16), lanes] = part.astype(BF)

        tiles(body)
        lon_in[v][0]()

    def analyse(v):
        lon_in[v][1]()
        modes[...] = dot(into_ref[...], recv1[v].reshape(lons * ROWS, 384))

        def step(b, carry):
            block = modes[pl.ds(pl.multiple_of(b * 24, 8), 24), :]
            turned = [tile_swap(block[:, g * 128 : (g + 1) * 128].reshape(3, 8, 128)) for g in range(3)]
            pieces = [turned[g][o] for o in range(3) for g in range(3)] + [blank]
            send2[v, b] = jnp.concatenate(pieces, axis=0).astype(BF)
            return carry

        lax.fori_loop(0, lats, step, 0, unroll=4)
        lat_in[v][0]()

    def filter_bands(v):
        lat_in[v][1]()
        lanes = slice(v * 128, (v + 1) * 128)

        def gather(b, carry):
            at = pl.ds(pl.multiple_of(b * 24, 8), 24)
            block = recv2[v, b].astype(F32)
            for o in range(3):
                rows_ref[o, at] = block[o * 24 : (o + 1) * 24] * in_scale[o, at]
            return carry

        lax.fori_loop(0, lats, gather, 0, unroll=4)
        gain_sum = None
        for o in range(3):
            every = dot(table_ref[o], rows_ref[o].astype(BF))
            band = every[:192]
            for m in range(1, 4):
                band = jnp.where(order == m, every[m * 192 : (m + 1) * 192], band)
            if forward:
                bands_ref[o, :, lanes] = band
            else:
                term = band * bands_ref[o, :, lanes]
                gain_sum = term if gain_sum is None else gain_sum + term
            band = band * gain_ref[:, lanes]
            spread_out = jnp.concatenate([jnp.where(order == m, band, 0.0).astype(BF) for m in range(4)], axis=0)
            rows_ref[o] = dot(turned_ref[o], spread_out) * out_scale[o]

        def scatter(b, carry):
            at = pl.ds(pl.multiple_of(b * 24, 8), 24)
            send3[v, b] = jnp.concatenate([rows_ref[o, at] for o in range(3)] + [blank], axis=0).astype(BF)
            return carry

        lax.fori_loop(0, lats, scatter, 0, unroll=4)
        lat_out[v][0]()
        if not forward:
            for width in (16, 32, 64):
                gain_sum = gain_sum + pltpu.roll(gain_sum, width, 1)
            gain_out[:, lanes] = jnp.where(lane_group == lon, gain_sum, 0.0)

    def synthesise(v):
        lat_out[v][1]()

        def step(b, carry):
            turned = tile_swap(recv3[v, b].astype(F32)[:72].reshape(9, 8, 128))
            wide = [jnp.concatenate([turned[o * 3 + g] for o in range(3)], axis=0) for g in range(3)]
            modes[pl.ds(pl.multiple_of(b * 24, 8), 24), :] = jnp.concatenate(wide, axis=1)
            return carry

        lax.fori_loop(0, lats, step, 0, unroll=4)
        send4[v] = dot(back_ref[...], modes[...].astype(BF)).astype(BF).reshape(lons, ROWS, 384)
        lon_out[v][0]()

    def join(v):
        lon_out[v][1]()

        def body(g, j):
            lanes = pl.ds(pl.multiple_of(g * 128, 128), 128)
            parts = [recv4[v, p, pl.ds(j, 16), lanes].astype(F32) for p in range(8)]
            for n, part in enumerate(block_swap(parts)):
                grid_ref[g * 8 + n, pl.ds(j, 16), v * 128 : (v + 1) * 128] = part.astype(BF)

        tiles(body)

    def early_begin():
        flat = red[0]
        for k in range(4):
            for v in range(3):
                block = (grad_ref[k] if k < 3 else gow_ref[...])[:, v * 128 : (v + 1) * 128]
                flat[(k * 3 + v) * 384 : (k * 3 + v + 1) * 384] = block.astype(BF)
        begin()

    def early_end():
        end()
        whole = red[4]
        for k in range(4):
            for v in range(3):
                early_ref[k, :, v * 128 : (v + 1) * 128] = whole[(k * 3 + v) * 384 : (k * 3 + v + 1) * 384].astype(F32)

    def own_rows(i, carry):
        pad_ref[i, 80:96] = jnp.zeros((16, chans), BF)
        pad_ref[i, :cells] = field_ref[i]
        return carry

    def weigh(v):
        lanes = slice(v * 128, (v + 1) * 128)

        def step(n, carry):
            some = pl.ds(n * 8, 8)
            own = pad_ref[some].reshape(8 * ROWS, chans)
            return carry + dot(own, grid_ref[some, :, lanes].reshape(8 * ROWS, 128), ((0,), (0,)))

        own = pad_ref[0:8].reshape(8 * ROWS, chans)
        first = dot(own, grid_ref[0:8, :, lanes].reshape(8 * ROWS, 128), ((0,), (0,)))
        gmw_ref[:, lanes] = lax.fori_loop(1, 3, step, first)

    def late_begin():
        flat = red2[0]
        for v in range(3):
            lanes = slice(v * 128, (v + 1) * 128)
            flat[v * 576 : v * 576 + 384] = gmw_ref[:, lanes].astype(BF)
            flat[v * 576 + 384 : (v + 1) * 576] = gain_out[:, lanes].astype(BF)
        flat[1728:] = jnp.zeros((64, 128), BF)
        begin2()

    def late_end():
        end2()
        whole = red2[4]
        for v in range(3):
            lanes = slice(v * 128, (v + 1) * 128)
            gmw_ref[:, lanes] = whole[v * 576 : v * 576 + 384].astype(F32)
            gain_total[:, lanes] = whole[v * 576 + 384 : (v + 1) * 576].astype(F32)

    def field_rows(first):
        def step(n, carry):
            some = pl.ds(first + n * 4, 4)
            mixed = dot(grid_ref[some].reshape(4 * ROWS, chans), wt_ref[...]).reshape(4, ROWS, chans)
            add = stencil_ref[some] + mixed
            out_ref[some] = (ct_ref[some].astype(F32) + add[:, :cells]).astype(BF)
            return carry

        lax.fori_loop(0, 2, step, 0)

    for c in late_copies:
        c.start()
    lax.fori_loop(0, rows, fill, 0, unroll=2)
    enter()
    to_right.start()
    to_left.start()
    for v in range(3):
        split(v)
    for c in late_copies:
        c.wait()
    halo_columns()
    START = 4
    if not forward:
        lax.fori_loop(0, rows, own_rows, 0, unroll=2)
    stencil(4)
    analyse(0)
    stencil(8)
    filter_bands(0)
    analyse(1)
    stencil(12)
    synthesise(0)
    filter_bands(1)
    halo_rows()
    if not forward:
        stencil(16)
        stencil(20)
        stencil(0)
        early_begin()
    analyse(2)
    if forward:
        stencil(16)
    synthesise(1)
    filter_bands(2)
    if not forward:
        across()
    if forward:
        stencil(20)
        stencil(0)
    join(0)
    if not forward:
        weigh(0)
    synthesise(2)
    if not forward:
        spread()
    join(1)
    if not forward:
        weigh(1)
        early_end()
    join(2)
    if not forward:
        weigh(2)
        late_begin()
        field_rows(0)
        across2()
        field_rows(8)
        spread2()
        field_rows(16)
        late_end()
    halo_drain()
    for road in (lon_in, lat_in, lat_out, lon_out):
        for v in range(3):
            road[v][2]()


def pass_call(forward, cells, first, late, outs):
    lons, lats = lax.axis_size("lon"), lax.axis_size("lat")
    rows, _, chans = first[0].shape
    lon_buf = pltpu.VMEM((3, lons, ROWS, 384), BF)
    lat_buf = pltpu.VMEM((3, lats, PAD, 128), BF)
    lon_sem = pltpu.SemaphoreType.DMA((3, lons))
    lat_sem = pltpu.SemaphoreType.DMA((3, lats))
    scratch = [pltpu.VMEM(a.shape, a.dtype) for a in late] + [pltpu.SemaphoreType.DMA((len(late),))]
    scratch += [lon_buf, lon_buf] + [lat_buf] * 4 + [lon_buf, lon_buf]
    scratch += [
        pltpu.VMEM((384, 384), F32),
        pltpu.VMEM((3, 384, 128), F32),
        pltpu.VMEM((rows + 2, EXT, chans), BF),
        pltpu.VMEM((rows, 16, chans), BF),
        pltpu.VMEM((rows, 16, chans), BF),
        pltpu.VMEM((2, 3 * ROWS, 3 * EXT), BF),
        pltpu.VMEM((rows, ROWS, 128) if forward else (8, 128), F32),
        pltpu.VMEM((3, 4, ROWS, chans), BF),
    ]
    scratch += [lon_sem, lon_sem, lat_sem, lat_sem, lat_sem, lat_sem, lon_sem, lon_sem]
    scratch += [pltpu.SemaphoreType.DMA((4,)), pltpu.SemaphoreType.DMA((4,))]
    if not forward:
        wide = (rows, ROWS, chans)
        scratch += [pltpu.VMEM(wide, BF), pltpu.VMEM((3, chans, chans), F32), pltpu.VMEM(wide, BF), pltpu.VMEM(wide, F32)]
        scratch += [pltpu.VMEM((192, chans), F32)]
        scratch += reducer_scratch(lats, lons, EARLY) + reducer_scratch(lats, lons, LATE)
    return pl.pallas_call(
        functools.partial(pass_kernel, forward, cells),
        out_shape=outs,
        in_specs=[VMEM] * len(first) + [pl.BlockSpec(memory_space=pl.ANY)] * len(late),
        out_specs=[VMEM] * len(outs),
        scratch_shapes=scratch,
        compiler_params=pltpu.CompilerParams(
            collective_id=1 if forward else 2, has_side_effects=True, vmem_limit_bytes=60 << 20
        ),
    )(*first, *late)


def fourier_tables(lon_count, cells, lat_parts):
    j = np.arange(lon_count)
    angles = (j[:, None] * np.arange(ORDERS)[None, :] % lon_count) * (2.0 * np.pi / lon_count)
    waves = np.stack([np.cos(angles), -np.sin(angles)], axis=-1).reshape(lon_count // cells, cells, 2 * ORDERS)
    waves = np.pad(waves, ((0, 0), (0, ROWS - cells), (0, 0))).reshape(-1, 2 * ORDERS)
    return jnp.asarray(waves.T, BF), jnp.asarray(waves, BF)


def legendre_kernel(m_ref, x_ref, diag_ref, out_ref):
    m = m_ref[...]
    x = x_ref[...]
    diag = diag_ref[...]
    reps = x.shape[1] // m.shape[1]

    def wide(a):
        return jnp.concatenate([a] * reps, axis=1)

    mw = wide(m)

    def step(l, carry):
        prev, before, a_prev = carry
        lf = l.astype(F32)
        above = lf > m
        den = jnp.where(above, lf * lf - m * m, 1.0)
        a = jnp.where(above, jnp.sqrt((4.0 * lf * lf - 1.0) / den), 1.0)
        cur = wide(a) * (x * prev - before * wide(1.0 / a_prev))
        cur = jnp.where(lf == mw, diag, jnp.where(lf > mw, cur, 0.0))
        out_ref[l] = cur.astype(BF)
        return cur, prev, a

    blank = x * 0.0
    lax.fori_loop(0, out_ref.shape[0], step, (blank, blank, m * 0.0 + 1.0), unroll=4)


def colatitudes(row_index, lat_count):
    return (row_index.astype(F32) + 0.5) * (math.pi / lat_count)


def legendre_rows(orders, lat_count, degrees):
    slots = 16
    m = jnp.pad(orders, (0, slots - orders.shape[0])).astype(F32)[:, None]
    colat = colatitudes(jnp.arange(lat_count, dtype=jnp.int32), lat_count)[None, :]
    log_start = 0.5 * (lax.lgamma(m + 1.5) - lax.lgamma(m + 1.0) - lax.lgamma(F32(1.5) + 0.0 * m))
    diag = jnp.exp(log_start + m * jnp.log(jnp.sin(colat))) / math.sqrt(4.0 * math.pi)
    x = jnp.broadcast_to(jnp.cos(colat), diag.shape)
    table = pl.pallas_call(
        legendre_kernel,
        out_shape=jax.ShapeDtypeStruct((degrees, slots, lat_count), BF),
        in_specs=[VMEM] * 3,
        out_specs=VMEM,
        compiler_params=pltpu.CompilerParams(vmem_limit_bytes=40 << 20),
    )(jnp.broadcast_to(m, (slots, 128)), x, diag)
    return jnp.transpose(table[:, : orders.shape[0]], (1, 0, 2))


def tap_table(kernel_basis, lon_reach):
    count = kernel_basis.shape[2]
    offsets = jnp.abs(jnp.arange(count, dtype=jnp.int32) - count // 2)
    mask = offsets[None, :, None] <= lon_reach[:, None, :]
    return kernel_basis * mask[None].astype(F32)


def by_rows(body, args, whole, outs, totals, scratch, group=4):
    def cut(a):
        return pl.BlockSpec((group,) + a.shape[1:], lambda g: (g, 0, 0))

    def full(a):
        return pl.BlockSpec(a.shape, lambda g: (0,) * len(a.shape))

    return pl.pallas_call(
        body,
        grid=(args[0].shape[0] // group,),
        in_specs=[cut(a) for a in args] + [full(a) for a in whole],
        out_specs=[cut(a) for a in outs] + [full(a) for a in totals],
        out_shape=list(outs) + list(totals),
        scratch_shapes=scratch,
        compiler_params=pltpu.CompilerParams(vmem_limit_bytes=56 << 20),
    )(*args, *whole)


def local(field, cotangent, kernel_weights, spectral_weight, out_weight, degree_gain, kernel_basis, lon_reach):
    rows, cells, chans = field.shape
    lat_parts, lon_parts = lax.axis_size("lat"), lax.axis_size("lon")
    lat, lon = lax.axis_index("lat"), lax.axis_index("lon")
    lat_count, lon_count = rows * lat_parts, cells * lon_parts
    degrees = degree_gain.shape[0]
    slots = ORDERS // lat_parts
    shape = jax.ShapeDtypeStruct

    taps = tap_table(kernel_basis, lon_reach)
    near = lax.dynamic_slice_in_dim(jnp.pad(taps, ((0, 0), (0, 0), (0, 0), (1, 1))), lat * rows, rows + 2, 3)
    own_taps = tap_rows(near[:, :, :, 1 : rows + 1])
    turned = near[:, ::-1, ::-1]
    adj_taps = tap_rows(jnp.stack([turned[:, r, :, r : r + rows] for r in range(3)], axis=1))

    my_orders = lat * slots + jnp.arange(slots, dtype=jnp.int32)
    table = legendre_rows(my_orders, lat_count, degrees)
    into, back = fourier_tables(lon_count, cells, lat_parts)
    table = table.reshape(3, 4 * degrees, lat_count)
    turned = jnp.transpose(table, (0, 2, 1))
    quad = 2.0 * math.pi / lon_count * (math.pi / lat_count) * jnp.sin(
        colatitudes(jnp.arange(lat_count, dtype=jnp.int32), lat_count)
    )
    quad = jnp.broadcast_to(quad[None, :, None], (3, lat_count, 128))
    mode_weight = jnp.where(my_orders == 0, 1.0, 2.0).astype(F32).reshape(3, 1, 4, 1)
    mode_weight = jnp.broadcast_to(mode_weight, (3, lat_count, 4, 32)).reshape(3, lat_count, 128)
    groups = degree_gain.reshape(degrees, 3, lon_parts, 16)
    gain = lax.dynamic_slice_in_dim(groups, lon, 1, 2)
    gain = jnp.broadcast_to(gain, groups.shape).reshape(degrees, chans)

    wide = (rows, ROWS, chans)
    spec_out, kernel_mix, bands = pass_call(
        True,
        cells,
        [field, into, spectral_weight],
        [table, turned, back, gain, quad, mode_weight, own_taps, kernel_weights],
        [shape(wide, BF), shape(wide, F32), shape((3, degrees, chans), F32)],
    )
    output_field, grad_pre, grad_out_w = by_rows(
        functools.partial(pointwise, cells),
        [kernel_mix, spec_out, field, cotangent],
        [out_weight, out_weight.T],
        [shape(field.shape, BF), shape(wide, BF)],
        [shape((chans, chans), F32)],
        [pltpu.VMEM((4, ROWS, chans), BF)],
    )
    turned_weights = jnp.transpose(kernel_weights, (0, 2, 1))
    grad_field, early, grad_mix_w, gain_total = pass_call(
        False,
        cells,
        [grad_pre, into],
        [table, turned, back, gain, mode_weight, quad, adj_taps, turned_weights]
        + [field, grad_out_w, bands, cotangent, spectral_weight.T],
        [shape(field.shape, BF), shape((4, chans, chans), F32), shape((chans, chans), F32), shape((degrees, chans), F32)],
    )
    weight_grads = jnp.concatenate([early[:3], grad_mix_w[None], early[3:]]) / math.sqrt(lat_count * lon_count)
    return output_field, grad_field, weight_grads, gain_total


def solution(mesh):
    placed = (P("lat", "lon", None), P("lat", "lon", None), P(), P(), P(), P(), P(), P())
    return jax.shard_map(
        local,
        mesh=mesh,
        in_specs=placed,
        out_specs=(P("lat", "lon", None), P("lat", "lon", None), P(), P()),
        check_vma=False,
    )
```

```python
import functools
import math

import jax
import jax.numpy as jnp
import numpy as np
from jax import lax
from jax.experimental import pallas as pl
from jax.experimental.pallas import tpu as pltpu
from jax.sharding import PartitionSpec as P

ORDERS = 192
BF = jnp.bfloat16
F32 = jnp.float32
VMEM = pl.BlockSpec(memory_space=pltpu.VMEM)
ROWS = 96
EXT = 128


def dot(a, b, dims=((1,), (0,))):
    return lax.dot_general(a, b, (dims, ((), ())), preferred_element_type=F32)


def tap_rows(taps):
    k, r, t, n = taps.shape
    flat = jnp.transpose(taps, (3, 0, 1, 2)).reshape(n, k * r, t)
    wide = jnp.concatenate([flat[:, :, 3:], jnp.zeros((n, k * r, EXT - t), F32), flat[:, :, :3]], axis=2)
    return jnp.pad(wide, ((0, 0), (0, 16 - k * r), (0, 0)))


def band_matrix(taps_ref, i, band_ref, cells):
    keep = lax.broadcasted_iota(jnp.int32, (ROWS, EXT), 0) < cells
    rows = taps_ref[i]
    for k in range(3):
        for r in range(3):
            row = jnp.broadcast_to(rows[3 * k + r : 3 * k + r + 1], (ROWS, EXT))
            block = pltpu.roll(row, 0, 1, stride=1, stride_axis=0)
            band_ref[k * ROWS : (k + 1) * ROWS, r * EXT : (r + 1) * EXT] = jnp.where(keep, block, 0.0).astype(BF)


def padded(pad_ref, ref, cells):
    pad_ref[:, 80:] = jnp.zeros_like(pad_ref[:, 80:])
    pad_ref[:, :cells] = ref[...]
    return pad_ref[...].reshape(-1, pad_ref.shape[2])


def pointwise(cells, km_ref, so_ref, f_ref, ct_ref, w_ref, wt_ref, out_ref, gp_ref, gow_ref, pad_ref):
    @pl.when(pl.program_id(0) == 0)
    def _():
        gow_ref[...] = jnp.zeros_like(gow_ref)

    group, rows, chans = km_ref.shape
    v = (km_ref[...] + so_ref[...].astype(F32)).reshape(group * rows, chans)
    ct = padded(pad_ref, ct_ref, cells)
    square = v * v
    s = jnp.tanh(0.7978845608 * v * (1.0 + 0.044715 * square))
    half = 0.5 * (1.0 + s)
    hidden = (v * half).astype(BF)
    slope = half + 0.5 * v * (1.0 - s * s) * (0.7978845608 * (1.0 + 3.0 * 0.044715 * square))
    mixed = dot(hidden, w_ref[...]).reshape(km_ref.shape)[:, :cells]
    out_ref[...] = (f_ref[...].astype(F32) + mixed).astype(BF)
    gp_ref[...] = (dot(ct, wt_ref[...]) * slope).astype(BF).reshape(km_ref.shape)
    gow_ref[...] += dot(hidden, ct, ((0,), (0,)))


def block_swap(parts):
    group = lax.broadcasted_iota(jnp.int32, parts[0].shape, 1) // 16
    for k in range(3):
        high = (group >> k) & 1 == 1
        width = 16 << k
        fresh = list(parts)
        for a in range(8):
            if (a >> k) & 1 == 0:
                b = a + (1 << k)
                fresh[a] = jnp.where(high, pltpu.roll(parts[b], width, 1), parts[a])
                fresh[b] = jnp.where(high, parts[b], pltpu.roll(parts[a], 128 - width, 1))
        parts = fresh
    return parts


def tile_swap(x):
    row = lax.broadcasted_iota(jnp.int32, x.shape, 1)
    group = lax.broadcasted_iota(jnp.int32, x.shape, 2) // 16
    for k in range(3):
        row_bit = (row >> k) & 1
        group_bit = (group >> k) & 1
        width = 16 << k
        down = pltpu.roll(pltpu.roll(x, 8 - (1 << k), 1), width, 2)
        up = down if k == 2 else pltpu.roll(pltpu.roll(x, 1 << k, 1), 128 - width, 2)
        x = jnp.where(row_bit == group_bit, x, jnp.where(group_bit == 1, down, up))
    return x


PAD = 80
MESH = pl.DeviceIdType.MESH


def transfer(axis, me, parts, source, target, bulk, send_sem, recv_sem):
    def start():
        def step(d, carry):
            peer = lax.rem(me + d, parts)
            pltpu.make_async_remote_copy(
                src_ref=source(peer),
                dst_ref=target(me),
                send_sem=send_sem,
                recv_sem=recv_sem,
                device_id={axis: peer},
                device_id_type=MESH,
            ).start()
            return carry

        lax.fori_loop(1, parts, step, 0, unroll=7 if parts == 8 else 5)

    def arrive():
        pltpu.make_async_copy(bulk, bulk, recv_sem).wait()

    def drain():
        pltpu.make_async_copy(bulk, bulk, send_sem).wait()

    return start, arrive, drain


def greet():
    barrier = pltpu.get_barrier_semaphore()
    total = 0
    for axis in ("lon", "lat"):
        me, parts = lax.axis_index(axis), lax.axis_size(axis)

        def body(d, carry, axis=axis, me=me, parts=parts):
            pl.semaphore_signal(barrier, inc=1, device_id={axis: lax.rem(me + d, parts)}, device_id_type=MESH)
            return carry

        lax.fori_loop(1, parts, body, 0, unroll=7 if parts == 8 else 5)
        total += parts - 1
    return lambda: pl.semaphore_wait(barrier, total)


def reducer(flat, got1, part, got2, whole, sems):
    s1, r1, s2, r2, s3, r3 = sems
    lat, lon = lax.axis_index("lat"), lax.axis_index("lon")
    lats, lons = lax.axis_size("lat"), lax.axis_size("lon")
    n = part.shape[0]

    def block(ref, b):
        return ref.at[pl.ds(pl.multiple_of(b * n, 16), n)]

    first = transfer(
        "lat", lat, lats, lambda p: block(flat, p), lambda s: got1.at[s], got1.at[pl.ds(0, lats - 1)], s1.at[0], r1.at[0]
    )
    second = transfer("lon", lon, lons, lambda p: part, lambda s: got2.at[s], got2.at[pl.ds(0, lons - 1)], s2.at[0], r2.at[0])
    third = transfer(
        "lat", lat, lats, lambda p: block(whole, lat), lambda s: block(whole, s),
        whole.at[pl.ds(0, (lats - 1) * n)], s3.at[0], r3.at[0],
    )

    def total(ref):
        add = lambda s, carry: carry + ref[s].astype(F32)
        return lax.fori_loop(1, ref.shape[0], add, ref[0].astype(F32)).astype(BF)

    def begin():
        first[0]()
        got1[lat] = flat[pl.ds(pl.multiple_of(lat * n, 16), n)]

    def across():
        first[1]()
        part[...] = total(got1)
        second[0]()
        got2[lon] = part[...]

    def spread():
        second[1]()
        whole[pl.ds(pl.multiple_of(lat * n, 16), n)] = total(got2)
        third[0]()

    def end():
        third[1]()
        for t in (first, second, third):
            t[2]()

    return begin, across, spread, end


def reducer_scratch(lats, lons, n):
    sem = pltpu.SemaphoreType.DMA((1,))
    return [
        pltpu.VMEM((lats * n, 128), BF),
        pltpu.VMEM((lats, n, 128), BF),
        pltpu.VMEM((n, 128), BF),
        pltpu.VMEM((lons, n, 128), BF),
        pltpu.VMEM((lats * n, 128), BF),
        *[sem] * 6,
    ]


EARLY = 288
LATE = 112


def pass_kernel(forward, cells, *refs):
    refs = list(refs)

    def take(n):
        head = refs[:n]
        del refs[:n]
        return head

    x_ref, into_ref = take(2)
    if forward:
        (mix_ref,) = take(1)
    late_in = take(8 if forward else 13)
    if forward:
        grid_ref, stencil_ref, bands_ref = take(3)
    else:
        out_ref, early_ref, gmw_ref, gain_total = take(4)
    late_ref = take(len(late_in))
    (late_sem,) = take(1)
    table_ref, turned_ref, back_ref, gain_ref, in_scale, out_scale, taps_ref, kernel_ref = late_ref[:8]
    if not forward:
        field_ref, gow_ref, bands_ref, ct_ref, wt_ref = late_ref[8:]
    send1, recv1, send2, recv2, send3, recv3, send4, recv4 = take(8)
    modes, rows_ref, ext, from_left, from_right, band_ref, spare, part_ref = take(8)
    s1, r1, s2, r2, s3, r3, s4, r4, hs, hr = take(10)
    if not forward:
        pad_ref, grad_ref, grid_ref, stencil_ref, gain_out = take(5)
        red = take(11)
        begin, across, spread, end = reducer(*red[:5], red[5:])
        red2 = take(11)
        begin2, across2, spread2, end2 = reducer(*red2[:5], red2[5:])
    late_copies = [pltpu.make_async_copy(a, b, late_sem.at[n]) for n, (a, b) in enumerate(zip(late_in, late_ref))]
    lat, lon = lax.axis_index("lat"), lax.axis_index("lon")
    lons, lats = lax.axis_size("lon"), lax.axis_size("lat")
    rows = x_ref.shape[0]
    chans = x_ref.shape[2]
    enter = greet()

    def way(axis, me, parts, send, recv, ss, rs):
        def at(v):
            start, arrive, drain = transfer(
                axis, me, parts,
                lambda p: send.at[v, p], lambda s: recv.at[v, s], recv.at[v, pl.ds(0, parts - 1)], ss.at[v], rs.at[v],
            )

            def go():
                start()
                recv[v, me] = send[v, me]

            return go, arrive, drain

        return [at(v) for v in range(3)]

    lon_in = way("lon", lon, lons, send1, recv1, s1, r1)
    lat_in = way("lat", lat, lats, send2, recv2, s2, r2)
    lat_out = way("lat", lat, lats, send3, recv3, s3, r3)
    lon_out = way("lon", lon, lons, send4, recv4, s4, r4)
    order = lax.broadcasted_iota(jnp.int32, (192, 128), 1) // 32
    lane_group = lax.broadcasted_iota(jnp.int32, (192, 128), 1) // 16
    blank = jnp.zeros((8, 128), F32)

    def sideways(source, target, n, step):
        return pltpu.make_async_remote_copy(
            src_ref=source, dst_ref=target, send_sem=hs.at[n], recv_sem=hr.at[n],
            device_id={"lon": lax.rem(lon + step + lons, lons)}, device_id_type=MESH,
        )

    def vertical(source, target, n, step):
        return pltpu.make_async_remote_copy(
            src_ref=source, dst_ref=target, send_sem=hs.at[n], recv_sem=hr.at[n],
            device_id={"lat": lax.rem(lat + step + lats, lats)}, device_id_type=MESH,
        )

    to_right = sideways(ext.at[pl.ds(1, rows), pl.ds(80, 16)], from_left, 0, 1)
    to_left = sideways(ext.at[pl.ds(1, rows), pl.ds(0, 16)], from_right, 1, -1)
    to_below = vertical(ext.at[rows], ext.at[0], 2, 1)
    to_above = vertical(ext.at[1], ext.at[rows + 1], 3, -1)

    def fill(i, carry):
        if forward:
            ext[1 + i, 80:96] = jnp.zeros((16, chans), BF)
        ext[1 + i, : x_ref.shape[1]] = x_ref[i]
        return carry

    def halo_columns():
        for c in (to_right, to_left):
            c.wait()
        place = lax.broadcasted_iota(jnp.int32, (16, chans), 0)

        def step(i, carry):
            own = ext[1 + i, 80:96].astype(F32)
            right = pltpu.roll(from_right[i].astype(F32), 10, 0)
            left = pltpu.roll(from_left[i].astype(F32), 6, 0)
            ext[1 + i, 80:96] = jnp.where(place < 10, own, jnp.where(place < 13, right, 0.0)).astype(BF)
            ext[1 + i, 96:112] = jnp.zeros((16, chans), BF)
            ext[1 + i, 112:128] = jnp.where(place >= 13, left, 0.0).astype(BF)
            return carry

        lax.fori_loop(0, rows, step, 0, unroll=2)

        @pl.when(lat < lats - 1)
        def _():
            to_below.start()

        @pl.when(lat > 0)
        def _():
            to_above.start()

        @pl.when(lat == 0)
        def _():
            ext[0] = jnp.zeros((EXT, chans), BF)

        @pl.when(lat == lats - 1)
        def _():
            ext[rows + 1] = jnp.zeros((EXT, chans), BF)

    def halo_rows():
        @pl.when(lat > 0)
        def _():
            to_below.wait_recv()

        @pl.when(lat < lats - 1)
        def _():
            to_above.wait_recv()

    def halo_drain():
        @pl.when(lat < lats - 1)
        def _():
            to_below.wait_send()

        @pl.when(lat > 0)
        def _():
            to_above.wait_send()

    def stencil(first):
        def step(n, carry):
            for a in range(2):
                i = first + 2 * n + a
                band_matrix(taps_ref, i, band_ref.at[a], cells)
                source = ext[pl.ds(i, 3)].reshape(3 * EXT, chans)
                part = dot(band_ref[a], source).astype(BF)
                for k in range(3):
                    part_ref[k, 2 * n + a] = part[k * ROWS : (k + 1) * ROWS]
            return carry

        lax.fori_loop(0, 2, step, 0)
        total = None
        for k in range(3):
            part = dot(part_ref[k].reshape(4 * ROWS, chans), kernel_ref[k])
            total = part if total is None else total + part
        stencil_ref[first : first + 4] = total.reshape(4, ROWS, chans)
        if not forward:
            own = pad_ref[first : first + 4].reshape(4 * ROWS, chans)
            for k in range(3):
                add = dot(own, part_ref[k].reshape(4 * ROWS, chans), ((0,), (0,)))
                grad_ref[k] = add if first == START else grad_ref[k] + add

    def tiles(body):
        def step(n, carry):
            body(n // 6, pl.multiple_of(n % 6 * 16, 16))
            return carry

        lax.fori_loop(0, 18, step, 0, unroll=3)

    def split(v):
        lanes_v = slice(v * 128, (v + 1) * 128)
        if forward:
            def mix(g, carry):
                block = ext[pl.ds(1 + g * 8, 8), 0:ROWS].reshape(8 * ROWS, chans)
                spare[pl.ds(g * 8, 8)] = dot(block, mix_ref[:, lanes_v]).reshape(8, ROWS, 128)
                return carry

            lax.fori_loop(0, 3, mix, 0)

        def body(g, j):
            if forward:
                parts = [spare[g * 8 + n, pl.ds(j, 16)] for n in range(8)]
            else:
                parts = [ext[1 + g * 8 + n, pl.ds(j, 16), lanes_v].astype(F32) for n in range(8)]
            lanes = pl.ds(pl.multiple_of(g * 128, 128), 128)
            for p, part in enumerate(block_swap(parts)):
                send1[v, p, pl.ds(j, 16), lanes] = part.astype(BF)

        tiles(body)
        lon_in[v][0]()

    def analyse(v):
        lon_in[v][1]()
        modes[...] = dot(into_ref[...], recv1[v].reshape(lons * ROWS, 384))

        def step(b, carry):
            block = modes[pl.ds(pl.multiple_of(b * 24, 8), 24), :]
            turned = [tile_swap(block[:, g * 128 : (g + 1) * 128].reshape(3, 8, 128)) for g in range(3)]
            pieces = [turned[g][o] for o in range(3) for g in range(3)] + [blank]
            send2[v, b] = jnp.concatenate(pieces, axis=0).astype(BF)
            return carry

        lax.fori_loop(0, lats, step, 0, unroll=4)
        lat_in[v][0]()

    def filter_bands(v):
        lat_in[v][1]()
        lanes = slice(v * 128, (v + 1) * 128)

        def gather(b, carry):
            at = pl.ds(pl.multiple_of(b * 24, 8), 24)
            block = recv2[v, b].astype(F32)
            for o in range(3):
                rows_ref[o, at] = block[o * 24 : (o + 1) * 24] * in_scale[o, at]
            return carry

        lax.fori_loop(0, lats, gather, 0, unroll=4)
        gain_sum = None
        for o in range(3):
            every = dot(table_ref[o], rows_ref[o].astype(BF))
            band = every[:192]
            for m in range(1, 4):
                band = jnp.where(order == m, every[m * 192 : (m + 1) * 192], band)
            if forward:
                bands_ref[o, :, lanes] = band
            else:
                term = band * bands_ref[o, :, lanes]
                gain_sum = term if gain_sum is None else gain_sum + term
            band = band * gain_ref[:, lanes]
            spread_out = jnp.concatenate([jnp.where(order == m, band, 0.0).astype(BF) for m in range(4)], axis=0)
            rows_ref[o] = dot(turned_ref[o], spread_out) * out_scale[o]

        def scatter(b, carry):
            at = pl.ds(pl.multiple_of(b * 24, 8), 24)
            send3[v, b] = jnp.concatenate([rows_ref[o, at] for o in range(3)] + [blank], axis=0).astype(BF)
            return carry

        lax.fori_loop(0, lats, scatter, 0, unroll=4)
        lat_out[v][0]()
        if not forward:
            for width in (16, 32, 64):
                gain_sum = gain_sum + pltpu.roll(gain_sum, width, 1)
            gain_out[:, lanes] = jnp.where(lane_group == lon, gain_sum, 0.0)

    def synthesise(v):
        lat_out[v][1]()

        def step(b, carry):
            turned = tile_swap(recv3[v, b].astype(F32)[:72].reshape(9, 8, 128))
            wide = [jnp.concatenate([turned[o * 3 + g] for o in range(3)], axis=0) for g in range(3)]
            modes[pl.ds(pl.multiple_of(b * 24, 8), 24), :] = jnp.concatenate(wide, axis=1)
            return carry

        lax.fori_loop(0, lats, step, 0, unroll=4)
        send4[v] = dot(back_ref[...], modes[...].astype(BF)).astype(BF).reshape(lons, ROWS, 384)
        lon_out[v][0]()

    def join(v):
        lon_out[v][1]()

        def body(g, j):
            lanes = pl.ds(pl.multiple_of(g * 128, 128), 128)
            parts = [recv4[v, p, pl.ds(j, 16), lanes].astype(F32) for p in range(8)]
            for n, part in enumerate(block_swap(parts)):
                grid_ref[g * 8 + n, pl.ds(j, 16), v * 128 : (v + 1) * 128] = part.astype(BF)

        tiles(body)

    def early_begin():
        flat = red[0]
        for k in range(4):
            for v in range(3):
                block = (grad_ref[k] if k < 3 else gow_ref[...])[:, v * 128 : (v + 1) * 128]
                flat[(k * 3 + v) * 384 : (k * 3 + v + 1) * 384] = block.astype(BF)
        begin()

    def early_end():
        end()
        whole = red[4]
        for k in range(4):
            for v in range(3):
                early_ref[k, :, v * 128 : (v + 1) * 128] = whole[(k * 3 + v) * 384 : (k * 3 + v + 1) * 384].astype(F32)

    def own_rows(i, carry):
        pad_ref[i, 80:96] = jnp.zeros((16, chans), BF)
        pad_ref[i, :cells] = field_ref[i]
        return carry

    def weigh(v):
        lanes = slice(v * 128, (v + 1) * 128)

        def step(n, carry):
            some = pl.ds(n * 8, 8)
            own = pad_ref[some].reshape(8 * ROWS, chans)
            return carry + dot(own, grid_ref[some, :, lanes].reshape(8 * ROWS, 128), ((0,), (0,)))

        own = pad_ref[0:8].reshape(8 * ROWS, chans)
        first = dot(own, grid_ref[0:8, :, lanes].reshape(8 * ROWS, 128), ((0,), (0,)))
        gmw_ref[:, lanes] = lax.fori_loop(1, 3, step, first)

    def late_begin():
        flat = red2[0]
        for v in range(3):
            lanes = slice(v * 128, (v + 1) * 128)
            flat[v * 576 : v * 576 + 384] = gmw_ref[:, lanes].astype(BF)
            flat[v * 576 + 384 : (v + 1) * 576] = gain_out[:, lanes].astype(BF)
        flat[1728:] = jnp.zeros((64, 128), BF)
        begin2()

    def late_end():
        end2()
        whole = red2[4]
        for v in range(3):
            lanes = slice(v * 128, (v + 1) * 128)
            gmw_ref[:, lanes] = whole[v * 576 : v * 576 + 384].astype(F32)
            gain_total[:, lanes] = whole[v * 576 + 384 : (v + 1) * 576].astype(F32)

    def field_rows(first):
        def step(n, carry):
            some = pl.ds(first + n * 4, 4)
            mixed = dot(grid_ref[some].reshape(4 * ROWS, chans), wt_ref[...]).reshape(4, ROWS, chans)
            add = stencil_ref[some] + mixed
            out_ref[some] = (ct_ref[some].astype(F32) + add[:, :cells]).astype(BF)
            return carry

        lax.fori_loop(0, 2, step, 0)

    for c in late_copies:
        c.start()
    lax.fori_loop(0, rows, fill, 0, unroll=2)
    enter()
    to_right.start()
    to_left.start()
    for v in range(3):
        split(v)
    for c in late_copies:
        c.wait()
    halo_columns()
    START = 4
    if not forward:
        lax.fori_loop(0, rows, own_rows, 0, unroll=2)
    stencil(4)
    stencil(8)
    analyse(0)
    stencil(12)
    stencil(16)
    filter_bands(0)
    analyse(1)
    halo_rows()
    stencil(20)
    if not forward:
        stencil(0)
        early_begin()
    synthesise(0)
    filter_bands(1)
    analyse(2)
    if forward:
        stencil(0)
    synthesise(1)
    filter_bands(2)
    if not forward:
        across()
    join(0)
    if not forward:
        weigh(0)
    synthesise(2)
    if not forward:
        spread()
    join(1)
    if not forward:
        weigh(1)
    join(2)
    if not forward:
        weigh(2)
        late_begin()
        field_rows(0)
        across2()
        field_rows(8)
        spread2()
        field_rows(16)
        early_end()
        late_end()
    halo_drain()
    for road in (lon_in, lat_in, lat_out, lon_out):
        for v in range(3):
            road[v][2]()


def pass_call(forward, cells, first, late, outs):
    lons, lats = lax.axis_size("lon"), lax.axis_size("lat")
    rows, _, chans = first[0].shape
    lon_buf = pltpu.VMEM((3, lons, ROWS, 384), BF)
    lat_buf = pltpu.VMEM((3, lats, PAD, 128), BF)
    lon_sem = lat_sem = pltpu.SemaphoreType.DMA((3,))
    scratch = [pltpu.VMEM(a.shape, a.dtype) for a in late] + [pltpu.SemaphoreType.DMA((len(late),))]
    scratch += [lon_buf, lon_buf] + [lat_buf] * 4 + [lon_buf, lon_buf]
    scratch += [
        pltpu.VMEM((384, 384), F32),
        pltpu.VMEM((3, 384, 128), F32),
        pltpu.VMEM((rows + 2, EXT, chans), BF),
        pltpu.VMEM((rows, 16, chans), BF),
        pltpu.VMEM((rows, 16, chans), BF),
        pltpu.VMEM((2, 3 * ROWS, 3 * EXT), BF),
        pltpu.VMEM((rows, ROWS, 128) if forward else (8, 128), F32),
        pltpu.VMEM((3, 4, ROWS, chans), BF),
    ]
    scratch += [lon_sem, lon_sem, lat_sem, lat_sem, lat_sem, lat_sem, lon_sem, lon_sem]
    scratch += [pltpu.SemaphoreType.DMA((4,)), pltpu.SemaphoreType.DMA((4,))]
    if not forward:
        wide = (rows, ROWS, chans)
        scratch += [pltpu.VMEM(wide, BF), pltpu.VMEM((3, chans, chans), F32), pltpu.VMEM(wide, BF), pltpu.VMEM(wide, F32)]
        scratch += [pltpu.VMEM((192, chans), F32)]
        scratch += reducer_scratch(lats, lons, EARLY) + reducer_scratch(lats, lons, LATE)
    return pl.pallas_call(
        functools.partial(pass_kernel, forward, cells),
        out_shape=outs,
        in_specs=[VMEM] * len(first) + [pl.BlockSpec(memory_space=pl.ANY)] * len(late),
        out_specs=[VMEM] * len(outs),
        scratch_shapes=scratch,
        compiler_params=pltpu.CompilerParams(
            collective_id=1 if forward else 2, has_side_effects=True, vmem_limit_bytes=60 << 20
        ),
    )(*first, *late)


def fourier_tables(lon_count, cells, lat_parts):
    j = np.arange(lon_count)
    angles = (j[:, None] * np.arange(ORDERS)[None, :] % lon_count) * (2.0 * np.pi / lon_count)
    waves = np.stack([np.cos(angles), -np.sin(angles)], axis=-1).reshape(lon_count // cells, cells, 2 * ORDERS)
    waves = np.pad(waves, ((0, 0), (0, ROWS - cells), (0, 0))).reshape(-1, 2 * ORDERS)
    return jnp.asarray(waves.T, BF), jnp.asarray(waves, BF)


def legendre_kernel(m_ref, x_ref, diag_ref, out_ref):
    m = m_ref[...]
    x = x_ref[...]
    diag = diag_ref[...]
    reps = x.shape[1] // m.shape[1]

    def wide(a):
        return jnp.concatenate([a] * reps, axis=1)

    mw = wide(m)

    def step(l, carry):
        prev, before, a_prev = carry
        lf = l.astype(F32)
        above = lf > m
        den = jnp.where(above, lf * lf - m * m, 1.0)
        a = jnp.where(above, jnp.sqrt((4.0 * lf * lf - 1.0) / den), 1.0)
        cur = wide(a) * (x * prev - before * wide(1.0 / a_prev))
        cur = jnp.where(lf == mw, diag, jnp.where(lf > mw, cur, 0.0))
        out_ref[l] = cur.astype(BF)
        return cur, prev, a

    blank = x * 0.0
    lax.fori_loop(0, out_ref.shape[0], step, (blank, blank, m * 0.0 + 1.0), unroll=4)


def colatitudes(row_index, lat_count):
    return (row_index.astype(F32) + 0.5) * (math.pi / lat_count)


def legendre_rows(orders, lat_count, degrees):
    slots = 16
    m = jnp.pad(orders, (0, slots - orders.shape[0])).astype(F32)[:, None]
    colat = colatitudes(jnp.arange(lat_count, dtype=jnp.int32), lat_count)[None, :]
    log_start = 0.5 * (lax.lgamma(m + 1.5) - lax.lgamma(m + 1.0) - lax.lgamma(F32(1.5) + 0.0 * m))
    diag = jnp.exp(log_start + m * jnp.log(jnp.sin(colat))) / math.sqrt(4.0 * math.pi)
    x = jnp.broadcast_to(jnp.cos(colat), diag.shape)
    table = pl.pallas_call(
        legendre_kernel,
        out_shape=jax.ShapeDtypeStruct((degrees, slots, lat_count), BF),
        in_specs=[VMEM] * 3,
        out_specs=VMEM,
        compiler_params=pltpu.CompilerParams(vmem_limit_bytes=40 << 20),
    )(jnp.broadcast_to(m, (slots, 128)), x, diag)
    return jnp.transpose(table[:, : orders.shape[0]], (1, 0, 2))


def tap_table(kernel_basis, lon_reach):
    count = kernel_basis.shape[2]
    offsets = jnp.abs(jnp.arange(count, dtype=jnp.int32) - count // 2)
    mask = offsets[None, :, None] <= lon_reach[:, None, :]
    return kernel_basis * mask[None].astype(F32)


def by_rows(body, args, whole, outs, totals, scratch, group=4):
    def cut(a):
        return pl.BlockSpec((group,) + a.shape[1:], lambda g: (g, 0, 0))

    def full(a):
        return pl.BlockSpec(a.shape, lambda g: (0,) * len(a.shape))

    return pl.pallas_call(
        body,
        grid=(args[0].shape[0] // group,),
        in_specs=[cut(a) for a in args] + [full(a) for a in whole],
        out_specs=[cut(a) for a in outs] + [full(a) for a in totals],
        out_shape=list(outs) + list(totals),
        scratch_shapes=scratch,
        compiler_params=pltpu.CompilerParams(vmem_limit_bytes=56 << 20),
    )(*args, *whole)


def local(field, cotangent, kernel_weights, spectral_weight, out_weight, degree_gain, kernel_basis, lon_reach):
    rows, cells, chans = field.shape
    lat_parts, lon_parts = lax.axis_size("lat"), lax.axis_size("lon")
    lat, lon = lax.axis_index("lat"), lax.axis_index("lon")
    lat_count, lon_count = rows * lat_parts, cells * lon_parts
    degrees = degree_gain.shape[0]
    slots = ORDERS // lat_parts
    shape = jax.ShapeDtypeStruct

    taps = tap_table(kernel_basis, lon_reach)
    near = lax.dynamic_slice_in_dim(jnp.pad(taps, ((0, 0), (0, 0), (0, 0), (1, 1))), lat * rows, rows + 2, 3)
    own_taps = tap_rows(near[:, :, :, 1 : rows + 1])
    turned = near[:, ::-1, ::-1]
    adj_taps = tap_rows(jnp.stack([turned[:, r, :, r : r + rows] for r in range(3)], axis=1))

    my_orders = lat * slots + jnp.arange(slots, dtype=jnp.int32)
    table = legendre_rows(my_orders, lat_count, degrees)
    into, back = fourier_tables(lon_count, cells, lat_parts)
    table = table.reshape(3, 4 * degrees, lat_count)
    turned = jnp.transpose(table, (0, 2, 1))
    quad = 2.0 * math.pi / lon_count * (math.pi / lat_count) * jnp.sin(
        colatitudes(jnp.arange(lat_count, dtype=jnp.int32), lat_count)
    )
    quad = jnp.broadcast_to(quad[None, :, None], (3, lat_count, 128))
    mode_weight = jnp.where(my_orders == 0, 1.0, 2.0).astype(F32).reshape(3, 1, 4, 1)
    mode_weight = jnp.broadcast_to(mode_weight, (3, lat_count, 4, 32)).reshape(3, lat_count, 128)
    groups = degree_gain.reshape(degrees, 3, lon_parts, 16)
    gain = lax.dynamic_slice_in_dim(groups, lon, 1, 2)
    gain = jnp.broadcast_to(gain, groups.shape).reshape(degrees, chans)

    wide = (rows, ROWS, chans)
    spec_out, kernel_mix, bands = pass_call(
        True,
        cells,
        [field, into, spectral_weight],
        [table, turned, back, gain, quad, mode_weight, own_taps, kernel_weights],
        [shape(wide, BF), shape(wide, F32), shape((3, degrees, chans), F32)],
    )
    output_field, grad_pre, grad_out_w = by_rows(
        functools.partial(pointwise, cells),
        [kernel_mix, spec_out, field, cotangent],
        [out_weight, out_weight.T],
        [shape(field.shape, BF), shape(wide, BF)],
        [shape((chans, chans), F32)],
        [pltpu.VMEM((4, ROWS, chans), BF)],
    )
    turned_weights = jnp.transpose(kernel_weights, (0, 2, 1))
    grad_field, early, grad_mix_w, gain_total = pass_call(
        False,
        cells,
        [grad_pre, into],
        [table, turned, back, gain, mode_weight, quad, adj_taps, turned_weights]
        + [field, grad_out_w, bands, cotangent, spectral_weight.T],
        [shape(field.shape, BF), shape((4, chans, chans), F32), shape((chans, chans), F32), shape((degrees, chans), F32)],
    )
    weight_grads = jnp.concatenate([early[:3], grad_mix_w[None], early[3:]]) / math.sqrt(lat_count * lon_count)
    return output_field, grad_field, weight_grads, gain_total


def solution(mesh):
    placed = (P("lat", "lon", None), P("lat", "lon", None), P(), P(), P(), P(), P(), P())
    return jax.shard_map(
        local,
        mesh=mesh,
        in_specs=placed,
        out_specs=(P("lat", "lon", None), P("lat", "lon", None), P(), P()),
        check_vma=False,
    )
```

```python
import functools
import math

import jax
import jax.numpy as jnp
import numpy as np
from jax import lax
from jax.experimental import pallas as pl
from jax.experimental.pallas import tpu as pltpu
from jax.sharding import PartitionSpec as P

ORDERS = 192
BF = jnp.bfloat16
F32 = jnp.float32
VMEM = pl.BlockSpec(memory_space=pltpu.VMEM)
ROWS = 96
EXT = 128


def dot(a, b, dims=((1,), (0,))):
    return lax.dot_general(a, b, (dims, ((), ())), preferred_element_type=F32)


def tap_rows(taps):
    k, r, t, n = taps.shape
    flat = jnp.transpose(taps, (3, 0, 1, 2)).reshape(n, k * r, t)
    wide = jnp.concatenate([flat[:, :, 3:], jnp.zeros((n, k * r, EXT - t), F32), flat[:, :, :3]], axis=2)
    return jnp.pad(wide, ((0, 0), (0, 16 - k * r), (0, 0)))


def band_matrix(taps_ref, i, band_ref, cells):
    keep = lax.broadcasted_iota(jnp.int32, (ROWS, EXT), 0) < cells
    rows = taps_ref[i]
    for k in range(3):
        for r in range(3):
            row = jnp.broadcast_to(rows[3 * k + r : 3 * k + r + 1], (ROWS, EXT))
            block = pltpu.roll(row, 0, 1, stride=1, stride_axis=0)
            band_ref[k * ROWS : (k + 1) * ROWS, r * EXT : (r + 1) * EXT] = jnp.where(keep, block, 0.0).astype(BF)


def padded(pad_ref, ref, cells):
    pad_ref[:, 80:] = jnp.zeros_like(pad_ref[:, 80:])
    pad_ref[:, :cells] = ref[...]
    return pad_ref[...].reshape(-1, pad_ref.shape[2])


def pointwise(cells, km_ref, so_ref, f_ref, ct_ref, w_ref, wt_ref, out_ref, gp_ref, gow_ref, pad_ref):
    @pl.when(pl.program_id(0) == 0)
    def _():
        gow_ref[...] = jnp.zeros_like(gow_ref)

    group, rows, chans = km_ref.shape
    v = (km_ref[...].astype(F32) + so_ref[...].astype(F32)).reshape(group * rows, chans)
    ct = padded(pad_ref, ct_ref, cells)
    square = v * v
    s = jnp.tanh(0.7978845608 * v * (1.0 + 0.044715 * square))
    half = 0.5 * (1.0 + s)
    hidden = (v * half).astype(BF)
    slope = half + 0.5 * v * (1.0 - s * s) * (0.7978845608 * (1.0 + 3.0 * 0.044715 * square))
    mixed = dot(hidden, w_ref[...]).reshape(km_ref.shape)[:, :cells]
    out_ref[...] = (f_ref[...].astype(F32) + mixed).astype(BF)
    gp_ref[...] = (dot(ct, wt_ref[...]) * slope).astype(BF).reshape(km_ref.shape)
    gow_ref[...] += dot(hidden, ct, ((0,), (0,)))


def block_swap(parts):
    group = lax.broadcasted_iota(jnp.int32, parts[0].shape, 1) // 16
    for k in range(3):
        high = (group >> k) & 1 == 1
        width = 16 << k
        fresh = list(parts)
        for a in range(8):
            if (a >> k) & 1 == 0:
                b = a + (1 << k)
                fresh[a] = jnp.where(high, pltpu.roll(parts[b], width, 1), parts[a])
                fresh[b] = jnp.where(high, parts[b], pltpu.roll(parts[a], 128 - width, 1))
        parts = fresh
    return parts


def tile_swap(x):
    row = lax.broadcasted_iota(jnp.int32, x.shape, 1)
    group = lax.broadcasted_iota(jnp.int32, x.shape, 2) // 16
    for k in range(3):
        row_bit = (row >> k) & 1
        group_bit = (group >> k) & 1
        width = 16 << k
        down = pltpu.roll(pltpu.roll(x, 8 - (1 << k), 1), width, 2)
        up = down if k == 2 else pltpu.roll(pltpu.roll(x, 1 << k, 1), 128 - width, 2)
        x = jnp.where(row_bit == group_bit, x, jnp.where(group_bit == 1, down, up))
    return x


PAD = 80
MESH = pl.DeviceIdType.MESH


def transfer(axis, me, parts, source, target, bulk, send_sem, recv_sem):
    def start():
        def step(d, carry):
            peer = lax.rem(me + d, parts)
            pltpu.make_async_remote_copy(
                src_ref=source(peer),
                dst_ref=target(me),
                send_sem=send_sem,
                recv_sem=recv_sem,
                device_id={axis: peer},
                device_id_type=MESH,
            ).start()
            return carry

        lax.fori_loop(1, parts, step, 0, unroll=7 if parts == 8 else 5)

    def arrive():
        pltpu.make_async_copy(bulk, bulk, recv_sem).wait()

    def drain():
        pltpu.make_async_copy(bulk, bulk, send_sem).wait()

    return start, arrive, drain


def greet():
    barrier = pltpu.get_barrier_semaphore()
    total = 0
    for axis in ("lon", "lat"):
        me, parts = lax.axis_index(axis), lax.axis_size(axis)

        def body(d, carry, axis=axis, me=me, parts=parts):
            pl.semaphore_signal(barrier, inc=1, device_id={axis: lax.rem(me + d, parts)}, device_id_type=MESH)
            return carry

        lax.fori_loop(1, parts, body, 0, unroll=7 if parts == 8 else 5)
        total += parts - 1
    return lambda: pl.semaphore_wait(barrier, total)


def reducer(flat, got1, part, got2, whole, sems):
    s1, r1, s2, r2, s3, r3 = sems
    lat, lon = lax.axis_index("lat"), lax.axis_index("lon")
    lats, lons = lax.axis_size("lat"), lax.axis_size("lon")
    n = part.shape[0]

    def block(ref, b):
        return ref.at[pl.ds(pl.multiple_of(b * n, 16), n)]

    first = transfer(
        "lat", lat, lats, lambda p: block(flat, p), lambda s: got1.at[s], got1.at[pl.ds(0, lats - 1)], s1.at[0], r1.at[0]
    )
    second = transfer("lon", lon, lons, lambda p: part, lambda s: got2.at[s], got2.at[pl.ds(0, lons - 1)], s2.at[0], r2.at[0])
    third = transfer(
        "lat", lat, lats, lambda p: block(whole, lat), lambda s: block(whole, s),
        whole.at[pl.ds(0, (lats - 1) * n)], s3.at[0], r3.at[0],
    )

    def total(ref):
        add = lambda s, carry: carry + ref[s].astype(F32)
        return lax.fori_loop(1, ref.shape[0], add, ref[0].astype(F32)).astype(BF)

    def begin():
        first[0]()
        got1[lat] = flat[pl.ds(pl.multiple_of(lat * n, 16), n)]

    def across():
        first[1]()
        part[...] = total(got1)
        second[0]()
        got2[lon] = part[...]

    def spread():
        second[1]()
        whole[pl.ds(pl.multiple_of(lat * n, 16), n)] = total(got2)
        third[0]()

    def end():
        third[1]()
        for t in (first, second, third):
            t[2]()

    return begin, across, spread, end


def reducer_scratch(lats, lons, n):
    sem = pltpu.SemaphoreType.DMA((1,))
    return [
        pltpu.VMEM((lats * n, 128), BF),
        pltpu.VMEM((lats, n, 128), BF),
        pltpu.VMEM((n, 128), BF),
        pltpu.VMEM((lons, n, 128), BF),
        pltpu.VMEM((lats * n, 128), BF),
        *[sem] * 6,
    ]


EARLY = 288
LATE = 112


def pass_kernel(forward, cells, *refs):
    refs = list(refs)

    def take(n):
        head = refs[:n]
        del refs[:n]
        return head

    x_ref, into_ref = take(2)
    if forward:
        (mix_ref,) = take(1)
    late_in = take(8 if forward else 13)
    if forward:
        grid_ref, stencil_ref, bands_ref = take(3)
    else:
        out_ref, early_ref, gmw_ref, gain_total = take(4)
    late_ref = take(len(late_in))
    (late_sem,) = take(1)
    table_ref, turned_ref, back_ref, gain_ref, in_scale, out_scale, taps_ref, kernel_ref = late_ref[:8]
    if not forward:
        field_ref, gow_ref, bands_ref, ct_ref, wt_ref = late_ref[8:]
    send1, recv1, send2, recv2, send3, recv3, send4, recv4 = take(8)
    modes, rows_ref, ext, from_left, from_right, band_ref, spare, part_ref = take(8)
    s1, r1, s2, r2, s3, r3, s4, r4, hs, hr = take(10)
    if not forward:
        pad_ref, grad_ref, grid_ref, stencil_ref, gain_out = take(5)
        red = take(11)
        begin, across, spread, end = reducer(*red[:5], red[5:])
        red2 = take(11)
        begin2, across2, spread2, end2 = reducer(*red2[:5], red2[5:])
    late_copies = [pltpu.make_async_copy(a, b, late_sem.at[n]) for n, (a, b) in enumerate(zip(late_in, late_ref))]
    lat, lon = lax.axis_index("lat"), lax.axis_index("lon")
    lons, lats = lax.axis_size("lon"), lax.axis_size("lat")
    rows = x_ref.shape[0]
    chans = x_ref.shape[2]
    enter = greet()

    def way(axis, me, parts, send, recv, ss, rs):
        def at(v):
            start, arrive, drain = transfer(
                axis, me, parts,
                lambda p: send.at[v, p], lambda s: recv.at[v, s], recv.at[v, pl.ds(0, parts - 1)], ss.at[v], rs.at[v],
            )

            def go():
                start()
                recv[v, me] = send[v, me]

            return go, arrive, drain

        return [at(v) for v in range(3)]

    lon_in = way("lon", lon, lons, send1, recv1, s1, r1)
    lat_in = way("lat", lat, lats, send2, recv2, s2, r2)
    lat_out = way("lat", lat, lats, send3, recv3, s3, r3)
    lon_out = way("lon", lon, lons, send4, recv4, s4, r4)
    order = lax.broadcasted_iota(jnp.int32, (192, 128), 1) // 32
    lane_group = lax.broadcasted_iota(jnp.int32, (192, 128), 1) // 16
    blank = jnp.zeros((8, 128), F32)

    def sideways(source, target, n, step):
        return pltpu.make_async_remote_copy(
            src_ref=source, dst_ref=target, send_sem=hs.at[n], recv_sem=hr.at[n],
            device_id={"lon": lax.rem(lon + step + lons, lons)}, device_id_type=MESH,
        )

    def vertical(source, target, n, step):
        return pltpu.make_async_remote_copy(
            src_ref=source, dst_ref=target, send_sem=hs.at[n], recv_sem=hr.at[n],
            device_id={"lat": lax.rem(lat + step + lats, lats)}, device_id_type=MESH,
        )

    to_right = sideways(ext.at[pl.ds(1, rows), pl.ds(80, 16)], from_left, 0, 1)
    to_left = sideways(ext.at[pl.ds(1, rows), pl.ds(0, 16)], from_right, 1, -1)
    to_below = vertical(ext.at[rows], ext.at[0], 2, 1)
    to_above = vertical(ext.at[1], ext.at[rows + 1], 3, -1)

    def fill(i, carry):
        if forward:
            ext[1 + i, 80:96] = jnp.zeros((16, chans), BF)
        ext[1 + i, : x_ref.shape[1]] = x_ref[i]
        return carry

    def halo_columns():
        for c in (to_right, to_left):
            c.wait()
        place = lax.broadcasted_iota(jnp.int32, (16, chans), 0)

        def step(i, carry):
            own = ext[1 + i, 80:96].astype(F32)
            right = pltpu.roll(from_right[i].astype(F32), 10, 0)
            left = pltpu.roll(from_left[i].astype(F32), 6, 0)
            ext[1 + i, 80:96] = jnp.where(place < 10, own, jnp.where(place < 13, right, 0.0)).astype(BF)
            ext[1 + i, 96:112] = jnp.zeros((16, chans), BF)
            ext[1 + i, 112:128] = jnp.where(place >= 13, left, 0.0).astype(BF)
            return carry

        lax.fori_loop(0, rows, step, 0, unroll=2)

        @pl.when(lat < lats - 1)
        def _():
            to_below.start()

        @pl.when(lat > 0)
        def _():
            to_above.start()

        @pl.when(lat == 0)
        def _():
            ext[0] = jnp.zeros((EXT, chans), BF)

        @pl.when(lat == lats - 1)
        def _():
            ext[rows + 1] = jnp.zeros((EXT, chans), BF)

    def halo_rows():
        @pl.when(lat > 0)
        def _():
            to_below.wait_recv()

        @pl.when(lat < lats - 1)
        def _():
            to_above.wait_recv()

    def halo_drain():
        @pl.when(lat < lats - 1)
        def _():
            to_below.wait_send()

        @pl.when(lat > 0)
        def _():
            to_above.wait_send()

    def stencil(first):
        def step(n, carry):
            for a in range(2):
                i = first + 2 * n + a
                band_matrix(taps_ref, i, band_ref.at[a], cells)
                source = ext[pl.ds(i, 3)].reshape(3 * EXT, chans)
                part = dot(band_ref[a], source).astype(BF)
                for k in range(3):
                    part_ref[k, 2 * n + a] = part[k * ROWS : (k + 1) * ROWS]
            return carry

        lax.fori_loop(0, 2, step, 0)
        total = None
        for k in range(3):
            part = dot(part_ref[k].reshape(4 * ROWS, chans), kernel_ref[k])
            total = part if total is None else total + part
        stencil_ref[first : first + 4] = total.reshape(4, ROWS, chans).astype(stencil_ref.dtype)
        if not forward:
            own = pad_ref[first : first + 4].reshape(4 * ROWS, chans)
            for k in range(3):
                add = dot(own, part_ref[k].reshape(4 * ROWS, chans), ((0,), (0,)))
                grad_ref[k] = add if first == START else grad_ref[k] + add

    def tiles(body):
        def step(n, carry):
            body(n // 6, pl.multiple_of(n % 6 * 16, 16))
            return carry

        lax.fori_loop(0, 18, step, 0, unroll=3)

    def split(v):
        lanes_v = slice(v * 128, (v + 1) * 128)
        if forward:
            def mix(g, carry):
                block = ext[pl.ds(1 + g * 8, 8), 0:ROWS].reshape(8 * ROWS, chans)
                spare[pl.ds(g * 8, 8)] = dot(block, mix_ref[:, lanes_v]).reshape(8, ROWS, 128)
                return carry

            lax.fori_loop(0, 3, mix, 0)

        def body(g, j):
            if forward:
                parts = [spare[g * 8 + n, pl.ds(j, 16)] for n in range(8)]
            else:
                parts = [ext[1 + g * 8 + n, pl.ds(j, 16), lanes_v].astype(F32) for n in range(8)]
            lanes = pl.ds(pl.multiple_of(g * 128, 128), 128)
            for p, part in enumerate(block_swap(parts)):
                send1[v, p, pl.ds(j, 16), lanes] = part.astype(BF)

        tiles(body)
        lon_in[v][0]()

    def analyse(v):
        lon_in[v][1]()
        modes[...] = dot(into_ref[...], recv1[v].reshape(lons * ROWS, 384))

        def step(b, carry):
            block = modes[pl.ds(pl.multiple_of(b * 24, 8), 24), :]
            turned = [tile_swap(block[:, g * 128 : (g + 1) * 128].reshape(3, 8, 128)) for g in range(3)]
            pieces = [turned[g][o] for o in range(3) for g in range(3)] + [blank]
            send2[v, b] = jnp.concatenate(pieces, axis=0).astype(BF)
            return carry

        lax.fori_loop(0, lats, step, 0, unroll=4)
        lat_in[v][0]()

    def filter_bands(v):
        lat_in[v][1]()
        lanes = slice(v * 128, (v + 1) * 128)

        def gather(b, carry):
            at = pl.ds(pl.multiple_of(b * 24, 8), 24)
            block = recv2[v, b].astype(F32)
            for o in range(3):
                rows_ref[o, at] = block[o * 24 : (o + 1) * 24] * in_scale[o, at]
            return carry

        lax.fori_loop(0, lats, gather, 0, unroll=4)
        gain_sum = None
        for o in range(3):
            every = dot(table_ref[o], rows_ref[o].astype(BF))
            band = every[:192]
            for m in range(1, 4):
                band = jnp.where(order == m, every[m * 192 : (m + 1) * 192], band)
            if forward:
                bands_ref[o, :, lanes] = band
            else:
                term = band * bands_ref[o, :, lanes]
                gain_sum = term if gain_sum is None else gain_sum + term
            band = band * gain_ref[:, lanes]
            spread_out = jnp.concatenate([jnp.where(order == m, band, 0.0).astype(BF) for m in range(4)], axis=0)
            rows_ref[o] = dot(turned_ref[o], spread_out) * out_scale[o]

        def scatter(b, carry):
            at = pl.ds(pl.multiple_of(b * 24, 8), 24)
            send3[v, b] = jnp.concatenate([rows_ref[o, at] for o in range(3)] + [blank], axis=0).astype(BF)
            return carry

        lax.fori_loop(0, lats, scatter, 0, unroll=4)
        lat_out[v][0]()
        if not forward:
            for width in (16, 32, 64):
                gain_sum = gain_sum + pltpu.roll(gain_sum, width, 1)
            gain_out[:, lanes] = jnp.where(lane_group == lon, gain_sum, 0.0)

    def synthesise(v):
        lat_out[v][1]()

        def step(b, carry):
            turned = tile_swap(recv3[v, b].astype(F32)[:72].reshape(9, 8, 128))
            wide = [jnp.concatenate([turned[o * 3 + g] for o in range(3)], axis=0) for g in range(3)]
            modes[pl.ds(pl.multiple_of(b * 24, 8), 24), :] = jnp.concatenate(wide, axis=1)
            return carry

        lax.fori_loop(0, lats, step, 0, unroll=4)
        send4[v] = dot(back_ref[...], modes[...].astype(BF)).astype(BF).reshape(lons, ROWS, 384)
        lon_out[v][0]()

    def join(v):
        lon_out[v][1]()

        def body(g, j):
            lanes = pl.ds(pl.multiple_of(g * 128, 128), 128)
            parts = [recv4[v, p, pl.ds(j, 16), lanes].astype(F32) for p in range(8)]
            for n, part in enumerate(block_swap(parts)):
                grid_ref[g * 8 + n, pl.ds(j, 16), v * 128 : (v + 1) * 128] = part.astype(BF)

        tiles(body)

    def early_begin():
        flat = red[0]
        for k in range(4):
            for v in range(3):
                block = (grad_ref[k] if k < 3 else gow_ref[...])[:, v * 128 : (v + 1) * 128]
                flat[(k * 3 + v) * 384 : (k * 3 + v + 1) * 384] = block.astype(BF)
        begin()

    def early_end():
        end()
        whole = red[4]
        for k in range(4):
            for v in range(3):
                early_ref[k, :, v * 128 : (v + 1) * 128] = whole[(k * 3 + v) * 384 : (k * 3 + v + 1) * 384].astype(F32)

    def own_rows(i, carry):
        pad_ref[i, 80:96] = jnp.zeros((16, chans), BF)
        pad_ref[i, :cells] = field_ref[i]
        return carry

    def weigh(v):
        lanes = slice(v * 128, (v + 1) * 128)

        def step(n, carry):
            some = pl.ds(n * 8, 8)
            own = pad_ref[some].reshape(8 * ROWS, chans)
            return carry + dot(own, grid_ref[some, :, lanes].reshape(8 * ROWS, 128), ((0,), (0,)))

        own = pad_ref[0:8].reshape(8 * ROWS, chans)
        first = dot(own, grid_ref[0:8, :, lanes].reshape(8 * ROWS, 128), ((0,), (0,)))
        gmw_ref[:, lanes] = lax.fori_loop(1, 3, step, first)

    def late_begin():
        flat = red2[0]
        for v in range(3):
            lanes = slice(v * 128, (v + 1) * 128)
            flat[v * 576 : v * 576 + 384] = gmw_ref[:, lanes].astype(BF)
            flat[v * 576 + 384 : (v + 1) * 576] = gain_out[:, lanes].astype(BF)
        flat[1728:] = jnp.zeros((64, 128), BF)
        begin2()

    def late_end():
        end2()
        whole = red2[4]
        for v in range(3):
            lanes = slice(v * 128, (v + 1) * 128)
            gmw_ref[:, lanes] = whole[v * 576 : v * 576 + 384].astype(F32)
            gain_total[:, lanes] = whole[v * 576 + 384 : (v + 1) * 576].astype(F32)

    def field_rows(first):
        def step(n, carry):
            some = pl.ds(first + n * 4, 4)
            mixed = dot(grid_ref[some].reshape(4 * ROWS, chans), wt_ref[...]).reshape(4, ROWS, chans)
            add = stencil_ref[some] + mixed
            out_ref[some] = (ct_ref[some].astype(F32) + add[:, :cells]).astype(BF)
            return carry

        lax.fori_loop(0, 2, step, 0)

    for c in late_copies:
        c.start()
    lax.fori_loop(0, rows, fill, 0, unroll=2)
    enter()
    to_right.start()
    to_left.start()
    for v in range(3):
        split(v)
    for c in late_copies:
        c.wait()
    halo_columns()
    START = 4
    if not forward:
        lax.fori_loop(0, rows, own_rows, 0, unroll=2)
    stencil(4)
    stencil(8)
    analyse(0)
    stencil(12)
    stencil(16)
    filter_bands(0)
    analyse(1)
    halo_rows()
    stencil(20)
    if not forward:
        stencil(0)
        early_begin()
    synthesise(0)
    filter_bands(1)
    analyse(2)
    if forward:
        stencil(0)
    synthesise(1)
    filter_bands(2)
    if not forward:
        across()
    join(0)
    if not forward:
        weigh(0)
    synthesise(2)
    if not forward:
        spread()
    join(1)
    if not forward:
        weigh(1)
    join(2)
    if not forward:
        weigh(2)
        late_begin()
        field_rows(0)
        across2()
        field_rows(8)
        spread2()
        field_rows(16)
        early_end()
        late_end()
    halo_drain()
    for road in (lon_in, lat_in, lat_out, lon_out):
        for v in range(3):
            road[v][2]()


def pass_call(forward, cells, first, late, outs):
    lons, lats = lax.axis_size("lon"), lax.axis_size("lat")
    rows, _, chans = first[0].shape
    lon_buf = pltpu.VMEM((3, lons, ROWS, 384), BF)
    lat_buf = pltpu.VMEM((3, lats, PAD, 128), BF)
    lon_sem = lat_sem = pltpu.SemaphoreType.DMA((3,))
    scratch = [pltpu.VMEM(a.shape, a.dtype) for a in late] + [pltpu.SemaphoreType.DMA((len(late),))]
    scratch += [lon_buf, lon_buf] + [lat_buf] * 4 + [lon_buf, lon_buf]
    scratch += [
        pltpu.VMEM((384, 384), F32),
        pltpu.VMEM((3, 384, 128), F32),
        pltpu.VMEM((rows + 2, EXT, chans), BF),
        pltpu.VMEM((rows, 16, chans), BF),
        pltpu.VMEM((rows, 16, chans), BF),
        pltpu.VMEM((2, 3 * ROWS, 3 * EXT), BF),
        pltpu.VMEM((rows, ROWS, 128) if forward else (8, 128), F32),
        pltpu.VMEM((3, 4, ROWS, chans), BF),
    ]
    scratch += [lon_sem, lon_sem, lat_sem, lat_sem, lat_sem, lat_sem, lon_sem, lon_sem]
    scratch += [pltpu.SemaphoreType.DMA((4,)), pltpu.SemaphoreType.DMA((4,))]
    if not forward:
        wide = (rows, ROWS, chans)
        scratch += [pltpu.VMEM(wide, BF), pltpu.VMEM((3, chans, chans), F32), pltpu.VMEM(wide, BF), pltpu.VMEM(wide, F32)]
        scratch += [pltpu.VMEM((192, chans), F32)]
        scratch += reducer_scratch(lats, lons, EARLY) + reducer_scratch(lats, lons, LATE)
    return pl.pallas_call(
        functools.partial(pass_kernel, forward, cells),
        out_shape=outs,
        in_specs=[VMEM] * len(first) + [pl.BlockSpec(memory_space=pl.ANY)] * len(late),
        out_specs=[VMEM] * len(outs),
        scratch_shapes=scratch,
        compiler_params=pltpu.CompilerParams(
            collective_id=1 if forward else 2, has_side_effects=True, vmem_limit_bytes=60 << 20
        ),
    )(*first, *late)


def fourier_tables(lon_count, cells, lat_parts):
    j = np.arange(lon_count)
    angles = (j[:, None] * np.arange(ORDERS)[None, :] % lon_count) * (2.0 * np.pi / lon_count)
    waves = np.stack([np.cos(angles), -np.sin(angles)], axis=-1).reshape(lon_count // cells, cells, 2 * ORDERS)
    waves = np.pad(waves, ((0, 0), (0, ROWS - cells), (0, 0))).reshape(-1, 2 * ORDERS)
    return jnp.asarray(waves.T, BF), jnp.asarray(waves, BF)


def legendre_kernel(m_ref, x_ref, diag_ref, out_ref):
    m = m_ref[...]
    x = x_ref[...]
    diag = diag_ref[...]
    reps = x.shape[1] // m.shape[1]

    def wide(a):
        return jnp.concatenate([a] * reps, axis=1)

    mw = wide(m)

    def step(l, carry):
        prev, before, a_prev = carry
        lf = l.astype(F32)
        above = lf > m
        den = jnp.where(above, lf * lf - m * m, 1.0)
        a = jnp.where(above, jnp.sqrt((4.0 * lf * lf - 1.0) / den), 1.0)
        cur = wide(a) * (x * prev - before * wide(1.0 / a_prev))
        cur = jnp.where(lf == mw, diag, jnp.where(lf > mw, cur, 0.0))
        out_ref[l] = cur.astype(BF)
        return cur, prev, a

    blank = x * 0.0
    lax.fori_loop(0, out_ref.shape[0], step, (blank, blank, m * 0.0 + 1.0), unroll=4)


def colatitudes(row_index, lat_count):
    return (row_index.astype(F32) + 0.5) * (math.pi / lat_count)


def legendre_rows(orders, lat_count, degrees):
    slots = 16
    m = jnp.pad(orders, (0, slots - orders.shape[0])).astype(F32)[:, None]
    colat = colatitudes(jnp.arange(lat_count, dtype=jnp.int32), lat_count)[None, :]
    log_start = 0.5 * (lax.lgamma(m + 1.5) - lax.lgamma(m + 1.0) - lax.lgamma(F32(1.5) + 0.0 * m))
    diag = jnp.exp(log_start + m * jnp.log(jnp.sin(colat))) / math.sqrt(4.0 * math.pi)
    x = jnp.broadcast_to(jnp.cos(colat), diag.shape)
    table = pl.pallas_call(
        legendre_kernel,
        out_shape=jax.ShapeDtypeStruct((degrees, slots, lat_count), BF),
        in_specs=[VMEM] * 3,
        out_specs=VMEM,
        compiler_params=pltpu.CompilerParams(vmem_limit_bytes=40 << 20),
    )(jnp.broadcast_to(m, (slots, 128)), x, diag)
    return jnp.transpose(table[:, : orders.shape[0]], (1, 0, 2))


def tap_table(kernel_basis, lon_reach):
    count = kernel_basis.shape[2]
    offsets = jnp.abs(jnp.arange(count, dtype=jnp.int32) - count // 2)
    mask = offsets[None, :, None] <= lon_reach[:, None, :]
    return kernel_basis * mask[None].astype(F32)


def by_rows(body, args, whole, outs, totals, scratch, group=4):
    def cut(a):
        return pl.BlockSpec((group,) + a.shape[1:], lambda g: (g, 0, 0))

    def full(a):
        return pl.BlockSpec(a.shape, lambda g: (0,) * len(a.shape))

    return pl.pallas_call(
        body,
        grid=(args[0].shape[0] // group,),
        in_specs=[cut(a) for a in args] + [full(a) for a in whole],
        out_specs=[cut(a) for a in outs] + [full(a) for a in totals],
        out_shape=list(outs) + list(totals),
        scratch_shapes=scratch,
        compiler_params=pltpu.CompilerParams(vmem_limit_bytes=56 << 20),
    )(*args, *whole)


def local(field, cotangent, kernel_weights, spectral_weight, out_weight, degree_gain, kernel_basis, lon_reach):
    rows, cells, chans = field.shape
    lat_parts, lon_parts = lax.axis_size("lat"), lax.axis_size("lon")
    lat, lon = lax.axis_index("lat"), lax.axis_index("lon")
    lat_count, lon_count = rows * lat_parts, cells * lon_parts
    degrees = degree_gain.shape[0]
    slots = ORDERS // lat_parts
    shape = jax.ShapeDtypeStruct

    taps = tap_table(kernel_basis, lon_reach)
    near = lax.dynamic_slice_in_dim(jnp.pad(taps, ((0, 0), (0, 0), (0, 0), (1, 1))), lat * rows, rows + 2, 3)
    own_taps = tap_rows(near[:, :, :, 1 : rows + 1])
    turned = near[:, ::-1, ::-1]
    adj_taps = tap_rows(jnp.stack([turned[:, r, :, r : r + rows] for r in range(3)], axis=1))

    my_orders = lat * slots + jnp.arange(slots, dtype=jnp.int32)
    table = legendre_rows(my_orders, lat_count, degrees)
    into, back = fourier_tables(lon_count, cells, lat_parts)
    table = table.reshape(3, 4 * degrees, lat_count)
    turned = jnp.transpose(table, (0, 2, 1))
    quad = 2.0 * math.pi / lon_count * (math.pi / lat_count) * jnp.sin(
        colatitudes(jnp.arange(lat_count, dtype=jnp.int32), lat_count)
    )
    quad = jnp.broadcast_to(quad[None, :, None], (3, lat_count, 128))
    mode_weight = jnp.where(my_orders == 0, 1.0, 2.0).astype(F32).reshape(3, 1, 4, 1)
    mode_weight = jnp.broadcast_to(mode_weight, (3, lat_count, 4, 32)).reshape(3, lat_count, 128)
    groups = degree_gain.reshape(degrees, 3, lon_parts, 16)
    gain = lax.dynamic_slice_in_dim(groups, lon, 1, 2)
    gain = jnp.broadcast_to(gain, groups.shape).reshape(degrees, chans)

    wide = (rows, ROWS, chans)
    spec_out, kernel_mix, bands = pass_call(
        True,
        cells,
        [field, into, spectral_weight],
        [table, turned, back, gain, quad, mode_weight, own_taps, kernel_weights],
        [shape(wide, BF), shape(wide, BF), shape((3, degrees, chans), F32)],
    )
    output_field, grad_pre, grad_out_w = by_rows(
        functools.partial(pointwise, cells),
        [kernel_mix, spec_out, field, cotangent],
        [out_weight, out_weight.T],
        [shape(field.shape, BF), shape(wide, BF)],
        [shape((chans, chans), F32)],
        [pltpu.VMEM((4, ROWS, chans), BF)],
    )
    turned_weights = jnp.transpose(kernel_weights, (0, 2, 1))
    grad_field, early, grad_mix_w, gain_total = pass_call(
        False,
        cells,
        [grad_pre, into],
        [table, turned, back, gain, mode_weight, quad, adj_taps, turned_weights]
        + [field, grad_out_w, bands, cotangent, spectral_weight.T],
        [shape(field.shape, BF), shape((4, chans, chans), F32), shape((chans, chans), F32), shape((degrees, chans), F32)],
    )
    weight_grads = jnp.concatenate([early[:3], grad_mix_w[None], early[3:]]) / math.sqrt(lat_count * lon_count)
    return output_field, grad_field, weight_grads, gain_total


def solution(mesh):
    placed = (P("lat", "lon", None), P("lat", "lon", None), P(), P(), P(), P(), P(), P())
    return jax.shard_map(
        local,
        mesh=mesh,
        in_specs=placed,
        out_specs=(P("lat", "lon", None), P("lat", "lon", None), P(), P()),
        check_vma=False,
    )
```

```python
import functools
import math

import jax
import jax.numpy as jnp
import numpy as np
from jax import lax
from jax.experimental import pallas as pl
from jax.experimental.pallas import tpu as pltpu
from jax.sharding import PartitionSpec as P

ORDERS = 192
BF = jnp.bfloat16
F32 = jnp.float32
VMEM = pl.BlockSpec(memory_space=pltpu.VMEM)
ROWS = 96
EXT = 128


def dot(a, b, dims=((1,), (0,))):
    return lax.dot_general(a, b, (dims, ((), ())), preferred_element_type=F32)


def tap_rows(taps):
    k, r, t, n = taps.shape
    flat = jnp.transpose(taps, (3, 0, 1, 2)).reshape(n, k * r, t)
    wide = jnp.concatenate([flat[:, :, 3:], jnp.zeros((n, k * r, EXT - t), F32), flat[:, :, :3]], axis=2)
    return jnp.pad(wide, ((0, 0), (0, 16 - k * r), (0, 0)))


def band_matrix(taps_ref, i, band_ref, cells):
    keep = lax.broadcasted_iota(jnp.int32, (ROWS, EXT), 0) < cells
    rows = taps_ref[i]
    for k in range(3):
        for r in range(3):
            row = jnp.broadcast_to(rows[3 * k + r : 3 * k + r + 1], (ROWS, EXT))
            block = pltpu.roll(row, 0, 1, stride=1, stride_axis=0)
            band_ref[k * ROWS : (k + 1) * ROWS, r * EXT : (r + 1) * EXT] = jnp.where(keep, block, 0.0).astype(BF)


def padded(pad_ref, ref, cells):
    pad_ref[:, 80:] = jnp.zeros_like(pad_ref[:, 80:])
    pad_ref[:, :cells] = ref[...]
    return pad_ref[...].reshape(-1, pad_ref.shape[2])


def pointwise(cells, km_ref, so_ref, f_ref, ct_ref, w_ref, wt_ref, out_ref, gp_ref, gow_ref, pad_ref):
    @pl.when(pl.program_id(0) == 0)
    def _():
        gow_ref[...] = jnp.zeros_like(gow_ref)

    group, rows, chans = km_ref.shape
    v = (km_ref[...].astype(F32) + so_ref[...].astype(F32)).reshape(group * rows, chans)
    ct = padded(pad_ref, ct_ref, cells)
    square = v * v
    s = jnp.tanh(0.7978845608 * v * (1.0 + 0.044715 * square))
    half = 0.5 * (1.0 + s)
    hidden = (v * half).astype(BF)
    slope = half + 0.5 * v * (1.0 - s * s) * (0.7978845608 * (1.0 + 3.0 * 0.044715 * square))
    mixed = dot(hidden, w_ref[...]).reshape(km_ref.shape)[:, :cells]
    out_ref[...] = (f_ref[...].astype(F32) + mixed).astype(BF)
    gp_ref[...] = (dot(ct, wt_ref[...]) * slope).astype(BF).reshape(km_ref.shape)
    gow_ref[...] += dot(hidden, ct, ((0,), (0,)))


def block_swap(parts):
    group = lax.broadcasted_iota(jnp.int32, parts[0].shape, 1) // 16
    for k in range(3):
        high = (group >> k) & 1 == 1
        width = 16 << k
        fresh = list(parts)
        for a in range(8):
            if (a >> k) & 1 == 0:
                b = a + (1 << k)
                fresh[a] = jnp.where(high, pltpu.roll(parts[b], width, 1), parts[a])
                fresh[b] = jnp.where(high, parts[b], pltpu.roll(parts[a], 128 - width, 1))
        parts = fresh
    return parts


def tile_swap(x):
    row = lax.broadcasted_iota(jnp.int32, x.shape, 1)
    group = lax.broadcasted_iota(jnp.int32, x.shape, 2) // 16
    for k in range(3):
        row_bit = (row >> k) & 1
        group_bit = (group >> k) & 1
        width = 16 << k
        down = pltpu.roll(pltpu.roll(x, 8 - (1 << k), 1), width, 2)
        up = down if k == 2 else pltpu.roll(pltpu.roll(x, 1 << k, 1), 128 - width, 2)
        x = jnp.where(row_bit == group_bit, x, jnp.where(group_bit == 1, down, up))
    return x


PAD = 80
MESH = pl.DeviceIdType.MESH


def transfer(axis, me, parts, source, target, bulk, send_sem, recv_sem):
    def start():
        def step(d, carry):
            peer = lax.rem(me + d, parts)
            pltpu.make_async_remote_copy(
                src_ref=source(peer),
                dst_ref=target(me),
                send_sem=send_sem,
                recv_sem=recv_sem,
                device_id={axis: peer},
                device_id_type=MESH,
            ).start()
            return carry

        lax.fori_loop(1, parts, step, 0, unroll=7 if parts == 8 else 5)

    def arrive():
        pltpu.make_async_copy(bulk, bulk, recv_sem).wait()

    def drain():
        pltpu.make_async_copy(bulk, bulk, send_sem).wait()

    return start, arrive, drain


def greet():
    barrier = pltpu.get_barrier_semaphore()
    total = 0
    for axis in ("lon", "lat"):
        me, parts = lax.axis_index(axis), lax.axis_size(axis)

        def body(d, carry, axis=axis, me=me, parts=parts):
            pl.semaphore_signal(barrier, inc=1, device_id={axis: lax.rem(me + d, parts)}, device_id_type=MESH)
            return carry

        lax.fori_loop(1, parts, body, 0, unroll=7 if parts == 8 else 5)
        total += parts - 1
    return lambda: pl.semaphore_wait(barrier, total)


def reducer(flat, got1, part, got2, whole, sems):
    s1, r1, s2, r2, s3, r3 = sems
    lat, lon = lax.axis_index("lat"), lax.axis_index("lon")
    lats, lons = lax.axis_size("lat"), lax.axis_size("lon")
    n = part.shape[0]

    def block(ref, b):
        return ref.at[pl.ds(pl.multiple_of(b * n, 16), n)]

    first = transfer(
        "lat", lat, lats, lambda p: block(flat, p), lambda s: got1.at[s], got1.at[pl.ds(0, lats - 1)], s1.at[0], r1.at[0]
    )
    second = transfer("lon", lon, lons, lambda p: part, lambda s: got2.at[s], got2.at[pl.ds(0, lons - 1)], s2.at[0], r2.at[0])
    third = transfer(
        "lat", lat, lats, lambda p: block(whole, lat), lambda s: block(whole, s),
        whole.at[pl.ds(0, (lats - 1) * n)], s3.at[0], r3.at[0],
    )

    def total(ref):
        add = lambda s, carry: carry + ref[s].astype(F32)
        return lax.fori_loop(1, ref.shape[0], add, ref[0].astype(F32)).astype(BF)

    def begin():
        first[0]()
        got1[lat] = flat[pl.ds(pl.multiple_of(lat * n, 16), n)]

    def across():
        first[1]()
        part[...] = total(got1)
        second[0]()
        got2[lon] = part[...]

    def spread():
        second[1]()
        whole[pl.ds(pl.multiple_of(lat * n, 16), n)] = total(got2)
        third[0]()

    def end():
        third[1]()
        for t in (first, second, third):
            t[2]()

    return begin, across, spread, end


def reducer_scratch(lats, lons, n):
    sem = pltpu.SemaphoreType.DMA((1,))
    return [
        pltpu.VMEM((lats * n, 128), BF),
        pltpu.VMEM((lats, n, 128), BF),
        pltpu.VMEM((n, 128), BF),
        pltpu.VMEM((lons, n, 128), BF),
        pltpu.VMEM((lats * n, 128), BF),
        *[sem] * 6,
    ]


EARLY = 288
LATE = 112


def pass_kernel(forward, cells, *refs):
    refs = list(refs)

    def take(n):
        head = refs[:n]
        del refs[:n]
        return head

    x_ref, into_ref = take(2)
    if forward:
        (mix_ref,) = take(1)
    late_in = take(8 if forward else 13)
    if forward:
        grid_ref, stencil_ref, bands_ref = take(3)
    else:
        out_ref, early_ref, gmw_ref, gain_total = take(4)
    late_ref = take(len(late_in))
    (late_sem,) = take(1)
    table_ref, turned_ref, back_ref, gain_ref, in_scale, out_scale, taps_ref, kernel_ref = late_ref[:8]
    if not forward:
        field_ref, gow_ref, bands_ref, ct_ref, wt_ref = late_ref[8:]
    send1, recv1, send2, recv2, send3, recv3, send4, recv4 = take(8)
    modes, rows_ref, ext, from_left, from_right, band_ref, spare, part_ref = take(8)
    s1, r1, s2, r2, s3, r3, s4, r4, hs, hr = take(10)
    if not forward:
        pad_ref, grad_ref, grid_ref, stencil_ref, gain_out = take(5)
        red = take(11)
        begin, across, spread, end = reducer(*red[:5], red[5:])
        red2 = take(11)
        begin2, across2, spread2, end2 = reducer(*red2[:5], red2[5:])
    late_copies = [pltpu.make_async_copy(a, b, late_sem.at[n]) for n, (a, b) in enumerate(zip(late_in, late_ref))]
    lat, lon = lax.axis_index("lat"), lax.axis_index("lon")
    lons, lats = lax.axis_size("lon"), lax.axis_size("lat")
    rows = x_ref.shape[0]
    chans = x_ref.shape[2]
    enter = greet()

    def way(axis, me, parts, send, recv, ss, rs):
        def at(v):
            start, arrive, drain = transfer(
                axis, me, parts,
                lambda p: send.at[v, p], lambda s: recv.at[v, s], recv.at[v, pl.ds(0, parts - 1)], ss.at[v], rs.at[v],
            )

            def go():
                start()
                recv[v, me] = send[v, me]

            return go, arrive, drain

        return [at(v) for v in range(3)]

    lon_in = way("lon", lon, lons, send1, recv1, s1, r1)
    lat_in = way("lat", lat, lats, send2, recv2, s2, r2)
    lat_out = way("lat", lat, lats, send3, recv3, s3, r3)
    lon_out = way("lon", lon, lons, send4, recv4, s4, r4)
    order = lax.broadcasted_iota(jnp.int32, (192, 128), 1) // 32
    lane_group = lax.broadcasted_iota(jnp.int32, (192, 128), 1) // 16
    blank = jnp.zeros((8, 128), F32)

    def sideways(source, target, n, step):
        return pltpu.make_async_remote_copy(
            src_ref=source, dst_ref=target, send_sem=hs.at[n], recv_sem=hr.at[n],
            device_id={"lon": lax.rem(lon + step + lons, lons)}, device_id_type=MESH,
        )

    def vertical(source, target, n, step):
        return pltpu.make_async_remote_copy(
            src_ref=source, dst_ref=target, send_sem=hs.at[n], recv_sem=hr.at[n],
            device_id={"lat": lax.rem(lat + step + lats, lats)}, device_id_type=MESH,
        )

    to_right = sideways(ext.at[pl.ds(1, rows), pl.ds(80, 16)], from_left, 0, 1)
    to_left = sideways(ext.at[pl.ds(1, rows), pl.ds(0, 16)], from_right, 1, -1)
    to_below = vertical(ext.at[rows], ext.at[0], 2, 1)
    to_above = vertical(ext.at[1], ext.at[rows + 1], 3, -1)

    def fill(i, carry):
        if forward:
            ext[1 + i, 80:96] = jnp.zeros((16, chans), BF)
        ext[1 + i, : x_ref.shape[1]] = x_ref[i]
        return carry

    def halo_columns():
        for c in (to_right, to_left):
            c.wait()
        place = lax.broadcasted_iota(jnp.int32, (16, chans), 0)

        def step(i, carry):
            own = ext[1 + i, 80:96].astype(F32)
            right = pltpu.roll(from_right[i].astype(F32), 10, 0)
            left = pltpu.roll(from_left[i].astype(F32), 6, 0)
            ext[1 + i, 80:96] = jnp.where(place < 10, own, jnp.where(place < 13, right, 0.0)).astype(BF)
            ext[1 + i, 96:112] = jnp.zeros((16, chans), BF)
            ext[1 + i, 112:128] = jnp.where(place >= 13, left, 0.0).astype(BF)
            return carry

        lax.fori_loop(0, rows, step, 0, unroll=2)

        @pl.when(lat < lats - 1)
        def _():
            to_below.start()

        @pl.when(lat > 0)
        def _():
            to_above.start()

        @pl.when(lat == 0)
        def _():
            ext[0] = jnp.zeros((EXT, chans), BF)

        @pl.when(lat == lats - 1)
        def _():
            ext[rows + 1] = jnp.zeros((EXT, chans), BF)

    def halo_rows():
        @pl.when(lat > 0)
        def _():
            to_below.wait_recv()

        @pl.when(lat < lats - 1)
        def _():
            to_above.wait_recv()

    def halo_drain():
        @pl.when(lat < lats - 1)
        def _():
            to_below.wait_send()

        @pl.when(lat > 0)
        def _():
            to_above.wait_send()

    def stencil(first):
        def step(n, carry):
            for a in range(2):
                i = first + 2 * n + a
                band_matrix(taps_ref, i, band_ref.at[a], cells)
                source = ext[pl.ds(i, 3)].reshape(3 * EXT, chans)
                part = dot(band_ref[a], source).astype(BF)
                for k in range(3):
                    part_ref[k, 2 * n + a] = part[k * ROWS : (k + 1) * ROWS]
            return carry

        lax.fori_loop(0, 2, step, 0)
        total = None
        for k in range(3):
            part = dot(part_ref[k].reshape(4 * ROWS, chans), kernel_ref[k])
            total = part if total is None else total + part
        stencil_ref[first : first + 4] = total.reshape(4, ROWS, chans).astype(stencil_ref.dtype)
        if not forward:
            own = pad_ref[first : first + 4].reshape(4 * ROWS, chans)
            for k in range(3):
                add = dot(own, part_ref[k].reshape(4 * ROWS, chans), ((0,), (0,)))
                grad_ref[k] = add if first == START else grad_ref[k] + add

    def tiles(body):
        def step(n, carry):
            body(n // 6, pl.multiple_of(n % 6 * 16, 16))
            return carry

        lax.fori_loop(0, 18, step, 0, unroll=6)

    def split(v):
        lanes_v = slice(v * 128, (v + 1) * 128)
        if forward:
            def mix(g, carry):
                block = ext[pl.ds(1 + g * 8, 8), 0:ROWS].reshape(8 * ROWS, chans)
                spare[pl.ds(g * 8, 8)] = dot(block, mix_ref[:, lanes_v]).reshape(8, ROWS, 128)
                return carry

            lax.fori_loop(0, 3, mix, 0)

        def body(g, j):
            if forward:
                parts = [spare[g * 8 + n, pl.ds(j, 16)] for n in range(8)]
            else:
                parts = [ext[1 + g * 8 + n, pl.ds(j, 16), lanes_v].astype(F32) for n in range(8)]
            lanes = pl.ds(pl.multiple_of(g * 128, 128), 128)
            for p, part in enumerate(block_swap(parts)):
                send1[v, p, pl.ds(j, 16), lanes] = part.astype(BF)

        tiles(body)
        lon_in[v][0]()

    def analyse(v):
        lon_in[v][1]()
        modes[...] = dot(into_ref[...], recv1[v].reshape(lons * ROWS, 384))

        def step(b, carry):
            block = modes[pl.ds(pl.multiple_of(b * 24, 8), 24), :]
            turned = [tile_swap(block[:, g * 128 : (g + 1) * 128].reshape(3, 8, 128)) for g in range(3)]
            pieces = [turned[g][o] for o in range(3) for g in range(3)] + [blank]
            send2[v, b] = jnp.concatenate(pieces, axis=0).astype(BF)
            return carry

        lax.fori_loop(0, lats, step, 0, unroll=4)
        lat_in[v][0]()

    def filter_bands(v):
        lat_in[v][1]()
        lanes = slice(v * 128, (v + 1) * 128)

        def gather(b, carry):
            at = pl.ds(pl.multiple_of(b * 24, 8), 24)
            block = recv2[v, b].astype(F32)
            for o in range(3):
                rows_ref[o, at] = block[o * 24 : (o + 1) * 24] * in_scale[o, at]
            return carry

        lax.fori_loop(0, lats, gather, 0, unroll=4)
        gain_sum = None
        for o in range(3):
            every = dot(table_ref[o], rows_ref[o].astype(BF))
            band = every[:192]
            for m in range(1, 4):
                band = jnp.where(order == m, every[m * 192 : (m + 1) * 192], band)
            if forward:
                bands_ref[o, :, lanes] = band
            else:
                term = band * bands_ref[o, :, lanes]
                gain_sum = term if gain_sum is None else gain_sum + term
            band = band * gain_ref[:, lanes]
            spread_out = jnp.concatenate([jnp.where(order == m, band, 0.0).astype(BF) for m in range(4)], axis=0)
            rows_ref[o] = dot(turned_ref[o], spread_out) * out_scale[o]

        def scatter(b, carry):
            at = pl.ds(pl.multiple_of(b * 24, 8), 24)
            send3[v, b] = jnp.concatenate([rows_ref[o, at] for o in range(3)] + [blank], axis=0).astype(BF)
            return carry

        lax.fori_loop(0, lats, scatter, 0, unroll=4)
        lat_out[v][0]()
        if not forward:
            for width in (16, 32, 64):
                gain_sum = gain_sum + pltpu.roll(gain_sum, width, 1)
            gain_out[:, lanes] = jnp.where(lane_group == lon, gain_sum, 0.0)

    def synthesise(v):
        lat_out[v][1]()

        def step(b, carry):
            turned = tile_swap(recv3[v, b].astype(F32)[:72].reshape(9, 8, 128))
            wide = [jnp.concatenate([turned[o * 3 + g] for o in range(3)], axis=0) for g in range(3)]
            modes[pl.ds(pl.multiple_of(b * 24, 8), 24), :] = jnp.concatenate(wide, axis=1)
            return carry

        lax.fori_loop(0, lats, step, 0, unroll=4)
        send4[v] = dot(back_ref[...], modes[...].astype(BF)).astype(BF).reshape(lons, ROWS, 384)
        lon_out[v][0]()

    def join(v):
        lon_out[v][1]()

        def body(g, j):
            lanes = pl.ds(pl.multiple_of(g * 128, 128), 128)
            parts = [recv4[v, p, pl.ds(j, 16), lanes].astype(F32) for p in range(8)]
            for n, part in enumerate(block_swap(parts)):
                grid_ref[g * 8 + n, pl.ds(j, 16), v * 128 : (v + 1) * 128] = part.astype(BF)

        tiles(body)

    def early_begin():
        flat = red[0]
        for k in range(4):
            for v in range(3):
                block = (grad_ref[k] if k < 3 else gow_ref[...])[:, v * 128 : (v + 1) * 128]
                flat[(k * 3 + v) * 384 : (k * 3 + v + 1) * 384] = block.astype(BF)
        begin()

    def early_end():
        end()
        whole = red[4]
        for k in range(4):
            for v in range(3):
                early_ref[k, :, v * 128 : (v + 1) * 128] = whole[(k * 3 + v) * 384 : (k * 3 + v + 1) * 384].astype(F32)

    def own_rows(i, carry):
        pad_ref[i, 80:96] = jnp.zeros((16, chans), BF)
        pad_ref[i, :cells] = field_ref[i]
        return carry

    def weigh(v):
        lanes = slice(v * 128, (v + 1) * 128)

        def step(n, carry):
            some = pl.ds(n * 8, 8)
            own = pad_ref[some].reshape(8 * ROWS, chans)
            return carry + dot(own, grid_ref[some, :, lanes].reshape(8 * ROWS, 128), ((0,), (0,)))

        own = pad_ref[0:8].reshape(8 * ROWS, chans)
        first = dot(own, grid_ref[0:8, :, lanes].reshape(8 * ROWS, 128), ((0,), (0,)))
        gmw_ref[:, lanes] = lax.fori_loop(1, 3, step, first)

    def late_begin():
        flat = red2[0]
        for v in range(3):
            lanes = slice(v * 128, (v + 1) * 128)
            flat[v * 576 : v * 576 + 384] = gmw_ref[:, lanes].astype(BF)
            flat[v * 576 + 384 : (v + 1) * 576] = gain_out[:, lanes].astype(BF)
        flat[1728:] = jnp.zeros((64, 128), BF)
        begin2()

    def late_end():
        end2()
        whole = red2[4]
        for v in range(3):
            lanes = slice(v * 128, (v + 1) * 128)
            gmw_ref[:, lanes] = whole[v * 576 : v * 576 + 384].astype(F32)
            gain_total[:, lanes] = whole[v * 576 + 384 : (v + 1) * 576].astype(F32)

    def field_rows(first):
        def step(n, carry):
            some = pl.ds(first + n * 4, 4)
            mixed = dot(grid_ref[some].reshape(4 * ROWS, chans), wt_ref[...]).reshape(4, ROWS, chans)
            add = stencil_ref[some] + mixed
            out_ref[some] = (ct_ref[some].astype(F32) + add[:, :cells]).astype(BF)
            return carry

        lax.fori_loop(0, 2, step, 0)

    for c in late_copies:
        c.start()
    lax.fori_loop(0, rows, fill, 0, unroll=2)
    enter()
    to_right.start()
    to_left.start()
    for v in range(3):
        split(v)
    for c in late_copies:
        c.wait()
    halo_columns()
    START = 4
    if not forward:
        lax.fori_loop(0, rows, own_rows, 0, unroll=2)
    stencil(4)
    stencil(8)
    analyse(0)
    stencil(12)
    stencil(16)
    filter_bands(0)
    analyse(1)
    halo_rows()
    stencil(20)
    if not forward:
        stencil(0)
        early_begin()
    synthesise(0)
    filter_bands(1)
    analyse(2)
    if forward:
        stencil(0)
    synthesise(1)
    filter_bands(2)
    if not forward:
        across()
    join(0)
    if not forward:
        weigh(0)
    synthesise(2)
    if not forward:
        spread()
    join(1)
    if not forward:
        weigh(1)
    join(2)
    if not forward:
        weigh(2)
        late_begin()
        field_rows(0)
        across2()
        field_rows(8)
        spread2()
        field_rows(16)
        early_end()
        late_end()
    halo_drain()
    for road in (lon_in, lat_in, lat_out, lon_out):
        for v in range(3):
            road[v][2]()


def pass_call(forward, cells, first, late, outs):
    lons, lats = lax.axis_size("lon"), lax.axis_size("lat")
    rows, _, chans = first[0].shape
    lon_buf = pltpu.VMEM((3, lons, ROWS, 384), BF)
    lat_buf = pltpu.VMEM((3, lats, PAD, 128), BF)
    lon_sem = lat_sem = pltpu.SemaphoreType.DMA((3,))
    scratch = [pltpu.VMEM(a.shape, a.dtype) for a in late] + [pltpu.SemaphoreType.DMA((len(late),))]
    scratch += [lon_buf, lon_buf] + [lat_buf] * 4 + [lon_buf, lon_buf]
    scratch += [
        pltpu.VMEM((384, 384), F32),
        pltpu.VMEM((3, 384, 128), F32),
        pltpu.VMEM((rows + 2, EXT, chans), BF),
        pltpu.VMEM((rows, 16, chans), BF),
        pltpu.VMEM((rows, 16, chans), BF),
        pltpu.VMEM((2, 3 * ROWS, 3 * EXT), BF),
        pltpu.VMEM((rows, ROWS, 128) if forward else (8, 128), F32),
        pltpu.VMEM((3, 4, ROWS, chans), BF),
    ]
    scratch += [lon_sem, lon_sem, lat_sem, lat_sem, lat_sem, lat_sem, lon_sem, lon_sem]
    scratch += [pltpu.SemaphoreType.DMA((4,)), pltpu.SemaphoreType.DMA((4,))]
    if not forward:
        wide = (rows, ROWS, chans)
        scratch += [pltpu.VMEM(wide, BF), pltpu.VMEM((3, chans, chans), F32), pltpu.VMEM(wide, BF), pltpu.VMEM(wide, F32)]
        scratch += [pltpu.VMEM((192, chans), F32)]
        scratch += reducer_scratch(lats, lons, EARLY) + reducer_scratch(lats, lons, LATE)
    return pl.pallas_call(
        functools.partial(pass_kernel, forward, cells),
        out_shape=outs,
        in_specs=[VMEM] * len(first) + [pl.BlockSpec(memory_space=pl.ANY)] * len(late),
        out_specs=[VMEM] * len(outs),
        scratch_shapes=scratch,
        compiler_params=pltpu.CompilerParams(
            collective_id=1 if forward else 2, has_side_effects=True, vmem_limit_bytes=60 << 20
        ),
    )(*first, *late)


def fourier_tables(lon_count, cells, lat_parts):
    j = np.arange(lon_count)
    angles = (j[:, None] * np.arange(ORDERS)[None, :] % lon_count) * (2.0 * np.pi / lon_count)
    waves = np.stack([np.cos(angles), -np.sin(angles)], axis=-1).reshape(lon_count // cells, cells, 2 * ORDERS)
    waves = np.pad(waves, ((0, 0), (0, ROWS - cells), (0, 0))).reshape(-1, 2 * ORDERS)
    return jnp.asarray(waves.T, BF), jnp.asarray(waves, BF)


def legendre_kernel(m_ref, x_ref, diag_ref, out_ref):
    m = m_ref[...]
    x = x_ref[...]
    diag = diag_ref[...]
    reps = x.shape[1] // m.shape[1]

    def wide(a):
        return jnp.concatenate([a] * reps, axis=1)

    mw = wide(m)

    def step(l, carry):
        prev, before, a_prev = carry
        lf = l.astype(F32)
        above = lf > m
        den = jnp.where(above, lf * lf - m * m, 1.0)
        a = jnp.where(above, jnp.sqrt((4.0 * lf * lf - 1.0) / den), 1.0)
        cur = wide(a) * (x * prev - before * wide(1.0 / a_prev))
        cur = jnp.where(lf == mw, diag, jnp.where(lf > mw, cur, 0.0))
        out_ref[l] = cur.astype(BF)
        return cur, prev, a

    blank = x * 0.0
    lax.fori_loop(0, out_ref.shape[0], step, (blank, blank, m * 0.0 + 1.0), unroll=4)


def colatitudes(row_index, lat_count):
    return (row_index.astype(F32) + 0.5) * (math.pi / lat_count)


def legendre_rows(orders, lat_count, degrees):
    slots = 16
    m = jnp.pad(orders, (0, slots - orders.shape[0])).astype(F32)[:, None]
    colat = colatitudes(jnp.arange(lat_count, dtype=jnp.int32), lat_count)[None, :]
    log_start = 0.5 * (lax.lgamma(m + 1.5) - lax.lgamma(m + 1.0) - lax.lgamma(F32(1.5) + 0.0 * m))
    diag = jnp.exp(log_start + m * jnp.log(jnp.sin(colat))) / math.sqrt(4.0 * math.pi)
    x = jnp.broadcast_to(jnp.cos(colat), diag.shape)
    table = pl.pallas_call(
        legendre_kernel,
        out_shape=jax.ShapeDtypeStruct((degrees, slots, lat_count), BF),
        in_specs=[VMEM] * 3,
        out_specs=VMEM,
        compiler_params=pltpu.CompilerParams(vmem_limit_bytes=40 << 20),
    )(jnp.broadcast_to(m, (slots, 128)), x, diag)
    return jnp.transpose(table[:, : orders.shape[0]], (1, 0, 2))


def tap_table(kernel_basis, lon_reach):
    count = kernel_basis.shape[2]
    offsets = jnp.abs(jnp.arange(count, dtype=jnp.int32) - count // 2)
    mask = offsets[None, :, None] <= lon_reach[:, None, :]
    return kernel_basis * mask[None].astype(F32)


def by_rows(body, args, whole, outs, totals, scratch, group=4):
    def cut(a):
        return pl.BlockSpec((group,) + a.shape[1:], lambda g: (g, 0, 0))

    def full(a):
        return pl.BlockSpec(a.shape, lambda g: (0,) * len(a.shape))

    return pl.pallas_call(
        body,
        grid=(args[0].shape[0] // group,),
        in_specs=[cut(a) for a in args] + [full(a) for a in whole],
        out_specs=[cut(a) for a in outs] + [full(a) for a in totals],
        out_shape=list(outs) + list(totals),
        scratch_shapes=scratch,
        compiler_params=pltpu.CompilerParams(vmem_limit_bytes=56 << 20),
    )(*args, *whole)


def local(field, cotangent, kernel_weights, spectral_weight, out_weight, degree_gain, kernel_basis, lon_reach):
    rows, cells, chans = field.shape
    lat_parts, lon_parts = lax.axis_size("lat"), lax.axis_size("lon")
    lat, lon = lax.axis_index("lat"), lax.axis_index("lon")
    lat_count, lon_count = rows * lat_parts, cells * lon_parts
    degrees = degree_gain.shape[0]
    slots = ORDERS // lat_parts
    shape = jax.ShapeDtypeStruct

    taps = tap_table(kernel_basis, lon_reach)
    near = lax.dynamic_slice_in_dim(jnp.pad(taps, ((0, 0), (0, 0), (0, 0), (1, 1))), lat * rows, rows + 2, 3)
    own_taps = tap_rows(near[:, :, :, 1 : rows + 1])
    turned = near[:, ::-1, ::-1]
    adj_taps = tap_rows(jnp.stack([turned[:, r, :, r : r + rows] for r in range(3)], axis=1))

    my_orders = lat * slots + jnp.arange(slots, dtype=jnp.int32)
    table = legendre_rows(my_orders, lat_count, degrees)
    into, back = fourier_tables(lon_count, cells, lat_parts)
    table = table.reshape(3, 4 * degrees, lat_count)
    turned = jnp.transpose(table, (0, 2, 1))
    quad = 2.0 * math.pi / lon_count * (math.pi / lat_count) * jnp.sin(
        colatitudes(jnp.arange(lat_count, dtype=jnp.int32), lat_count)
    )
    quad = jnp.broadcast_to(quad[None, :, None], (3, lat_count, 128))
    mode_weight = jnp.where(my_orders == 0, 1.0, 2.0).astype(F32).reshape(3, 1, 4, 1)
    mode_weight = jnp.broadcast_to(mode_weight, (3, lat_count, 4, 32)).reshape(3, lat_count, 128)
    groups = degree_gain.reshape(degrees, 3, lon_parts, 16)
    gain = lax.dynamic_slice_in_dim(groups, lon, 1, 2)
    gain = jnp.broadcast_to(gain, groups.shape).reshape(degrees, chans)

    wide = (rows, ROWS, chans)
    spec_out, kernel_mix, bands = pass_call(
        True,
        cells,
        [field, into, spectral_weight],
        [table, turned, back, gain, quad, mode_weight, own_taps, kernel_weights],
        [shape(wide, BF), shape(wide, BF), shape((3, degrees, chans), F32)],
    )
    output_field, grad_pre, grad_out_w = by_rows(
        functools.partial(pointwise, cells),
        [kernel_mix, spec_out, field, cotangent],
        [out_weight, out_weight.T],
        [shape(field.shape, BF), shape(wide, BF)],
        [shape((chans, chans), F32)],
        [pltpu.VMEM((4, ROWS, chans), BF)],
    )
    turned_weights = jnp.transpose(kernel_weights, (0, 2, 1))
    grad_field, early, grad_mix_w, gain_total = pass_call(
        False,
        cells,
        [grad_pre, into],
        [table, turned, back, gain, mode_weight, quad, adj_taps, turned_weights]
        + [field, grad_out_w, bands, cotangent, spectral_weight.T],
        [shape(field.shape, BF), shape((4, chans, chans), F32), shape((chans, chans), F32), shape((degrees, chans), F32)],
    )
    weight_grads = jnp.concatenate([early[:3], grad_mix_w[None], early[3:]]) / math.sqrt(lat_count * lon_count)
    return output_field, grad_field, weight_grads, gain_total


def solution(mesh):
    placed = (P("lat", "lon", None), P("lat", "lon", None), P(), P(), P(), P(), P(), P())
    return jax.shard_map(
        local,
        mesh=mesh,
        in_specs=placed,
        out_specs=(P("lat", "lon", None), P("lat", "lon", None), P(), P()),
        check_vma=False,
    )
```
